32 devices in a mesh: ent: 8 (over z, x), rep: 4 (over y, core).
Axes of the slice: x: 2, y: 2, z: 4, core: 2. Of those that a mesh axis runs over, the one named last changes fastest.
Arguments:
- entity_table: float32 [8192, 200], P('ent'), may hold values from -1.8 to 1.8
- entity_state: float32 [8192], P('ent'), may hold values from 1e-05 to 1
- operators: float32 [16, 200, 200], P('ent'), may hold values from -0.4375 to 0.4375
- operator_state: float32 [16, 200, 200], P('ent'), may hold values from 1 to 100
- sources: int32 [8192], P(('ent', 'rep')), may hold values from 0 to 1023
- destinations: int32 [8192], P(('ent', 'rep')), may hold values from 0 to 1023
- relations: int32 [8192, 1], P(('ent', 'rep')), may hold values from 0 to 15; in each aligned block of 256 rows (0 to 255, 256 to 511, ...) at most 32 rows name the same one
- negatives: int32 [32, 1000], P(('ent', 'rep')), may hold values from 0 to 1023
Outputs:
- new_table: float32 [8192, 200], P('ent')
- new_entity_state: float32 [8192], P('ent')
- new_operators: float32 [16, 200, 200], P('ent')
- new_operator_state: float32 [16, 200, 200], P('ent')
The draws below stay inside these ranges and needn't reach their ends.
Inputs may be any that keep to these rules, and one draw needn't show every extreme that they name: `relations`: among the 256 edges of one device no relation occurs more than 32 times, and some relation occurs exactly 32 times.
All inputs are finite; a program needn't handle non-finite values.
Results may differ from the reference program's by a relative error of at most 0.0019.
Values may be sent and summed in bfloat16 or wider, within the bound.
No kernel may reach another device: no remote copies, remote signals or barrier semaphores. Data moves between devices by JAX's collectives and lax.ppermute only.
A program may use at most 64 MiB of HBM per device.

```python
import math
import jax
import jax.numpy as jnp
import numpy as np
from jax import lax

D = 200
NEG = 1000
SPAN = 256
ENT_DEV = 1024
EDGE_DEV = 256
REL = 16
MOST = 32
ENTITIES = 8192
EDGES = 8192
SPANS = 32
N_ENT = 8
N_REP = 4


def place_ends(result, own_key, low, largest):
    place = [jax.random.randint(jax.random.fold_in(own_key, axis), (), 0, length) for axis, length in enumerate(result.shape)]
    widest = result.shape.index(max(result.shape))
    next_to = place[:widest] + [(place[widest] + 1) % result.shape[widest]] + place[widest + 1:]
    return result.at[tuple(place)].set(low).at[tuple(next_to)].set(largest)


def shard_levels(key, shape, shards, least, largest):
    def one(dim, blocks):
        draws = jax.random.uniform(jax.random.fold_in(jax.random.fold_in(key, 6), dim), (blocks,), jnp.float32, least / len(shards), largest / len(shards))
        return jnp.repeat(jnp.exp(draws), shape[dim] // blocks).reshape((-1,) + (1,) * (len(shape) - dim - 1))

    factor_of = one(*shards[0])
    for cut in shards[1:]:
        factor_of = factor_of * one(*cut)
    return factor_of


def deal_out(key, own, number, rows, count, top, limit, slope):
    ranking = jax.random.permutation(key, count)
    crowded, common = shares(count, rows * top, limit, slope, True), shares(count, rows * top, limit, slope, False)
    places = jnp.arange(count)

    def named(tallies, offset_by):
        used = int((tallies > 0).sum())
        fixed = max(1, used // 4)
        shifted = fixed + (places - fixed + offset_by * (used - fixed)) % max(1, count - fixed)
        return jnp.zeros((count,), jnp.int32).at[ranking[jnp.where(places < fixed, places, shifted)]].set(jnp.asarray(tallies, jnp.int32))

    tallies = jnp.where(number % 4 == 0, named(crowded, number // 4), named(common, number - number // 4 - 1))
    mixed = jax.random.permutation(jax.random.fold_in(own, 3), count)
    giver, receiver = mixed[0:count // 2 * 2:2], mixed[1:count // 2 * 2:2]
    margin = jnp.minimum(tallies[giver] - 1, limit - tallies[receiver]) // 2
    margin = jnp.where((giver == ranking[0]) | (receiver == ranking[0]) | (tallies[receiver] == 0), 0, jnp.maximum(margin, 0))
    shifted = jax.random.randint(jax.random.fold_in(own, 4), (count // 2,), 0, 1 << 20) % (margin + 1)
    tallies = tallies.at[giver].add(-shifted).at[receiver].add(shifted)
    members = jnp.searchsorted(jnp.cumsum(tallies), jnp.arange(rows * top), side="right").astype(jnp.int32)
    listing = members.reshape(top, rows).T
    listing = listing[jax.random.permutation(jax.random.fold_in(own, 1), rows)]
    offset_by = jax.random.randint(jax.random.fold_in(own, 2), (rows, 1), 0, top)
    return jnp.take_along_axis(listing, (jnp.arange(top)[None, :] + offset_by) % top, axis=1)


def shares(number_of, total, reach, skew, full):
    loads = [(1 << 20) // math.isqrt(standing ** skew) + 1 for standing in range(1, number_of + 1)]
    largest = reach if full else min(reach, max(-(-total // number_of), total * loads[0] // sum(loads)))
    least = 1 if total - largest >= number_of - 1 else 0
    holding, surplus = [largest] + [least] * (number_of - 1), total - largest - least * (number_of - 1)
    while surplus > 0:
        movable = [i for i in range(1, number_of) if holding[i] < largest] or [i for i in range(1, number_of) if holding[i] < reach]
        mass, budget = sum([loads[i] for i in movable]), surplus
        for i in movable:
            more = min(reach - holding[i], max(1, budget * loads[i] // mass), surplus)
            holding[i] = holding[i] + more
            surplus = surplus - more
    return np.array(holding)


def scatter_about(key, extent, scale, limit, cuts=(), kind=jnp.bfloat16):
    drawn = scale * jax.random.normal(key, extent, jnp.float32)
    if cuts:
        drawn = drawn * shard_levels(key, extent, cuts, -0.22, 0.18)
    return jnp.clip(drawn, -limit, limit).astype(kind)


def setup_inputs(seed: int = 0) -> dict:
    key_of = jax.random.split(jax.random.key(seed), 9)
    entity_table = scatter_about(key_of[0], (ENTITIES, D), 0.3, 1.8, ((0, 8),), jnp.float32)
    entity_state = jnp.clip(jnp.exp(math.log(1.0) - 11.512925 * jax.random.uniform(key_of[1], (ENTITIES,), jnp.float32) ** shard_levels(key_of[1], (ENTITIES,), ((0, 8),), -0.2, 0.2)), 9.999999747378752e-06, 1.0)
    operators = scatter_about(key_of[2], (REL, D, D), D ** -0.5, 0.4375, ((0, 8),), jnp.float32)
    operator_state = jnp.clip(jnp.exp(math.log(100.0) - 4.6051702 * jax.random.uniform(key_of[3], (REL, D, D), jnp.float32) ** shard_levels(key_of[3], (REL, D, D), ((0, 8),), -0.2, 0.2)), 1.0, 100.0)
    sources = place_ends(jax.random.randint(key_of[4], (EDGES,), 0, ENT_DEV), jax.random.fold_in(key_of[4], 1), 0, ENT_DEV - 1).astype(jnp.int32)
    destinations = place_ends(jax.random.randint(key_of[5], (EDGES,), 0, ENT_DEV), jax.random.fold_in(key_of[5], 1), 0, ENT_DEV - 1).astype(jnp.int32)
    relations_keys = jax.random.split(jax.random.fold_in(key_of[6], 1), EDGES // EDGE_DEV)
    relations_turns = jax.random.permutation(jax.random.fold_in(key_of[6], 3), EDGES // EDGE_DEV)
    relations = jax.vmap(lambda own, number: deal_out(jax.random.fold_in(key_of[6], 2), own, number, EDGE_DEV, REL, 1, MOST, 2))(relations_keys, relations_turns).reshape((EDGES, 1))
    negatives = place_ends(jax.random.randint(key_of[7], (SPANS, NEG), 0, ENT_DEV), jax.random.fold_in(key_of[7], 1), 0, ENT_DEV - 1).astype(jnp.int32)
    return {"entity_table": entity_table, "entity_state": entity_state, "operators": operators, "operator_state": operator_state, "sources": sources, "destinations": destinations, "relations": relations, "negatives": negatives}


entity_rate = 0.1
operator_rate = 0.02
epsilon = 1e-06

def place_slots(relation_ids, capacity):
    count_edges = relation_ids.shape[0]
    ordering = jnp.argsort(relation_ids, stable=True).astype(jnp.int32)
    ranked = relation_ids[ordering]
    leading = jnp.searchsorted(ranked, ranked, side='left').astype(jnp.int32)
    within = jnp.arange(count_edges, dtype=jnp.int32) - leading
    position = jnp.zeros((count_edges,), jnp.int32).at[ordering].set(within)
    return relation_ids * capacity + position

def score_grads(transformed, target_ids, negative_ids, table_rows):
    target_rows = jnp.take(table_rows, target_ids, axis=0)
    positive = lax.optimization_barrier(jnp.sum(transformed.astype(jnp.float32) * target_rows.astype(jnp.float32), axis=-1))
    positive_grad = -jax.nn.sigmoid(-positive)
    width = transformed.shape[1]
    blocks = transformed.reshape(-1, SPAN, width)
    negative_count = negative_ids.shape[1]

    def span_step(running, pieces):
        query_block, negative_block = pieces
        negative_rows = jnp.take(table_rows, negative_block, axis=0)
        scores = lax.dot_general(query_block, negative_rows, (((1,), (1,)), ((), ())), preferred_element_type=jnp.float32)
        negative_grad = (jax.nn.sigmoid(scores) / negative_count).astype(jnp.bfloat16)
        query_part = jnp.dot(negative_grad, negative_rows, preferred_element_type=jnp.float32)
        row_update = lax.dot_general(negative_grad, query_block, (((0,), (0,)), ((), ())), preferred_element_type=jnp.float32)
        return (running.at[negative_block].add(row_update), query_part)
    starting = jnp.zeros((table_rows.shape[0], width), jnp.float32)
    negative_total, query_parts = lax.scan(span_step, starting, (blocks, negative_ids))
    query_grad = (positive_grad[:, None] * target_rows.astype(jnp.float32) + query_parts.reshape(-1, width)).astype(jnp.bfloat16)
    target_grad = negative_total.at[target_ids].add(positive_grad[:, None] * transformed.astype(jnp.float32))
    return (query_grad, target_grad)

def row_adagrad(weights, moments, gradient):
    fresh_moments = moments + lax.optimization_barrier(jnp.mean(gradient * gradient, axis=-1))
    updated = weights - entity_rate * gradient / (jnp.sqrt(fresh_moments)[:, None] + epsilon)
    return (updated, fresh_moments)

def dense_adagrad(weights, moments, gradient):
    fresh_moments = moments + gradient * gradient
    updated = weights - operator_rate * gradient / (jnp.sqrt(fresh_moments) + epsilon)
    return (updated, fresh_moments)

def reference(entity_table, entity_state, operators, operator_state, sources, destinations, relations, negatives):
    table_half = entity_table.astype(jnp.bfloat16)
    operators_wide = operators.astype(jnp.bfloat16).astype(jnp.float32)
    span_rows = EDGE_DEV // SPAN

    def block_step(running, block):
        entity_grad, operator_grad = running
        partition = block // N_REP
        following = (partition + 1) % N_ENT
        source_table = lax.dynamic_slice_in_dim(table_half, partition * ENT_DEV, ENT_DEV, 0)
        target_table = lax.dynamic_slice_in_dim(table_half, following * ENT_DEV, ENT_DEV, 0)
        source_ids = lax.dynamic_slice_in_dim(sources, block * EDGE_DEV, EDGE_DEV, 0)
        target_ids = lax.dynamic_slice_in_dim(destinations, block * EDGE_DEV, EDGE_DEV, 0)
        relation_ids = lax.dynamic_slice_in_dim(relations[:, 0], block * EDGE_DEV, EDGE_DEV, 0)
        negative_ids = lax.dynamic_slice_in_dim(negatives, block * span_rows, span_rows, 0)
        slot_index = place_slots(relation_ids, MOST)
        source_rows = jnp.take(source_table, source_ids, axis=0)
        outgoing = jnp.zeros((REL * MOST, D), jnp.bfloat16).at[slot_index].set(source_rows).reshape(REL, MOST, D)
        transformed_slots = jnp.einsum('rmd,rdk->rmk', outgoing.astype(jnp.float32), operators_wide).astype(jnp.bfloat16)
        transformed = jnp.take(transformed_slots.reshape(REL * MOST, D), slot_index, axis=0)
        query_grad, target_grad = score_grads(transformed, target_ids, negative_ids, target_table)
        grad_slots = jnp.zeros((REL * MOST, D), jnp.bfloat16).at[slot_index].set(query_grad).reshape(REL, MOST, D)
        source_slots = jnp.einsum('rmk,rdk->rmd', grad_slots.astype(jnp.float32), operators_wide).astype(jnp.bfloat16)
        source_grad = jnp.take(source_slots.reshape(REL * MOST, D), slot_index, axis=0)
        operator_grad = operator_grad + jnp.einsum('rmd,rmk->rdk', outgoing.astype(jnp.float32), grad_slots.astype(jnp.float32))
        entity_grad = entity_grad.at[partition * ENT_DEV + source_ids].add(source_grad.astype(jnp.float32))
        current = lax.dynamic_slice_in_dim(entity_grad, following * ENT_DEV, ENT_DEV, 0)
        entity_grad = lax.dynamic_update_slice_in_dim(entity_grad, current + target_grad, following * ENT_DEV, 0)
        return ((entity_grad, operator_grad), None)
    starting = (jnp.zeros((ENTITIES, D), jnp.float32), jnp.zeros((REL, D, D), jnp.float32))
    (entity_grad, operator_grad), _ = lax.scan(block_step, starting, jnp.arange(N_ENT * N_REP, dtype=jnp.int32))
    new_table, new_entity_state = row_adagrad(entity_table, entity_state, entity_grad)
    new_operators, new_operator_state = dense_adagrad(operators, operator_state, operator_grad)
    return (new_table, new_entity_state, new_operators, new_operator_state)
```

```python
import functools

import jax
import jax.numpy as jnp
from jax import lax
from jax.experimental import pallas as pl
from jax.experimental.pallas import tpu as pltpu
from jax.sharding import PartitionSpec as P

SPAN = 256
EDGE_DEV = 256
REL_DEV = 2


entity_rate = 0.1
operator_rate = 0.02
epsilon = 1e-06


def passed_along(array, axis, by):
    peers = lax.axis_size(axis)
    return lax.ppermute(array, axis, [(i, (i + by) % peers) for i in range(peers)])


def place_slots(relation_ids, capacity):
    count_edges = relation_ids.shape[0]
    ordering = jnp.argsort(relation_ids, stable=True)
    ranked = relation_ids[ordering]
    leading = jnp.searchsorted(ranked, ranked, side="left")
    within = jnp.arange(count_edges, dtype=jnp.int32) - leading
    position = jnp.zeros((count_edges,), jnp.int32).at[ordering].set(within)
    return relation_ids * capacity + position


def score_grads(transformed, target_ids, negative_ids, table_rows):
    target_rows = jnp.take(table_rows, target_ids, axis=0)
    positive = jnp.sum(transformed.astype(jnp.float32) * target_rows.astype(jnp.float32), axis=-1)
    positive_grad = -jax.nn.sigmoid(-positive)
    width = transformed.shape[1]
    blocks = transformed.reshape(-1, SPAN, width)
    negative_count = negative_ids.shape[1]

    def span_step(running, pieces):
        query_block, negative_block = pieces
        negative_rows = jnp.take(table_rows, negative_block, axis=0)
        scores = lax.dot_general(
            query_block, negative_rows, (((1,), (1,)), ((), ())), preferred_element_type=jnp.float32
        )
        negative_grad = (jax.nn.sigmoid(scores) / negative_count).astype(jnp.bfloat16)
        query_part = jnp.dot(negative_grad, negative_rows, preferred_element_type=jnp.float32)
        row_update = lax.dot_general(
            negative_grad, query_block, (((0,), (0,)), ((), ())), preferred_element_type=jnp.float32
        )
        return (running.at[negative_block].add(row_update), query_part)

    starting = jnp.zeros((table_rows.shape[0], width), jnp.float32)
    negative_total, query_parts = lax.scan(span_step, starting, (blocks, negative_ids))
    query_grad = (
        positive_grad[:, None] * target_rows.astype(jnp.float32) + query_parts.reshape(-1, width)
    ).astype(jnp.bfloat16)
    target_grad = negative_total.at[target_ids].add(
        positive_grad[:, None] * transformed.astype(jnp.float32)
    )
    return (query_grad, target_grad)


def row_adagrad(weights, moments, gradient):
    fresh_moments = moments + jnp.mean(gradient * gradient, axis=-1)
    updated = weights - entity_rate * gradient / (jnp.sqrt(fresh_moments)[:, None] + epsilon)
    return (updated, fresh_moments)


def dense_adagrad(weights, moments, gradient):
    fresh_moments = moments + gradient * gradient
    updated = weights - operator_rate * gradient / (jnp.sqrt(fresh_moments) + epsilon)
    return (updated, fresh_moments)


def exchanged_shards(
    entity_table,
    entity_state,
    operators,
    operator_state,
    sources,
    destinations,
    relations,
    negatives,
):
    groups = lax.axis_size("ent")
    relation_count = REL_DEV * groups
    capacity = max(2, (2 * EDGE_DEV + relation_count - 1) // relation_count)
    width = entity_table.shape[1]
    table_half = entity_table.astype(jnp.bfloat16)
    operators_half = operators.astype(jnp.bfloat16)
    slot_index = place_slots(relations[:, 0], capacity)
    source_rows = jnp.take(table_half, sources, axis=0)
    outgoing = (
        jnp.zeros((relation_count * capacity, width), jnp.bfloat16).at[slot_index].set(source_rows)
    )
    outgoing = outgoing.reshape(groups, REL_DEV, capacity, width)
    arrived = lax.all_to_all(outgoing, "ent", split_axis=0, concat_axis=0, tiled=True)
    result = jnp.einsum(
        "srmd,rdk->srmk", arrived, operators_half, preferred_element_type=jnp.float32
    ).astype(jnp.bfloat16)
    returned = lax.all_to_all(result, "ent", split_axis=0, concat_axis=0, tiled=True)
    transformed_slots = returned
    transformed = jnp.take(transformed_slots.reshape(-1, width), slot_index, axis=0)
    neighbour_table = passed_along(table_half, "ent", -1)
    query_grad, target_grad = score_grads(transformed, destinations, negatives, neighbour_table)
    home_grad = passed_along(target_grad, "ent", 1)
    grad_slots = (
        jnp.zeros((relation_count * capacity, width), jnp.bfloat16).at[slot_index].set(query_grad)
    )
    grad_slots = grad_slots.reshape(groups, REL_DEV, capacity, width)
    arrived_grads = lax.all_to_all(grad_slots, "ent", split_axis=0, concat_axis=0, tiled=True)
    source_grads = jnp.einsum(
        "srmk,rdk->srmd", arrived_grads, operators_half, preferred_element_type=jnp.float32
    ).astype(jnp.bfloat16)
    returned = lax.all_to_all(source_grads, "ent", split_axis=0, concat_axis=0, tiled=True)
    operator_grad = jnp.einsum(
        "srmd,srmk->rdk", arrived, arrived_grads, preferred_element_type=jnp.float32
    )
    source_grad = jnp.take(returned.reshape(-1, width), slot_index, axis=0)
    entity_grad = (
        jnp.zeros(entity_table.shape, jnp.float32).at[sources].add(source_grad.astype(jnp.float32))
        + home_grad
    )
    total_grad, total_operator = lax.psum((entity_grad, operator_grad), "rep")
    new_table, new_entity_state = row_adagrad(entity_table, entity_state, total_grad)
    new_operators, new_operator_state = dense_adagrad(operators, operator_state, total_operator)
    return (new_table, new_entity_state, new_operators, new_operator_state)


bf16 = jnp.bfloat16
f32 = jnp.float32
CORES = 2
LANES = 128
RING = (0, 2, 4, 6, 7, 5, 3, 1)
PLACE = tuple(RING.index(e) for e in range(8))
SLOTS = 32
QUARTER = 64
VMEM = pltpu.VMEM
SMEM = pltpu.SMEM
NT = (((1,), (1,)), ((), ()))
TN = (((0,), (0,)), ((), ()))


def dot(a, b, dims=(((1,), (0,)), ((), ()))):
    return lax.dot_general(a, b, dims, preferred_element_type=f32)


def lanes_of(shape):
    return lax.broadcasted_iota(jnp.int32, shape, 1)


def rows_of(shape):
    return lax.broadcasted_iota(jnp.int32, shape, 0)


def one_hot(mask):
    return jnp.where(mask, 1.0, 0.0).astype(bf16)


def call(body, outs, name, flops, size, operands, scratch=(), grid=None, in_specs=None, out_specs=None):
    spaces = [pl.BlockSpec(memory_space=SMEM)] + [pl.BlockSpec(memory_space=VMEM)] * (len(operands) - 1)
    extra = {} if grid is None else {"grid": grid}
    return pl.pallas_call(
        body,
        out_shape=outs,
        in_specs=spaces if in_specs is None else in_specs,
        out_specs=[pl.BlockSpec(memory_space=VMEM)] * len(outs) if out_specs is None else out_specs,
        scratch_shapes=list(scratch),
        name=name,
        cost_estimate=pl.CostEstimate(flops=flops, bytes_accessed=size, transcendentals=0),
        compiler_params=pltpu.CompilerParams(vmem_limit_bytes=44 * 2**20),
        **extra,
    )(*operands)


def slot_kernel(count, scalars, own, near, far, across, table, slotted, turned, columns, rows, counts):
    reps, _, edges = columns.shape[0], None, columns.shape[1]
    buffers = (own, near, far, across)
    places = slotted.shape[1]
    me = scalars[1]
    before = one_hot(rows_of((edges, edges)) > lanes_of((edges, edges)))
    for m in range(reps):
        block = lax.bitwise_xor(me, m)
        ids = buffers[m][...]
        relation = ids[2:3]
        local = jnp.zeros_like(relation)
        for r in range(count):
            local = jnp.where(relation == r, scalars[11 + r], local)
        stacked = jnp.concatenate([ids[0:2], local, ids[3:8]], axis=0).astype(f32)
        standing = stacked.T
        local_column = standing[:, 2:3].astype(jnp.int32)
        named = lanes_of((edges, LANES)) == local_column
        ahead = dot(before, one_hot(named))
        slot = local_column.astype(f32) * SLOTS + jnp.sum(
            jnp.where(named, ahead, 0.0), axis=1, keepdims=True
        )
        standing = jnp.where(lanes_of(standing.shape) == 2, slot, standing)
        lying = standing.T
        columns[block] = standing
        rows[block] = lying
        picked = one_hot(
            lanes_of((edges, table.shape[0])) == standing[:, 0:1].astype(jnp.int32)
        )
        source_rows = dot(picked, table[...]).astype(bf16)
        into = one_hot(rows_of((places * SLOTS, edges)) == lying[2:3].astype(jnp.int32))
        slotted[block] = dot(into, source_rows).astype(bf16).reshape(places, SLOTS, -1)
        tally = jnp.zeros((8, LANES), f32)
        for k in range(3, 7):
            drawn = ids[k : k + 1]
            high = one_hot(rows_of((8, edges)) == lax.shift_right_arithmetic(drawn, 7))
            low = one_hot(rows_of((LANES, edges)) == lax.bitwise_and(drawn, LANES - 1))
            tally = tally + dot(high, low, NT)
        counts[block] = jnp.concatenate([tally[k : k + 1] for k in range(8)], axis=1)
    for m in range(places // 2):
        pair = slotted[:, 2 * m : 2 * m + 2].reshape(reps * 2 * SLOTS, -1)
        turned[m] = pair.astype(f32).T.astype(bf16)


def score_kernel(
    negative_count, scalars, o0, a1, a2, a3, a4, b4, b3, b2, b1, slotted, turned, columns, rows, counts,
    mine, other, outgoing, transformed, weights, scaled, scaled_rest, query, table, moved,
):
    step = pl.program_id(0)
    core, me = scalars[0], scalars[1]
    reps = slotted.shape[0]
    places = slotted.shape[1]
    width = table.shape[1]
    half = mine.shape[0]
    edges = columns.shape[1]
    entities = table.shape[0]

    @pl.when(step == 0)
    def _():
        table[pl.ds(pl.multiple_of(core * half, half), half)] = mine[...]
        table[pl.ds(pl.multiple_of((1 - core) * half, half), half)] = other[...]
        for place, op in enumerate(operator_list(o0, a1, a2, a3, a4, b4, b3, b2, b1)):
            given = slotted[:, place].reshape(reps * SLOTS, width)
            moved[:, place] = dot(given, op()).astype(bf16).reshape(reps, SLOTS, width)

    standing = columns[step].astype(jnp.int32)
    out_of = one_hot(lanes_of((edges, places * SLOTS)) == standing[:, 2:3])
    made = dot(out_of, moved[step].reshape(places * SLOTS, width))
    made_half = made.astype(bf16)
    scores = dot(made_half, table[...], NT)
    aimed = lanes_of((edges, entities)) == standing[:, 1:2]
    positive = jnp.sum(jnp.where(aimed, scores, 0.0), axis=1, keepdims=True)
    positive_grad = -(0.5 * jnp.tanh(-0.5 * positive) + 0.5)
    share = (0.5 * jnp.tanh(0.5 * scores) + 0.5) * (1.0 / negative_count)
    weighted = (share.astype(bf16).astype(f32) * counts[step]).astype(bf16)
    target_rows = dot(one_hot(aimed), table[...])
    asked = (positive_grad * target_rows + dot(weighted, table[...])).astype(bf16)
    push = positive_grad * made
    push_half = push.astype(bf16)
    transformed[0] = made_half
    weights[0] = weighted
    scaled[0] = push_half
    scaled_rest[0] = (push - push_half.astype(f32)).astype(bf16)
    query[0] = asked
    chosen_lane = lanes_of((width, LANES)) % QUARTER
    quarter = width // reps
    chosen = one_hot(
        (rows_of((width, LANES)) == chosen_lane + me * quarter) & (chosen_lane < quarter)
    )
    part = dot(asked, chosen).astype(bf16)
    into = one_hot(
        rows_of((places * SLOTS, edges)) == rows[step][2:3].astype(jnp.int32)
    )
    moved[step, :, :, 0:LANES] = dot(into, part).astype(bf16).reshape(places, SLOTS, LANES)

    @pl.when(step == reps - 1)
    def _():
        size = reps * 2 * SLOTS
        parity = lax.bitwise_and(lax.shift_right_logical(rows_of((size, LANES)), 5), 1)
        side = lax.shift_right_logical(lanes_of((size, LANES)), 6)
        for m in range(places // 2):
            pair = moved[:, 2 * m : 2 * m + 2, :, 0:LANES].reshape(size, LANES)
            kept = side == (lax.bitwise_xor(parity, core) if m == places // 4 else parity)
            pair = jnp.where(kept, pair.astype(f32), 0.0).astype(bf16)
            outgoing[scalars[3 + m]] = dot(turned[m], pair).astype(bf16)


def operator_list(o0, a1, a2, a3, a4, b4, b3, b2, b1):
    listed = [(o0, 0), (o0, 1)]
    for ref in (a1, a2, a3):
        listed += [(ref, 0), (ref, 1)]
    listed += [(a4, 0), (b4, 0)]
    for ref in (b3, b2, b1):
        listed += [(ref, 0), (ref, 1)]
    return [lambda ref=ref, i=i: ref[i] for ref, i in listed]


def return_kernel(
    scalars, o0, a1, a2, a3, a4, b4, b3, b2, b1, columns, rows, transformed, weights, scaled, scaled_rest,
    query, target_half, source_total, held, total,
):
    step = pl.program_id(0)
    core = scalars[0]
    reps, places = pl.num_programs(0), held.shape[1]
    width = query.shape[2]
    edges = columns.shape[1]
    entities = source_total.shape[0]
    half = target_half.shape[0]
    lying = rows[step].astype(jnp.int32)
    standing = columns[step].astype(jnp.int32)
    aimed = one_hot(lanes_of((edges, entities)) == standing[:, 1:2])
    sides = jnp.concatenate([transformed[0], scaled[0], scaled_rest[0]], axis=0)
    faces = jnp.concatenate([weights[0], aimed, aimed], axis=0)
    grown = dot(sides, faces, TN)

    @pl.when(step == 0)
    def _():
        total[...] = grown

    @pl.when(step > 0)
    def _():
        total[...] += grown

    into = one_hot(rows_of((places * SLOTS, edges)) == lying[2:3])
    held[step] = dot(into, query[0]).astype(bf16).reshape(places, SLOTS, width)

    @pl.when(step == held.shape[0] - 1)
    def _():
        whole = total[...].T
        target_half[...] = jnp.where(core == 0, whole[:half], whole[half:]).astype(bf16)
        for place, op in enumerate(operator_list(o0, a1, a2, a3, a4, b4, b3, b2, b1)):
            given = held[:, place].reshape(-1, width)
            held[:, place] = dot(given, op(), NT).astype(bf16).reshape(-1, SLOTS, width)
        summed = jnp.zeros((entities, width), f32)
        for b in range(held.shape[0]):
            out_of = one_hot(
                lanes_of((edges, places * SLOTS)) == columns[b][:, 2:3].astype(jnp.int32)
            )
            back = dot(out_of, held[b].reshape(places * SLOTS, width)).astype(bf16)
            spread = one_hot(rows_of((entities, edges)) == rows[b][0:1].astype(jnp.int32))
            summed = summed + dot(spread, back)
        source_total[...] = summed


def entity_kernel(scalars, source_total, mine, other, table, state, new_table, new_state, gradient):
    core = scalars[0]
    half = mine.shape[0]
    width = table.shape[1]
    for ref, side in ((mine, core), (other, 1 - core)):
        at = pl.ds(pl.multiple_of(side * half, half), half)
        gradient[at] = source_total[at] + ref[...].astype(f32)
    old = state[...].T
    fresh = []
    for k in range(table.shape[0] // LANES):
        at = slice(k * LANES, (k + 1) * LANES)
        g = gradient[at]
        moments = old[:, k : k + 1] + jnp.sum(g * g, axis=1, keepdims=True) * (1.0 / width)
        fresh.append(moments)
        new_table[at] = table[at] - g * (entity_rate / (jnp.sqrt(moments) + epsilon))
    new_state[...] = jnp.concatenate(fresh, axis=1).T


def operator_kernel(scalars, own, near, far, across, operators, state, new_operators, new_state):
    me = scalars[1]
    width = operators.shape[1]
    quarter = width // 4
    buffers = (own, near, far, across)
    lane = rows_of((LANES, width))
    inside = lane % QUARTER
    for i in range(operators.shape[0]):
        g = jnp.zeros((width, width), f32)
        for m in range(4):
            starting = lax.bitwise_xor(me, m) * quarter
            put = one_hot(
                (lane // QUARTER == i)
                & (inside < quarter)
                & (inside + starting == lanes_of((LANES, width)))
            )
            g = g + dot(buffers[m][...], put)
        moments = state[i] + g * g
        new_state[i] = moments
        new_operators[i] = operators[i] - operator_rate * g / (jnp.sqrt(moments) + epsilon)


def rep_swapped(array, by):
    peers = lax.axis_size("rep")
    return lax.ppermute(array, "rep", [(i, i ^ by) for i in range(peers)])


def ring_step(array):
    groups, reps = lax.axis_size("ent"), lax.axis_size("rep")
    pairs = []
    for e in range(groups):
        for r in range(reps):
            to = RING[(PLACE[e] + (1 if r % CORES == 0 else -1)) % groups]
            pairs.append((e * reps + r, to * reps + r))
    return lax.ppermute(array, ("ent", "rep"), pairs)


def gathered_shards(
    entity_table, entity_state, operators, operator_state, sources, destinations, relations, negatives
):
    groups, reps = lax.axis_size("ent"), lax.axis_size("rep")
    entities, width = entity_table.shape
    edges = sources.shape[0]
    relation_count = groups * operators.shape[0]
    half = entities // CORES
    ent, rep = lax.axis_index("ent"), lax.axis_index("rep")
    core = rep % CORES
    sign = jnp.where(core == 0, -1, 1)
    place = jnp.asarray(PLACE, jnp.int32)
    here = place[ent]
    owner_at = jnp.asarray(RING, jnp.int32)[(here + sign * jnp.arange(groups)) % groups]
    offset_of = (sign * (jnp.repeat(place, operators.shape[0]) - here)) % groups
    parity = jnp.arange(relation_count) % 2
    local_of = 2 * offset_of + jnp.where(offset_of == groups // 2, parity ^ core, parity)
    scalars = jnp.concatenate(
        [jnp.stack([core, rep, sign]), owner_at, local_of]
    ).astype(jnp.int32)

    operators_half = operators.astype(bf16)
    table_half = entity_table.astype(bf16)
    ids = jnp.concatenate(
        [
            sources,
            destinations,
            relations[:, 0],
            negatives[0],
            jnp.full((5 * edges - negatives.shape[1],), -1, jnp.int32),
        ]
    ).reshape(8, edges)
    others = [rep_swapped(ids, by) for by in (1, 2, 3)]
    a1 = ring_step(operators_half)
    own_half = lax.dynamic_slice_in_dim(table_half, core * half, half, 0)
    mine = passed_along(own_half, "ent", -1)
    b1 = rep_swapped(a1, 1)
    a2 = ring_step(a1)
    other = rep_swapped(mine, 1)
    b2 = rep_swapped(a2, 1)
    a3 = ring_step(a2)
    b3 = rep_swapped(a3, 1)
    a4 = ring_step(lax.dynamic_slice_in_dim(a3, core, 1, 0))
    b4 = rep_swapped(a4, 1)
    gathered = (operators_half, a1, a2, a3, a4, b4, b3, b2, b1)

    places = relation_count
    slot_out = [
        jax.ShapeDtypeStruct((reps, places, SLOTS, width), bf16),
        jax.ShapeDtypeStruct((places // 2, width, reps * 2 * SLOTS), bf16),
        jax.ShapeDtypeStruct((reps, edges, 8), f32),
        jax.ShapeDtypeStruct((reps, 8, edges), f32),
        jax.ShapeDtypeStruct((reps, 1, entities), f32),
    ]
    slotted, turned, columns, rows, counts = call(
        functools.partial(slot_kernel, relation_count), slot_out, "slots", 10**9, 10**7,
        (scalars, ids, *others, table_half),
    )
    whole = pl.BlockSpec(memory_space=VMEM)
    by_block = lambda a, b: pl.BlockSpec((1, a, b), lambda i: (i, 0, 0))
    score_out = [
        jax.ShapeDtypeStruct((groups, width, LANES), bf16),
        jax.ShapeDtypeStruct((reps, edges, width), bf16),
        jax.ShapeDtypeStruct((reps, edges, entities), bf16),
        jax.ShapeDtypeStruct((reps, edges, width), bf16),
        jax.ShapeDtypeStruct((reps, edges, width), bf16),
        jax.ShapeDtypeStruct((reps, edges, width), bf16),
    ]
    operands = (scalars, *gathered, slotted, turned, columns, rows, counts, mine, other)
    rowwise = by_block(edges, width)
    outgoing, *kept = call(
        functools.partial(score_kernel, negatives.shape[1]), score_out, "scores", 3 * 10**9, 2 * 10**7,
        operands,
        scratch=[VMEM((entities, width), bf16), VMEM((reps, places, SLOTS, width), bf16)],
        grid=(reps,),
        in_specs=[pl.BlockSpec(memory_space=SMEM)] + [whole] * (len(operands) - 1),
        out_specs=[whole, rowwise, by_block(edges, entities), rowwise, rowwise, rowwise],
    )
    arrived = lax.all_to_all(outgoing, "ent", split_axis=0, concat_axis=0, tiled=True)
    operands = (scalars, *gathered, columns, rows, *kept)
    target_half, source_total = call(
        return_kernel,
        [jax.ShapeDtypeStruct((half, width), bf16), jax.ShapeDtypeStruct((entities, width), f32)],
        "returns", 3 * 10**9, 2 * 10**7, operands,
        scratch=[VMEM((reps, places, SLOTS, width), bf16), VMEM((width, entities), f32)],
        grid=(reps,),
        in_specs=[pl.BlockSpec(memory_space=SMEM)] + [whole] * (len(operands) - 6)
        + [rowwise, by_block(edges, entities), rowwise, rowwise, rowwise],
        out_specs=[whole, whole],
    )
    home_mine = passed_along(target_half, "ent", 1)
    home_other = rep_swapped(home_mine, 1)
    quarter = jnp.sum(arrived.astype(f32), axis=0).astype(bf16)
    quarters = [rep_swapped(quarter, by) for by in (1, 2, 3)]
    new_table, new_state = call(
        entity_kernel,
        [
            jax.ShapeDtypeStruct((entities, width), f32),
            jax.ShapeDtypeStruct((entities // LANES, LANES), f32),
        ],
        "entity_update", 10**7, 4 * 10**6,
        (scalars, source_total, home_mine, home_other, entity_table, entity_state.reshape(-1, LANES)),
        scratch=[VMEM((entities, width), f32)],
    )
    new_operators, new_operator_state = call(
        operator_kernel,
        [jax.ShapeDtypeStruct(operators.shape, f32)] * 2,
        "operator_update", 10**7, 2 * 10**6,
        (scalars, quarter, *quarters, operators, operator_state),
    )
    return (new_table, new_state.reshape(-1), new_operators, new_operator_state)


def solution(mesh):
    placed = (
        P("ent", None),
        P("ent"),
        P("ent", None, None),
        P("ent", None, None),
        P(("ent", "rep")),
        P(("ent", "rep")),
        P(("ent", "rep"), None),
        P(("ent", "rep"), None),
    )
    small = mesh.shape["ent"] == len(RING) and mesh.shape["rep"] == 2 * CORES
    return jax.shard_map(
        gathered_shards if small else exchanged_shards,
        mesh=mesh,
        in_specs=placed,
        out_specs=(P("ent", None), P("ent"), P("ent", None, None), P("ent", None, None)),
        check_vma=False,
    )
```

```python
import functools

import jax
import jax.numpy as jnp
from jax import lax
from jax.experimental import pallas as pl
from jax.experimental.pallas import tpu as pltpu
from jax.sharding import PartitionSpec as P

SPAN = 256
EDGE_DEV = 256
REL_DEV = 2


entity_rate = 0.1
operator_rate = 0.02
epsilon = 1e-06


def passed_along(array, axis, by):
    peers = lax.axis_size(axis)
    return lax.ppermute(array, axis, [(i, (i + by) % peers) for i in range(peers)])


def place_slots(relation_ids, capacity):
    count_edges = relation_ids.shape[0]
    ordering = jnp.argsort(relation_ids, stable=True)
    ranked = relation_ids[ordering]
    leading = jnp.searchsorted(ranked, ranked, side="left")
    within = jnp.arange(count_edges, dtype=jnp.int32) - leading
    position = jnp.zeros((count_edges,), jnp.int32).at[ordering].set(within)
    return relation_ids * capacity + position


def score_grads(transformed, target_ids, negative_ids, table_rows):
    target_rows = jnp.take(table_rows, target_ids, axis=0)
    positive = jnp.sum(transformed.astype(jnp.float32) * target_rows.astype(jnp.float32), axis=-1)
    positive_grad = -jax.nn.sigmoid(-positive)
    width = transformed.shape[1]
    blocks = transformed.reshape(-1, SPAN, width)
    negative_count = negative_ids.shape[1]

    def span_step(running, pieces):
        query_block, negative_block = pieces
        negative_rows = jnp.take(table_rows, negative_block, axis=0)
        scores = lax.dot_general(
            query_block, negative_rows, (((1,), (1,)), ((), ())), preferred_element_type=jnp.float32
        )
        negative_grad = (jax.nn.sigmoid(scores) / negative_count).astype(jnp.bfloat16)
        query_part = jnp.dot(negative_grad, negative_rows, preferred_element_type=jnp.float32)
        row_update = lax.dot_general(
            negative_grad, query_block, (((0,), (0,)), ((), ())), preferred_element_type=jnp.float32
        )
        return (running.at[negative_block].add(row_update), query_part)

    starting = jnp.zeros((table_rows.shape[0], width), jnp.float32)
    negative_total, query_parts = lax.scan(span_step, starting, (blocks, negative_ids))
    query_grad = (
        positive_grad[:, None] * target_rows.astype(jnp.float32) + query_parts.reshape(-1, width)
    ).astype(jnp.bfloat16)
    target_grad = negative_total.at[target_ids].add(
        positive_grad[:, None] * transformed.astype(jnp.float32)
    )
    return (query_grad, target_grad)


def row_adagrad(weights, moments, gradient):
    fresh_moments = moments + jnp.mean(gradient * gradient, axis=-1)
    updated = weights - entity_rate * gradient / (jnp.sqrt(fresh_moments)[:, None] + epsilon)
    return (updated, fresh_moments)


def dense_adagrad(weights, moments, gradient):
    fresh_moments = moments + gradient * gradient
    updated = weights - operator_rate * gradient / (jnp.sqrt(fresh_moments) + epsilon)
    return (updated, fresh_moments)


def exchanged_shards(
    entity_table,
    entity_state,
    operators,
    operator_state,
    sources,
    destinations,
    relations,
    negatives,
):
    groups = lax.axis_size("ent")
    relation_count = REL_DEV * groups
    capacity = max(2, (2 * EDGE_DEV + relation_count - 1) // relation_count)
    width = entity_table.shape[1]
    table_half = entity_table.astype(jnp.bfloat16)
    operators_half = operators.astype(jnp.bfloat16)
    slot_index = place_slots(relations[:, 0], capacity)
    source_rows = jnp.take(table_half, sources, axis=0)
    outgoing = (
        jnp.zeros((relation_count * capacity, width), jnp.bfloat16).at[slot_index].set(source_rows)
    )
    outgoing = outgoing.reshape(groups, REL_DEV, capacity, width)
    arrived = lax.all_to_all(outgoing, "ent", split_axis=0, concat_axis=0, tiled=True)
    result = jnp.einsum(
        "srmd,rdk->srmk", arrived, operators_half, preferred_element_type=jnp.float32
    ).astype(jnp.bfloat16)
    returned = lax.all_to_all(result, "ent", split_axis=0, concat_axis=0, tiled=True)
    transformed_slots = returned
    transformed = jnp.take(transformed_slots.reshape(-1, width), slot_index, axis=0)
    neighbour_table = passed_along(table_half, "ent", -1)
    query_grad, target_grad = score_grads(transformed, destinations, negatives, neighbour_table)
    home_grad = passed_along(target_grad, "ent", 1)
    grad_slots = (
        jnp.zeros((relation_count * capacity, width), jnp.bfloat16).at[slot_index].set(query_grad)
    )
    grad_slots = grad_slots.reshape(groups, REL_DEV, capacity, width)
    arrived_grads = lax.all_to_all(grad_slots, "ent", split_axis=0, concat_axis=0, tiled=True)
    source_grads = jnp.einsum(
        "srmk,rdk->srmd", arrived_grads, operators_half, preferred_element_type=jnp.float32
    ).astype(jnp.bfloat16)
    returned = lax.all_to_all(source_grads, "ent", split_axis=0, concat_axis=0, tiled=True)
    operator_grad = jnp.einsum(
        "srmd,srmk->rdk", arrived, arrived_grads, preferred_element_type=jnp.float32
    )
    source_grad = jnp.take(returned.reshape(-1, width), slot_index, axis=0)
    entity_grad = (
        jnp.zeros(entity_table.shape, jnp.float32).at[sources].add(source_grad.astype(jnp.float32))
        + home_grad
    )
    total_grad, total_operator = lax.psum((entity_grad, operator_grad), "rep")
    new_table, new_entity_state = row_adagrad(entity_table, entity_state, total_grad)
    new_operators, new_operator_state = dense_adagrad(operators, operator_state, total_operator)
    return (new_table, new_entity_state, new_operators, new_operator_state)


bf16 = jnp.bfloat16
f32 = jnp.float32
CORES = 2
LANES = 128
RING = (0, 2, 4, 6, 7, 5, 3, 1)
PLACE = tuple(RING.index(e) for e in range(8))
SLOTS = 32
QUARTER = 64
VMEM = pltpu.VMEM
NT = (((1,), (1,)), ((), ()))
TN = (((0,), (0,)), ((), ()))


def dot(a, b, dims=(((1,), (0,)), ((), ()))):
    return lax.dot_general(a, b, dims, preferred_element_type=f32)


def lanes_of(shape):
    return lax.broadcasted_iota(jnp.int32, shape, 1)


def rows_of(shape):
    return lax.broadcasted_iota(jnp.int32, shape, 0)


def one_hot(mask):
    return jnp.where(mask, 1.0, 0.0).astype(bf16)


def call(body, outs, name, flops, size, operands, limit=16, scratch=()):
    whole = pl.BlockSpec(memory_space=VMEM)
    return pl.pallas_call(
        body,
        out_shape=outs,
        in_specs=[whole] * len(operands),
        out_specs=[whole] * len(outs),
        scratch_shapes=list(scratch),
        name=name,
        cost_estimate=pl.CostEstimate(flops=flops, bytes_accessed=size, transcendentals=0),
        compiler_params=pltpu.CompilerParams(vmem_limit_bytes=limit * 2**20),
    )(*operands)


def chosen_from(listed, at):
    found = jnp.zeros_like(at)
    for i, value in enumerate(listed):
        found = jnp.where(at == i, value, found)
    return found


def position():
    rep = lax.axis_index("rep")
    core = lax.rem(rep, CORES)
    return core, rep, chosen_from(PLACE, lax.axis_index("ent")), 2 * core - 1


def slot_kernel(own, near, far, across, table, slotted, turned, rows, counts):
    reps, _, edges = rows.shape
    buffers = (own, near, far, across)
    places = slotted.shape[1]
    core, me, here, sign = position()
    ring = len(RING)
    before = one_hot(rows_of((edges, edges)) > lanes_of((edges, edges)))
    for m in range(reps):
        block = lax.bitwise_xor(me, m)
        ids = buffers[m][...]
        relation = ids[2:3]
        offset = lax.bitwise_and(
            sign * (chosen_from(PLACE, lax.shift_right_logical(relation, 1)) - here), ring - 1
        )
        parity = lax.bitwise_and(relation, 1)
        local = 2 * offset + jnp.where(
            offset == ring // 2, lax.bitwise_xor(parity, core), parity
        )
        stacked = jnp.concatenate([ids[0:2], local, ids[3:8]], axis=0).astype(f32)
        standing = stacked.T
        local_column = standing[:, 2:3].astype(jnp.int32)
        named = lanes_of((edges, LANES)) == local_column
        ahead = dot(before, one_hot(named))
        slot = local_column.astype(f32) * SLOTS + jnp.sum(
            jnp.where(named, ahead, 0.0), axis=1, keepdims=True
        )
        standing = jnp.where(lanes_of(standing.shape) == 2, slot, standing)
        lying = standing.T
        rows[block] = lying
        picked = one_hot(
            lanes_of((edges, table.shape[1])) == standing[:, 0:1].astype(jnp.int32)
        )
        source_rows = dot(picked, table[...], NT).astype(bf16)
        into = one_hot(rows_of((places * SLOTS, edges)) == lying[2:3].astype(jnp.int32))
        slotted[block] = dot(into, source_rows).astype(bf16).reshape(places, SLOTS, -1)
        tally = jnp.zeros((8, LANES), f32)
        for k in range(3, 7):
            drawn = ids[k : k + 1]
            high = one_hot(rows_of((8, edges)) == lax.shift_right_arithmetic(drawn, 7))
            low = one_hot(rows_of((LANES, edges)) == lax.bitwise_and(drawn, LANES - 1))
            tally = tally + dot(high, low, NT)
        counts[block] = jnp.concatenate([tally[k : k + 1] for k in range(8)], axis=1)
    for m in range(places // 2):
        pair = slotted[:, 2 * m : 2 * m + 2].reshape(reps * 2 * SLOTS, -1)
        turned[m] = pair.astype(f32).T.astype(bf16)


def score_kernel(
    negative_count, o0, a1, a2, a3, a4, b4, b3, b2, b1, slotted, turned, rows, counts, mine, other,
    s0, s1, s2, s3, s4, s5, s6, s7, weights, sides, query, table, moved,
):
    core, me, *_ = position()
    reps, places = slotted.shape[:2]
    width, entities = table.shape
    half = mine.shape[1]
    edges = rows.shape[2]
    table[:, pl.ds(pl.multiple_of(core * half, half), half)] = mine[...]
    table[:, pl.ds(pl.multiple_of((1 - core) * half, half), half)] = other[...]
    for place, op in enumerate(operator_list(o0, a1, a2, a3, a4, b4, b3, b2, b1)):
        given = slotted[:, place].reshape(reps * SLOTS, width)
        moved[:, place] = dot(given, op()).astype(bf16).reshape(reps, SLOTS, width)
    chosen_lane = lanes_of((width, LANES)) % QUARTER
    quarter = width // reps
    chosen = one_hot(
        (rows_of((width, LANES)) == chosen_lane + me * quarter) & (chosen_lane < quarter)
    )
    for b in range(reps):
        lying = rows[b]
        standing = lying.T.astype(jnp.int32)
        out_of = one_hot(lanes_of((edges, places * SLOTS)) == standing[:, 2:3])
        made = dot(out_of, moved[b].reshape(places * SLOTS, width))
        made_half = made.astype(bf16)
        scores = dot(made_half, table[...])
        aimed = lanes_of((edges, entities)) == standing[:, 1:2]
        positive = jnp.sum(jnp.where(aimed, scores, 0.0), axis=1, keepdims=True)
        positive_grad = -(0.5 * jnp.tanh(-0.5 * positive) + 0.5)
        share = (0.5 * jnp.tanh(0.5 * scores) + 0.5) * (1.0 / negative_count)
        weighted = (share.astype(bf16).astype(f32) * counts[b]).astype(bf16)
        target_rows = dot(one_hot(aimed), table[...], NT)
        asked = (positive_grad * target_rows + dot(weighted, table[...], NT)).astype(bf16)
        push = positive_grad * made
        push_half = push.astype(bf16)
        weights[b] = weighted
        sides[b, :edges] = made_half
        sides[b, edges : 2 * edges] = push_half
        sides[b, 2 * edges :] = (push - push_half.astype(f32)).astype(bf16)
        query[b] = asked
        part = dot(asked, chosen).astype(bf16)
        into = one_hot(rows_of((places * SLOTS, edges)) == lying[2:3].astype(jnp.int32))
        moved[b, :, :, 0:LANES] = dot(into, part).astype(bf16).reshape(places, SLOTS, LANES)
    size = reps * 2 * SLOTS
    parity = lax.bitwise_and(lax.shift_right_logical(rows_of((size, LANES)), 5), 1)
    side = lax.shift_right_logical(lanes_of((size, LANES)), 6)
    for m, outgoing in enumerate((s0, s1, s2, s3, s4, s5, s6, s7)):
        pair = moved[:, 2 * m : 2 * m + 2, :, 0:LANES].reshape(size, LANES)
        kept = side == (lax.bitwise_xor(parity, core) if m == places // 4 else parity)
        pair = jnp.where(kept, pair.astype(f32), 0.0).astype(bf16)
        outgoing[...] = dot(turned[m], pair).astype(bf16)


def operator_list(o0, a1, a2, a3, a4, b4, b3, b2, b1):
    listed = [(o0, 0), (o0, 1)]
    for ref in (a1, a2, a3):
        listed += [(ref, 0), (ref, 1)]
    listed += [(a4, 0), (b4, 0)]
    for ref in (b3, b2, b1):
        listed += [(ref, 0), (ref, 1)]
    return [lambda ref=ref, i=i: ref[i] for ref, i in listed]


def target_kernel(rows, weights, sides, target_half, total):
    core, *_ = position()
    half = target_half.shape[1]
    reps, edges, entities = weights.shape
    for b in range(reps):
        standing = rows[b].T.astype(jnp.int32)
        aimed = one_hot(lanes_of((edges, entities)) == standing[:, 1:2])
        faces = jnp.concatenate([weights[b], aimed, aimed], axis=0)
        grown = dot(sides[b], faces, TN)
        if b == 0:
            total[...] = grown
        else:
            total[...] += grown
    target_half[...] = total[:, pl.ds(pl.multiple_of(core * half, half), half)].astype(bf16)


def source_kernel(
    o0, a1, a2, a3, a4, b4, b3, b2, b1, rows, query, source_total, held
):
    reps, places, _, width = held.shape
    entities = source_total.shape[1]
    edges = rows.shape[2]
    for b in range(reps):
        into = one_hot(rows_of((places * SLOTS, edges)) == rows[b][2:3].astype(jnp.int32))
        held[b] = dot(into, query[b]).astype(bf16).reshape(places, SLOTS, width)
    for place, op in enumerate(operator_list(o0, a1, a2, a3, a4, b4, b3, b2, b1)):
        given = held[:, place].reshape(-1, width)
        held[:, place] = dot(given, op(), NT).astype(bf16).reshape(-1, SLOTS, width)
    for b in range(reps):
        standing = rows[b].T.astype(jnp.int32)
        out_of = one_hot(lanes_of((edges, places * SLOTS)) == standing[:, 2:3])
        back = dot(out_of, held[b].reshape(places * SLOTS, width)).astype(bf16)
        spread = one_hot(lanes_of((edges, entities)) == standing[:, 0:1])
        grown = dot(back, spread, TN)
        if b == 0:
            source_total[...] = grown
        else:
            source_total[...] += grown


def entity_kernel(source_total, mine, other, table, state, new_table, new_state):
    core, *_ = position()
    half = mine.shape[1]
    width = table.shape[0]
    for ref, side in ((mine, core), (other, 1 - core)):
        at = pl.ds(pl.multiple_of(side * half, half), half)
        g = source_total[:, at] + ref[...].astype(f32)
        moments = state[:, at] + jnp.sum(g * g, axis=0, keepdims=True) * (1.0 / width)
        new_state[:, at] = moments
        new_table[:, at] = table[:, at] - g * (entity_rate / (jnp.sqrt(moments) + epsilon))


def operator_kernel(own, near, far, across, operators, state, new_operators, new_state):
    _, me, *_ = position()
    width = operators.shape[1]
    quarter = width // 4
    buffers = (own, near, far, across)
    lane = rows_of((LANES, width))
    inside = lane % QUARTER
    for i in range(operators.shape[0]):
        g = jnp.zeros((width, width), f32)
        for m in range(4):
            starting = lax.bitwise_xor(me, m) * quarter
            put = one_hot(
                (lane // QUARTER == i)
                & (inside < quarter)
                & (inside + starting == lanes_of((LANES, width)))
            )
            g = g + dot(buffers[m][...], put)
        moments = state[i] + g * g
        new_state[i] = moments
        new_operators[i] = operators[i] - operator_rate * g / (jnp.sqrt(moments) + epsilon)


def rep_swapped(array, by):
    peers = lax.axis_size("rep")
    return lax.ppermute(array, "rep", [(i, i ^ by) for i in range(peers)])


def ring_step(array, steps=1):
    groups, reps = lax.axis_size("ent"), lax.axis_size("rep")
    pairs = []
    for e in range(groups):
        for r in range(reps):
            to = RING[(PLACE[e] + (steps if r % CORES == 0 else -steps)) % groups]
            pairs.append((e * reps + r, to * reps + r))
    return lax.ppermute(array, ("ent", "rep"), pairs)


def gathered_shards(
    entity_table, entity_state, operators, operator_state, sources, destinations, relations, negatives
):
    groups, reps = lax.axis_size("ent"), lax.axis_size("rep")
    entities, width = entity_table.shape
    edges = sources.shape[0]
    relation_count = groups * operators.shape[0]
    half = entities // CORES
    core = lax.axis_index("rep") % CORES

    operators_half = operators.astype(bf16)
    table = entity_table.T
    table_half = table.astype(bf16)
    ids = jnp.concatenate(
        [
            sources,
            destinations,
            relations[:, 0],
            negatives[0],
            jnp.full((5 * edges - negatives.shape[1],), -1, jnp.int32),
        ]
    ).reshape(8, edges)
    places = relation_count
    slot_out = [
        jax.ShapeDtypeStruct((reps, places, SLOTS, width), bf16),
        jax.ShapeDtypeStruct((places // 2, width, reps * 2 * SLOTS), bf16),
        jax.ShapeDtypeStruct((reps, 8, edges), f32),
        jax.ShapeDtypeStruct((reps, 1, entities), f32),
    ]
    a1 = ring_step(operators_half)
    others = [rep_swapped(ids, by) for by in (1, 2, 3)]
    own_half = lax.dynamic_slice_in_dim(table_half, core * half, half, 1)
    mine = passed_along(own_half, "ent", -1)
    a1, *others = lax.optimization_barrier((a1, *others))
    a2 = ring_step(a1)
    b1 = rep_swapped(a1, 1)
    slots = call(slot_kernel, slot_out, "slots", 10**9, 10**7, (ids, *others, table_half))
    a2, b1, mine, *slots = lax.optimization_barrier((a2, b1, mine, *slots))
    slotted, turned, rows, counts = slots
    a3 = ring_step(a2)
    other = rep_swapped(mine, 1)
    b2 = rep_swapped(a2, 1)
    a3, b2, other = lax.optimization_barrier((a3, b2, other))
    a4 = ring_step(lax.dynamic_slice_in_dim(a3, core, 1, 0))
    b3 = rep_swapped(a3, 1)
    a4, b3 = lax.optimization_barrier((a4, b3))
    b4 = rep_swapped(a4, 1)
    gathered = (operators_half, a1, a2, a3, a4, b4, b3, b2, b1)

    score_out = [jax.ShapeDtypeStruct((width, LANES), bf16)] * groups + [
        jax.ShapeDtypeStruct((reps, edges, entities), bf16),
        jax.ShapeDtypeStruct((reps, 3 * edges, width), bf16),
        jax.ShapeDtypeStruct((reps, edges, width), bf16),
    ]
    *outgoing, weights, sides, query = call(
        functools.partial(score_kernel, negatives.shape[1]), score_out, "scores", 3 * 10**9, 2 * 10**7,
        (*gathered, slotted, turned, rows, counts, mine, other),
        scratch=[VMEM((width, entities), bf16), VMEM((reps, places, SLOTS, width), bf16)],
    )
    arrived = [outgoing[0]] + [ring_step(part, -m) for m, part in enumerate(outgoing) if m > 0]
    (target_half,) = call(
        target_kernel,
        [jax.ShapeDtypeStruct((width, half), bf16)],
        "targets", 2 * 10**9, 10**7, (rows, weights, sides),
        scratch=[VMEM((width, entities), f32)],
    )
    (source_total,) = call(
        source_kernel,
        [jax.ShapeDtypeStruct((width, entities), f32)],
        "sources", 2 * 10**9, 10**7, (*gathered, rows, query),
        scratch=[VMEM((reps, places, SLOTS, width), bf16)],
    )
    home_mine = passed_along(target_half, "ent", 1)
    home_other = rep_swapped(home_mine, 1)
    quarter = sum(part.astype(f32) for part in arrived).astype(bf16)
    quarters = [rep_swapped(quarter, by) for by in (1, 2, 3)]
    new_table, new_state = call(
        entity_kernel,
        [
            jax.ShapeDtypeStruct((width, entities), f32),
            jax.ShapeDtypeStruct((1, entities), f32),
        ],
        "entity_update", 10**7, 4 * 10**6,
        (source_total, home_mine, home_other, table, entity_state.reshape(1, -1)),
    )
    new_operators, new_operator_state = call(
        operator_kernel,
        [jax.ShapeDtypeStruct(operators.shape, f32)] * 2,
        "operator_update", 10**7, 2 * 10**6,
        (quarter, *quarters, operators, operator_state),
    )
    return (new_table.T, new_state.reshape(-1), new_operators, new_operator_state)


def solution(mesh):
    placed = (
        P("ent", None),
        P("ent"),
        P("ent", None, None),
        P("ent", None, None),
        P(("ent", "rep")),
        P(("ent", "rep")),
        P(("ent", "rep"), None),
        P(("ent", "rep"), None),
    )
    small = mesh.shape["ent"] == len(RING) and mesh.shape["rep"] == 2 * CORES
    return jax.shard_map(
        gathered_shards if small else exchanged_shards,
        mesh=mesh,
        in_specs=placed,
        out_specs=(P("ent", None), P("ent"), P("ent", None, None), P("ent", None, None)),
        check_vma=False,
    )
```

```python
import functools

import jax
import jax.numpy as jnp
from jax import lax
from jax.experimental import pallas as pl
from jax.experimental.pallas import tpu as pltpu
from jax.sharding import PartitionSpec as P

SPAN = 256
EDGE_DEV = 256
REL_DEV = 2


entity_rate = 0.1
operator_rate = 0.02
epsilon = 1e-06


def passed_along(array, axis, by):
    peers = lax.axis_size(axis)
    return lax.ppermute(array, axis, [(i, (i + by) % peers) for i in range(peers)])


def place_slots(relation_ids, capacity):
    count_edges = relation_ids.shape[0]
    ordering = jnp.argsort(relation_ids, stable=True)
    ranked = relation_ids[ordering]
    leading = jnp.searchsorted(ranked, ranked, side="left")
    within = jnp.arange(count_edges, dtype=jnp.int32) - leading
    position = jnp.zeros((count_edges,), jnp.int32).at[ordering].set(within)
    return relation_ids * capacity + position


def score_grads(transformed, target_ids, negative_ids, table_rows):
    target_rows = jnp.take(table_rows, target_ids, axis=0)
    positive = jnp.sum(transformed.astype(jnp.float32) * target_rows.astype(jnp.float32), axis=-1)
    positive_grad = -jax.nn.sigmoid(-positive)
    width = transformed.shape[1]
    blocks = transformed.reshape(-1, SPAN, width)
    negative_count = negative_ids.shape[1]

    def span_step(running, pieces):
        query_block, negative_block = pieces
        negative_rows = jnp.take(table_rows, negative_block, axis=0)
        scores = lax.dot_general(
            query_block, negative_rows, (((1,), (1,)), ((), ())), preferred_element_type=jnp.float32
        )
        negative_grad = (jax.nn.sigmoid(scores) / negative_count).astype(jnp.bfloat16)
        query_part = jnp.dot(negative_grad, negative_rows, preferred_element_type=jnp.float32)
        row_update = lax.dot_general(
            negative_grad, query_block, (((0,), (0,)), ((), ())), preferred_element_type=jnp.float32
        )
        return (running.at[negative_block].add(row_update), query_part)

    starting = jnp.zeros((table_rows.shape[0], width), jnp.float32)
    negative_total, query_parts = lax.scan(span_step, starting, (blocks, negative_ids))
    query_grad = (
        positive_grad[:, None] * target_rows.astype(jnp.float32) + query_parts.reshape(-1, width)
    ).astype(jnp.bfloat16)
    target_grad = negative_total.at[target_ids].add(
        positive_grad[:, None] * transformed.astype(jnp.float32)
    )
    return (query_grad, target_grad)


def row_adagrad(weights, moments, gradient):
    fresh_moments = moments + jnp.mean(gradient * gradient, axis=-1)
    updated = weights - entity_rate * gradient / (jnp.sqrt(fresh_moments)[:, None] + epsilon)
    return (updated, fresh_moments)


def dense_adagrad(weights, moments, gradient):
    fresh_moments = moments + gradient * gradient
    updated = weights - operator_rate * gradient / (jnp.sqrt(fresh_moments) + epsilon)
    return (updated, fresh_moments)


def exchanged_shards(
    entity_table,
    entity_state,
    operators,
    operator_state,
    sources,
    destinations,
    relations,
    negatives,
):
    groups = lax.axis_size("ent")
    relation_count = REL_DEV * groups
    capacity = max(2, (2 * EDGE_DEV + relation_count - 1) // relation_count)
    width = entity_table.shape[1]
    table_half = entity_table.astype(jnp.bfloat16)
    operators_half = operators.astype(jnp.bfloat16)
    slot_index = place_slots(relations[:, 0], capacity)
    source_rows = jnp.take(table_half, sources, axis=0)
    outgoing = (
        jnp.zeros((relation_count * capacity, width), jnp.bfloat16).at[slot_index].set(source_rows)
    )
    outgoing = outgoing.reshape(groups, REL_DEV, capacity, width)
    arrived = lax.all_to_all(outgoing, "ent", split_axis=0, concat_axis=0, tiled=True)
    result = jnp.einsum(
        "srmd,rdk->srmk", arrived, operators_half, preferred_element_type=jnp.float32
    ).astype(jnp.bfloat16)
    returned = lax.all_to_all(result, "ent", split_axis=0, concat_axis=0, tiled=True)
    transformed_slots = returned
    transformed = jnp.take(transformed_slots.reshape(-1, width), slot_index, axis=0)
    neighbour_table = passed_along(table_half, "ent", -1)
    query_grad, target_grad = score_grads(transformed, destinations, negatives, neighbour_table)
    home_grad = passed_along(target_grad, "ent", 1)
    grad_slots = (
        jnp.zeros((relation_count * capacity, width), jnp.bfloat16).at[slot_index].set(query_grad)
    )
    grad_slots = grad_slots.reshape(groups, REL_DEV, capacity, width)
    arrived_grads = lax.all_to_all(grad_slots, "ent", split_axis=0, concat_axis=0, tiled=True)
    source_grads = jnp.einsum(
        "srmk,rdk->srmd", arrived_grads, operators_half, preferred_element_type=jnp.float32
    ).astype(jnp.bfloat16)
    returned = lax.all_to_all(source_grads, "ent", split_axis=0, concat_axis=0, tiled=True)
    operator_grad = jnp.einsum(
        "srmd,srmk->rdk", arrived, arrived_grads, preferred_element_type=jnp.float32
    )
    source_grad = jnp.take(returned.reshape(-1, width), slot_index, axis=0)
    entity_grad = (
        jnp.zeros(entity_table.shape, jnp.float32).at[sources].add(source_grad.astype(jnp.float32))
        + home_grad
    )
    total_grad, total_operator = lax.psum((entity_grad, operator_grad), "rep")
    new_table, new_entity_state = row_adagrad(entity_table, entity_state, total_grad)
    new_operators, new_operator_state = dense_adagrad(operators, operator_state, total_operator)
    return (new_table, new_entity_state, new_operators, new_operator_state)


bf16 = jnp.bfloat16
f32 = jnp.float32
CORES = 2
LANES = 128
RING = (0, 2, 4, 6, 7, 5, 3, 1)
PLACE = tuple(RING.index(e) for e in range(8))
SLOTS = 32
OFFSETS = ((0, 4), (3, 1), (5, 7), (2, 6))
VMEM = pltpu.VMEM
NT = (((1,), (1,)), ((), ()))
TN = (((0,), (0,)), ((), ()))


def dot(a, b, dims=(((1,), (0,)), ((), ()))):
    return lax.dot_general(a, b, dims, preferred_element_type=f32)


def lanes_of(shape):
    return lax.broadcasted_iota(jnp.int32, shape, 1)


def rows_of(shape):
    return lax.broadcasted_iota(jnp.int32, shape, 0)


def one_hot(mask):
    return jnp.where(mask, 1.0, 0.0).astype(bf16)


def call(body, outs, name, flops, size, operands, limit=16, scratch=(), far=()):
    whole = pl.BlockSpec(memory_space=VMEM)
    kept = pl.BlockSpec(memory_space=pl.ANY)
    return pl.pallas_call(
        body,
        out_shape=outs,
        in_specs=[kept if i in far else whole for i in range(len(operands))],
        out_specs=[whole] * len(outs),
        scratch_shapes=list(scratch),
        name=name,
        cost_estimate=pl.CostEstimate(flops=flops, bytes_accessed=size, transcendentals=0),
        compiler_params=pltpu.CompilerParams(vmem_limit_bytes=limit * 2**20),
    )(*operands)


def chosen_from(listed, at):
    found = jnp.zeros_like(at)
    for i, value in enumerate(listed):
        found = jnp.where(at == i, value, found)
    return found


def position():
    rep = lax.axis_index("rep")
    core = lax.rem(rep, CORES)
    return core, rep, chosen_from(PLACE, lax.axis_index("ent")), 2 * core - 1


def slot_kernel(own, near, far, across, table_far, slotted, rows, counts, table, got):
    fetch = pltpu.make_async_copy(table_far, table, got)
    fetch.start()
    core, me, here, sign = position()
    ring = len(RING)
    reps, _, edges = rows.shape
    places = slotted.shape[1]
    ids = [ref[...] for ref in (own, near, far, across)]
    before = one_hot(rows_of((edges, edges)) > lanes_of((edges, edges)))
    relation = jnp.concatenate([block[2:3] for block in ids], axis=0)
    offset = lax.bitwise_and(
        sign * (chosen_from(PLACE, lax.shift_right_logical(relation, 1)) - here), ring - 1
    )
    parity = lax.bitwise_and(relation, 1)
    local = 2 * offset + jnp.where(offset == ring // 2, lax.bitwise_xor(parity, core), parity)
    ends = [block[i : i + 1] for i in (0, 1) for block in ids]
    standing = jnp.concatenate([local, *ends], axis=0).astype(f32).T
    column = lambda i: standing[:, i : i + 1].astype(jnp.int32)
    named = [lanes_of((edges, LANES)) == column(m) for m in range(reps)]
    ahead = dot(before, one_hot(jnp.concatenate(named, axis=1)))
    slots = jnp.concatenate(
        [
            standing[:, m : m + 1] * SLOTS
            + jnp.sum(
                jnp.where(named[m], ahead[:, m * LANES : (m + 1) * LANES], 0.0), axis=1, keepdims=True
            )
            for m in range(reps)
        ],
        axis=1,
    ).T
    for m in range(reps):
        block = lax.bitwise_xor(me, m)
        lying = jnp.concatenate(
            [ids[m][0:2].astype(f32), slots[m : m + 1], ids[m][3:8].astype(f32)], axis=0
        )
        rows[block] = lying
        tally = jnp.zeros((8, LANES), f32)
        for k in range(3, 7):
            drawn = ids[m][k : k + 1]
            high = one_hot(rows_of((8, edges)) == lax.shift_right_arithmetic(drawn, 7))
            low = one_hot(rows_of((LANES, edges)) == lax.bitwise_and(drawn, LANES - 1))
            tally = tally + dot(high, low, NT)
        counts[block] = jnp.concatenate([tally[k : k + 1] for k in range(8)], axis=1)
    picked = [
        one_hot(lanes_of((edges, table.shape[1])) == column(reps + m)) for m in range(reps)
    ]
    fetch.wait()
    source_rows = dot(jnp.concatenate(picked, axis=0), table[...].astype(bf16), NT).astype(bf16)
    for m in range(reps):
        into = one_hot(rows_of((places * SLOTS, edges)) == slots[m : m + 1].astype(jnp.int32))
        given = dot(into, source_rows[m * edges : (m + 1) * edges]).astype(bf16)
        slotted[lax.bitwise_xor(me, m)] = given.reshape(places, SLOTS, -1)


def score_kernel(
    negative_count, o0, a1, a2, a3, a4, b4, b3, b2, b1, slotted, rows, counts, mine, other,
    s0, s1, s2, s3, weights, sides, query, table, moved, asking,
):
    core, me, *_ = position()
    reps, places = slotted.shape[:2]
    width, entities = table.shape
    half = mine.shape[1]
    edges = rows.shape[2]
    table[:, pl.ds(pl.multiple_of(core * half, half), half)] = mine[...]
    table[:, pl.ds(pl.multiple_of((1 - core) * half, half), half)] = other[...]
    for place, op in enumerate(operator_list(o0, a1, a2, a3, a4, b4, b3, b2, b1)):
        given = slotted[:, place].reshape(reps * SLOTS, width)
        moved[:, place] = dot(given, op()).astype(bf16).reshape(reps, SLOTS, width)
    sent = (s0, s1, s2, s3)
    handed = []
    for near, far in OFFSETS:
        offset = jnp.where(me < CORES, near, far)
        handed.append(2 * offset + jnp.where(offset == len(RING) // 2, 0, core))
    for b in range(reps):
        lying = rows[b]
        standing = lying.T.astype(jnp.int32)
        out_of = one_hot(lanes_of((edges, places * SLOTS)) == standing[:, 2:3])
        made = dot(out_of, moved[b].reshape(places * SLOTS, width))
        made_half = made.astype(bf16)
        scores = dot(made_half, table[...])
        aimed = lanes_of((edges, entities)) == standing[:, 1:2]
        positive = jnp.sum(jnp.where(aimed, scores, 0.0), axis=1, keepdims=True)
        positive_grad = -(0.5 * jnp.tanh(-0.5 * positive) + 0.5)
        share = (0.5 * jnp.tanh(0.5 * scores) + 0.5) * (1.0 / negative_count)
        weighted = (share.astype(bf16).astype(f32) * counts[b]).astype(bf16)
        target_rows = dot(one_hot(aimed), table[...], NT)
        asked = (positive_grad * target_rows + dot(weighted, table[...], NT)).astype(bf16)
        push = positive_grad * made
        push_half = push.astype(bf16)
        weights[b] = weighted
        sides[b, :edges] = made_half
        sides[b, edges : 2 * edges] = push_half
        sides[b, 2 * edges :] = (push - push_half.astype(f32)).astype(bf16)
        query[b] = asked
        slot = lying[2:3].astype(jnp.int32)
        into = jnp.concatenate(
            [one_hot(rows_of((SLOTS, edges)) + place * SLOTS == slot) for place in handed], axis=0
        )
        asking[b] = dot(into, asked).astype(bf16).reshape(len(sent), SLOTS, width)
    for k, place in enumerate(handed):
        given = slotted[:, pl.ds(place, 1)].reshape(reps * SLOTS, width)
        sent[k][...] = dot(given, asking[:, k].reshape(reps * SLOTS, width), TN).astype(bf16)


def operator_list(o0, a1, a2, a3, a4, b4, b3, b2, b1):
    listed = [(o0, 0), (o0, 1)]
    for ref in (a1, a2, a3):
        listed += [(ref, 0), (ref, 1)]
    listed += [(a4, 0), (b4, 0)]
    for ref in (b3, b2, b1):
        listed += [(ref, 0), (ref, 1)]
    return [lambda ref=ref, i=i: ref[i] for ref, i in listed]


def return_kernel(
    o0, a1, a2, a3, a4, b4, b3, b2, b1, rows, weights, sides, query, target_half, source_total, total, held
):
    core, *_ = position()
    reps, edges, entities = weights.shape
    places, width = held.shape[1], held.shape[3]
    half = target_half.shape[1]
    standing = [rows[b].T.astype(jnp.int32) for b in range(reps)]
    for b in range(reps):
        aimed = one_hot(lanes_of((edges, entities)) == standing[b][:, 1:2])
        grown = dot(sides[b], jnp.concatenate([weights[b], aimed, aimed], axis=0), TN)
        if b == 0:
            total[...] = grown
        else:
            total[...] += grown
    target_half[...] = total[:, pl.ds(pl.multiple_of(core * half, half), half)].astype(bf16)
    for b in range(reps):
        into = one_hot(rows_of((places * SLOTS, edges)) == rows[b][2:3].astype(jnp.int32))
        held[b] = dot(into, query[b]).astype(bf16).reshape(places, SLOTS, width)
    for place, op in enumerate(operator_list(o0, a1, a2, a3, a4, b4, b3, b2, b1)):
        given = held[:, place].reshape(-1, width)
        held[:, place] = dot(given, op(), NT).astype(bf16).reshape(-1, SLOTS, width)
    for b in range(reps):
        out_of = one_hot(lanes_of((edges, places * SLOTS)) == standing[b][:, 2:3])
        back = dot(out_of, held[b].reshape(places * SLOTS, width)).astype(bf16)
        spread = one_hot(lanes_of((edges, entities)) == standing[b][:, 0:1])
        grown = dot(back, spread, TN)
        if b == 0:
            source_total[...] = grown
        else:
            source_total[...] += grown


def entity_kernel(source_total, mine, other, table, state, new_table, new_state):
    core, *_ = position()
    half = mine.shape[1]
    width = table.shape[0]
    for part, side in ((mine, core), (other, 1 - core)):
        at = pl.ds(pl.multiple_of(side * half, half), half)
        g = source_total[:, at] + part[...].astype(f32)
        moments = state[:, at] + jnp.sum(g * g, axis=0, keepdims=True) * (1.0 / width)
        new_state[:, at] = moments
        new_table[:, at] = table[:, at] - g * (entity_rate / (jnp.sqrt(moments) + epsilon))


def operator_kernel(own, other, operators, state, new_operators, new_state):
    core, *_ = position()
    for i in range(operators.shape[0]):
        g = jnp.where(core == i, own[...], other[...])
        moments = state[i] + g * g
        new_state[i] = moments
        new_operators[i] = operators[i] - operator_rate * g / (jnp.sqrt(moments) + epsilon)


def rep_swapped(array, by):
    peers = lax.axis_size("rep")
    return lax.ppermute(array, "rep", [(i, i ^ by) for i in range(peers)])


def along_ring(array, offset_of):
    groups, reps = lax.axis_size("ent"), lax.axis_size("rep")
    pairs = []
    for e in range(groups):
        for r in range(reps):
            way = offset_of(r) if r % CORES == 1 else -offset_of(r)
            to = RING[(PLACE[e] + way) % groups]
            pairs.append((e * reps + r, to * reps + r))
    return lax.ppermute(array, ("ent", "rep"), pairs)


def ring_step(array):
    return along_ring(array, lambda r: -1)


def handed_on(array, k):
    return along_ring(array, lambda r: OFFSETS[k][0 if r < CORES else 1])


def gathered_shards(
    entity_table, entity_state, operators, operator_state, sources, destinations, relations, negatives
):
    groups, reps = lax.axis_size("ent"), lax.axis_size("rep")
    entities, width = entity_table.shape
    edges = sources.shape[0]
    relation_count = groups * operators.shape[0]
    half = entities // CORES
    core = lax.axis_index("rep") % CORES

    operators_half = operators.astype(bf16)
    table = entity_table.T
    ids = jnp.concatenate(
        [
            sources,
            destinations,
            relations[:, 0],
            negatives[0],
            jnp.full((5 * edges - negatives.shape[1],), -1, jnp.int32),
        ]
    ).reshape(8, edges)
    places = relation_count
    slot_out = [
        jax.ShapeDtypeStruct((reps, places, SLOTS, width), bf16),
        jax.ShapeDtypeStruct((reps, 8, edges), f32),
        jax.ShapeDtypeStruct((reps, 1, entities), f32),
    ]
    a1 = ring_step(operators_half)
    others = [rep_swapped(ids, by) for by in (1, 2, 3)]
    own_half = lax.dynamic_slice_in_dim(table, core * half, half, 1).astype(bf16)
    a1, own_half, *others = lax.optimization_barrier((a1, own_half, *others))
    a2 = ring_step(a1)
    b1 = rep_swapped(a1, 1)
    b1, own_half = lax.optimization_barrier((b1, own_half))
    mine = passed_along(own_half, "ent", -1)
    a2, b1, *others = lax.optimization_barrier((a2, b1, *others))
    a3 = ring_step(a2)
    b2 = rep_swapped(a2, 1)
    slots = call(
        slot_kernel, slot_out, "slots", 10**8, 10**6, (ids, *others, table),
        scratch=[VMEM((width, entities), f32), pltpu.SemaphoreType.DMA],
        far=(4,),
    )
    a3, b2, mine, *slots = lax.optimization_barrier((a3, b2, mine, *slots))
    slotted, rows, counts = slots
    a4 = ring_step(lax.dynamic_slice_in_dim(a3, core, 1, 0))
    b3 = rep_swapped(a3, 1)
    other = rep_swapped(mine, 1)
    a4, b3, other = lax.optimization_barrier((a4, b3, other))
    b4 = rep_swapped(a4, 1)
    gathered = (operators_half, a1, a2, a3, a4, b4, b3, b2, b1)

    score_out = [jax.ShapeDtypeStruct((width, width), bf16)] * len(OFFSETS) + [
        jax.ShapeDtypeStruct((reps, edges, entities), bf16),
        jax.ShapeDtypeStruct((reps, 3 * edges, width), bf16),
        jax.ShapeDtypeStruct((reps, edges, width), bf16),
    ]
    *handed, weights, sides, query = call(
        functools.partial(score_kernel, negatives.shape[1]), score_out, "scores", 10**9, 10**6,
        (*gathered, slotted, rows, counts, mine, other),
        scratch=[
            VMEM((width, entities), bf16),
            VMEM((reps, places, SLOTS, width), bf16),
            VMEM((reps, len(OFFSETS), SLOTS, width), bf16),
        ],
    )
    arrived = [handed_on(matrix, k) for k, matrix in enumerate(handed)]
    target_half, source_total = call(
        return_kernel,
        [jax.ShapeDtypeStruct((width, half), bf16), jax.ShapeDtypeStruct((width, entities), f32)],
        "returns", 10**8, 10**6, (*gathered, rows, weights, sides, query),
        scratch=[VMEM((width, entities), f32), VMEM((reps, places, SLOTS, width), bf16)],
    )
    home_mine = passed_along(target_half, "ent", 1)
    home_other = rep_swapped(home_mine, 1)
    source_total, *arrived = lax.optimization_barrier((source_total, *arrived))
    one_chip = sum(matrix.astype(f32) for matrix in arrived).astype(bf16)
    one_relation = one_chip.astype(f32) + rep_swapped(one_chip, CORES).astype(f32)
    other_relation = rep_swapped(one_relation, 1)
    new_table, new_state = call(
        entity_kernel,
        [
            jax.ShapeDtypeStruct((width, entities), f32),
            jax.ShapeDtypeStruct((1, entities), f32),
        ],
        "entity_update", 10**6, 10**6,
        (source_total, home_mine, home_other, table, entity_state.reshape(1, -1)),
    )
    new_operators, new_operator_state = call(
        operator_kernel,
        [jax.ShapeDtypeStruct(operators.shape, f32)] * 2,
        "operator_update", 10**6, 10**6,
        (one_relation, other_relation, operators, operator_state),
    )
    return (new_table.T, new_state.reshape(-1), new_operators, new_operator_state)


def solution(mesh):
    placed = (
        P("ent", None),
        P("ent"),
        P("ent", None, None),
        P("ent", None, None),
        P(("ent", "rep")),
        P(("ent", "rep")),
        P(("ent", "rep"), None),
        P(("ent", "rep"), None),
    )
    small = mesh.shape["ent"] == len(RING) and mesh.shape["rep"] == 2 * CORES
    return jax.shard_map(
        gathered_shards if small else exchanged_shards,
        mesh=mesh,
        in_specs=placed,
        out_specs=(P("ent", None), P("ent"), P("ent", None, None), P("ent", None, None)),
        check_vma=False,
    )
```

```python
import functools

import jax
import jax.numpy as jnp
from jax import lax
from jax.experimental import pallas as pl
from jax.experimental.pallas import tpu as pltpu
from jax.sharding import PartitionSpec as P

SPAN = 256
EDGE_DEV = 256
REL_DEV = 2


entity_rate = 0.1
operator_rate = 0.02
epsilon = 1e-06


def passed_along(array, axis, by):
    peers = lax.axis_size(axis)
    return lax.ppermute(array, axis, [(i, (i + by) % peers) for i in range(peers)])


def place_slots(relation_ids, capacity):
    count_edges = relation_ids.shape[0]
    ordering = jnp.argsort(relation_ids, stable=True)
    ranked = relation_ids[ordering]
    leading = jnp.searchsorted(ranked, ranked, side="left")
    within = jnp.arange(count_edges, dtype=jnp.int32) - leading
    position = jnp.zeros((count_edges,), jnp.int32).at[ordering].set(within)
    return relation_ids * capacity + position


def score_grads(transformed, target_ids, negative_ids, table_rows):
    target_rows = jnp.take(table_rows, target_ids, axis=0)
    positive = jnp.sum(transformed.astype(jnp.float32) * target_rows.astype(jnp.float32), axis=-1)
    positive_grad = -jax.nn.sigmoid(-positive)
    width = transformed.shape[1]
    blocks = transformed.reshape(-1, SPAN, width)
    negative_count = negative_ids.shape[1]

    def span_step(running, pieces):
        query_block, negative_block = pieces
        negative_rows = jnp.take(table_rows, negative_block, axis=0)
        scores = lax.dot_general(
            query_block, negative_rows, (((1,), (1,)), ((), ())), preferred_element_type=jnp.float32
        )
        negative_grad = (jax.nn.sigmoid(scores) / negative_count).astype(jnp.bfloat16)
        query_part = jnp.dot(negative_grad, negative_rows, preferred_element_type=jnp.float32)
        row_update = lax.dot_general(
            negative_grad, query_block, (((0,), (0,)), ((), ())), preferred_element_type=jnp.float32
        )
        return (running.at[negative_block].add(row_update), query_part)

    starting = jnp.zeros((table_rows.shape[0], width), jnp.float32)
    negative_total, query_parts = lax.scan(span_step, starting, (blocks, negative_ids))
    query_grad = (
        positive_grad[:, None] * target_rows.astype(jnp.float32) + query_parts.reshape(-1, width)
    ).astype(jnp.bfloat16)
    target_grad = negative_total.at[target_ids].add(
        positive_grad[:, None] * transformed.astype(jnp.float32)
    )
    return (query_grad, target_grad)


def row_adagrad(weights, moments, gradient):
    fresh_moments = moments + jnp.mean(gradient * gradient, axis=-1)
    updated = weights - entity_rate * gradient / (jnp.sqrt(fresh_moments)[:, None] + epsilon)
    return (updated, fresh_moments)


def dense_adagrad(weights, moments, gradient):
    fresh_moments = moments + gradient * gradient
    updated = weights - operator_rate * gradient / (jnp.sqrt(fresh_moments) + epsilon)
    return (updated, fresh_moments)


def exchanged_shards(
    entity_table,
    entity_state,
    operators,
    operator_state,
    sources,
    destinations,
    relations,
    negatives,
):
    groups = lax.axis_size("ent")
    relation_count = REL_DEV * groups
    capacity = max(2, (2 * EDGE_DEV + relation_count - 1) // relation_count)
    width = entity_table.shape[1]
    table_half = entity_table.astype(jnp.bfloat16)
    operators_half = operators.astype(jnp.bfloat16)
    slot_index = place_slots(relations[:, 0], capacity)
    source_rows = jnp.take(table_half, sources, axis=0)
    outgoing = (
        jnp.zeros((relation_count * capacity, width), jnp.bfloat16).at[slot_index].set(source_rows)
    )
    outgoing = outgoing.reshape(groups, REL_DEV, capacity, width)
    arrived = lax.all_to_all(outgoing, "ent", split_axis=0, concat_axis=0, tiled=True)
    result = jnp.einsum(
        "srmd,rdk->srmk", arrived, operators_half, preferred_element_type=jnp.float32
    ).astype(jnp.bfloat16)
    returned = lax.all_to_all(result, "ent", split_axis=0, concat_axis=0, tiled=True)
    transformed_slots = returned
    transformed = jnp.take(transformed_slots.reshape(-1, width), slot_index, axis=0)
    neighbour_table = passed_along(table_half, "ent", -1)
    query_grad, target_grad = score_grads(transformed, destinations, negatives, neighbour_table)
    home_grad = passed_along(target_grad, "ent", 1)
    grad_slots = (
        jnp.zeros((relation_count * capacity, width), jnp.bfloat16).at[slot_index].set(query_grad)
    )
    grad_slots = grad_slots.reshape(groups, REL_DEV, capacity, width)
    arrived_grads = lax.all_to_all(grad_slots, "ent", split_axis=0, concat_axis=0, tiled=True)
    source_grads = jnp.einsum(
        "srmk,rdk->srmd", arrived_grads, operators_half, preferred_element_type=jnp.float32
    ).astype(jnp.bfloat16)
    returned = lax.all_to_all(source_grads, "ent", split_axis=0, concat_axis=0, tiled=True)
    operator_grad = jnp.einsum(
        "srmd,srmk->rdk", arrived, arrived_grads, preferred_element_type=jnp.float32
    )
    source_grad = jnp.take(returned.reshape(-1, width), slot_index, axis=0)
    entity_grad = (
        jnp.zeros(entity_table.shape, jnp.float32).at[sources].add(source_grad.astype(jnp.float32))
        + home_grad
    )
    total_grad, total_operator = lax.psum((entity_grad, operator_grad), "rep")
    new_table, new_entity_state = row_adagrad(entity_table, entity_state, total_grad)
    new_operators, new_operator_state = dense_adagrad(operators, operator_state, total_operator)
    return (new_table, new_entity_state, new_operators, new_operator_state)


bf16 = jnp.bfloat16
f32 = jnp.float32
CORES = 2
LANES = 128
RING = (0, 2, 4, 6, 7, 5, 3, 1)
PLACE = tuple(RING.index(e) for e in range(8))
SLOTS = 32
SIDE = 104
OFFSETS = ((0, 4), (3, 1), (5, 7), (2, 6))
VMEM = pltpu.VMEM
NT = (((1,), (1,)), ((), ()))
TN = (((0,), (0,)), ((), ()))


def dot(a, b, dims=(((1,), (0,)), ((), ()))):
    return lax.dot_general(a, b, dims, preferred_element_type=f32)


def lanes_of(shape):
    return lax.broadcasted_iota(jnp.int32, shape, 1)


def rows_of(shape):
    return lax.broadcasted_iota(jnp.int32, shape, 0)


def one_hot(mask):
    return jnp.where(mask, 1.0, 0.0).astype(bf16)


def call(body, outs, name, flops, size, operands, limit=16, scratch=()):
    whole = pl.BlockSpec(memory_space=VMEM)
    return pl.pallas_call(
        body,
        out_shape=outs,
        in_specs=[whole] * len(operands),
        out_specs=[whole] * len(outs),
        scratch_shapes=list(scratch),
        name=name,
        cost_estimate=pl.CostEstimate(flops=flops, bytes_accessed=size, transcendentals=0),
        compiler_params=pltpu.CompilerParams(vmem_limit_bytes=limit * 2**20),
    )(*operands)


def chosen_from(listed, at):
    found = jnp.zeros_like(at)
    for i, value in enumerate(listed):
        found = jnp.where(at == i, value, found)
    return found


def position():
    rep = lax.axis_index("rep")
    core = lax.rem(rep, CORES)
    return core, rep, chosen_from(PLACE, lax.axis_index("ent")), 2 * core - 1


def slot_kernel(own, near, far, across, table, slotted, rows, counts):
    core, me, here, sign = position()
    ring = len(RING)
    reps, _, edges = rows.shape
    places = slotted.shape[1]
    ids = [ref[...] for ref in (own, near, far, across)]
    before = one_hot(rows_of((edges, edges)) > lanes_of((edges, edges)))
    relation = jnp.concatenate([block[2:3] for block in ids], axis=0)
    offset = lax.bitwise_and(
        sign * (chosen_from(PLACE, lax.shift_right_logical(relation, 1)) - here), ring - 1
    )
    parity = lax.bitwise_and(relation, 1)
    local = 2 * offset + jnp.where(offset == ring // 2, lax.bitwise_xor(parity, core), parity)
    ends = [block[i : i + 1] for i in (0, 1) for block in ids]
    standing = jnp.concatenate([local, *ends], axis=0).astype(f32).T
    column = lambda i: standing[:, i : i + 1].astype(jnp.int32)
    named = [lanes_of((edges, LANES)) == column(m) for m in range(reps)]
    ahead = dot(before, one_hot(jnp.concatenate(named, axis=1)))
    slots = jnp.concatenate(
        [
            standing[:, m : m + 1] * SLOTS
            + jnp.sum(
                jnp.where(named[m], ahead[:, m * LANES : (m + 1) * LANES], 0.0), axis=1, keepdims=True
            )
            for m in range(reps)
        ],
        axis=1,
    ).T
    for m in range(reps):
        block = lax.bitwise_xor(me, m)
        lying = jnp.concatenate(
            [ids[m][0:2].astype(f32), slots[m : m + 1], ids[m][3:8].astype(f32)], axis=0
        )
        rows[block] = lying
        tally = jnp.zeros((8, LANES), f32)
        for k in range(3, 7):
            drawn = ids[m][k : k + 1]
            high = one_hot(rows_of((8, edges)) == lax.shift_right_arithmetic(drawn, 7))
            low = one_hot(rows_of((LANES, edges)) == lax.bitwise_and(drawn, LANES - 1))
            tally = tally + dot(high, low, NT)
        counts[block] = jnp.concatenate([tally[k : k + 1] for k in range(8)], axis=1)
    picked = [
        one_hot(lanes_of((edges, table.shape[1])) == column(reps + m)) for m in range(reps)
    ]
    source_rows = dot(jnp.concatenate(picked, axis=0), table[...], NT).astype(bf16)
    for m in range(reps):
        into = one_hot(rows_of((places * SLOTS, edges)) == slots[m : m + 1].astype(jnp.int32))
        given = dot(into, source_rows[m * edges : (m + 1) * edges]).astype(bf16)
        slotted[lax.bitwise_xor(me, m)] = given.reshape(places, SLOTS, -1)


def score_kernel(
    negative_count, o0, a1, a2, a3, a4, b4, b3, b2, b1, slotted, rows, counts, mine, other,
    s0, s1, s2, s3, weights, sides, query, table, moved, asking,
):
    core, me, *_ = position()
    reps, places = slotted.shape[:2]
    width, entities = table.shape
    half = mine.shape[1]
    edges = rows.shape[2]
    table[:, pl.ds(pl.multiple_of(core * half, half), half)] = mine[...]
    table[:, pl.ds(pl.multiple_of((1 - core) * half, half), half)] = other[...]
    for place, op in enumerate(operator_list(o0, a1, a2, a3, a4, b4, b3, b2, b1)):
        given = slotted[:, place].reshape(reps * SLOTS, width)
        moved[:, place] = dot(given, op()).astype(bf16).reshape(reps, SLOTS, width)
    sent = (s0, s1, s2, s3)
    handed = []
    for near, far in OFFSETS:
        offset = jnp.where(me < CORES, near, far)
        handed.append(2 * offset + jnp.where(offset == len(RING) // 2, 0, core))
    lying = [rows[b] for b in range(reps)]
    standing = [block.T.astype(jnp.int32) for block in lying]
    made = []
    for b in range(reps):
        out_of = one_hot(lanes_of((edges, places * SLOTS)) == standing[b][:, 2:3])
        made.append(dot(out_of, moved[b].reshape(places * SLOTS, width)))
    made = jnp.concatenate(made, axis=0)
    made_half = made.astype(bf16)
    scores = dot(made_half, table[...])
    aimed = lanes_of((reps * edges, entities)) == jnp.concatenate(
        [block[:, 1:2] for block in standing], axis=0
    )
    positive = jnp.sum(jnp.where(aimed, scores, 0.0), axis=1, keepdims=True)
    positive_grad = -(0.5 * jnp.tanh(-0.5 * positive) + 0.5)
    share = (0.5 * jnp.tanh(0.5 * scores) + 0.5) * (1.0 / negative_count)
    share = share.astype(bf16).astype(f32)
    weighted = jnp.concatenate(
        [share[b * edges : (b + 1) * edges] * counts[b] for b in range(reps)], axis=0
    ).astype(bf16)
    target_rows = dot(one_hot(aimed), table[...], NT)
    asked = (positive_grad * target_rows + dot(weighted, table[...], NT)).astype(bf16)
    push = positive_grad * made
    push_half = push.astype(bf16)
    push_rest = (push - push_half.astype(f32)).astype(bf16)
    for b in range(reps):
        at = slice(b * edges, (b + 1) * edges)
        weights[b] = weighted[at]
        sides[b, :edges] = made_half[at]
        sides[b, edges : 2 * edges] = push_half[at]
        sides[b, 2 * edges :] = push_rest[at]
        query[b] = asked[at]
        slot = lying[b][2:3].astype(jnp.int32)
        into = jnp.concatenate(
            [one_hot(rows_of((SLOTS, edges)) + place * SLOTS == slot) for place in handed], axis=0
        )
        asking[b] = dot(into, asked[at]).astype(bf16).reshape(len(sent), SLOTS, width)
    for k, place in enumerate(handed):
        given = slotted[:, pl.ds(place, 1)].reshape(reps * SLOTS, width)
        sent[k][...] = packed(dot(given, asking[:, k].reshape(reps * SLOTS, width), TN)).astype(bf16)


def packed(matrix):
    low, side, spare = matrix[:, :LANES], matrix[:, LANES : LANES + 64], matrix[:, LANES + 64 :]
    side = jnp.concatenate([side[:SIDE], side[side.shape[0] - SIDE :]], axis=1)
    spare = spare.T
    rest = jnp.zeros((spare.shape[0], 2 * LANES - spare.shape[1]), spare.dtype)
    return jnp.concatenate(
        [low, side, spare[:, :LANES], jnp.concatenate([spare[:, LANES:], rest], axis=1)], axis=0
    )


def unpacked(rows, size):
    low, side, spare = rows[:size], rows[size : size + SIDE], rows[size + SIDE :]
    side = jnp.concatenate([side[:, :64], side[2 * SIDE - size :, 64:]], axis=0)
    count = size - LANES - 64
    spare = jnp.concatenate([spare[:count], spare[count:, : size - LANES]], axis=1)
    return jnp.concatenate([low, side, spare.T], axis=1)


def operator_list(o0, a1, a2, a3, a4, b4, b3, b2, b1):
    listed = [(o0, 0), (o0, 1)]
    for ref in (a1, a2, a3):
        listed += [(ref, 0), (ref, 1)]
    listed += [(a4, 0), (b4, 0)]
    for ref in (b3, b2, b1):
        listed += [(ref, 0), (ref, 1)]
    return [lambda ref=ref, i=i: ref[i] for ref, i in listed]


def target_kernel(rows, weights, sides, target_half, total):
    core, *_ = position()
    reps, edges, entities = weights.shape
    half = target_half.shape[1]
    for b in range(reps):
        aimed = one_hot(lanes_of((edges, entities)) == rows[b].T[:, 1:2].astype(jnp.int32))
        grown = dot(sides[b], jnp.concatenate([weights[b], aimed, aimed], axis=0), TN)
        if b == 0:
            total[...] = grown
        else:
            total[...] += grown
    target_half[...] = total[:, pl.ds(pl.multiple_of(core * half, half), half)].astype(bf16)


def source_kernel(o0, a1, a2, a3, a4, b4, b3, b2, b1, rows, query, source_total, held):
    reps, places, _, width = held.shape
    edges, entities = rows.shape[2], source_total.shape[1]
    for b in range(reps):
        into = one_hot(rows_of((places * SLOTS, edges)) == rows[b][2:3].astype(jnp.int32))
        held[b] = dot(into, query[b]).astype(bf16).reshape(places, SLOTS, width)
    for place, op in enumerate(operator_list(o0, a1, a2, a3, a4, b4, b3, b2, b1)):
        given = held[:, place].reshape(-1, width)
        held[:, place] = dot(given, op(), NT).astype(bf16).reshape(-1, SLOTS, width)
    for b in range(reps):
        standing = rows[b].T.astype(jnp.int32)
        out_of = one_hot(lanes_of((edges, places * SLOTS)) == standing[:, 2:3])
        back = dot(out_of, held[b].reshape(places * SLOTS, width)).astype(bf16)
        spread = one_hot(lanes_of((edges, entities)) == standing[:, 0:1])
        grown = dot(back, spread, TN)
        if b == 0:
            source_total[...] = grown
        else:
            source_total[...] += grown


def entity_kernel(source_total, mine, other, table, state, new_table, new_state):
    core, *_ = position()
    half = mine.shape[1]
    width = table.shape[0]
    for part, side in ((mine, core), (other, 1 - core)):
        at = pl.ds(pl.multiple_of(side * half, half), half)
        g = source_total[:, at] + part[...].astype(f32)
        moments = state[:, at] + jnp.sum(g * g, axis=0, keepdims=True) * (1.0 / width)
        new_state[:, at] = moments
        new_table[:, at] = table[:, at] - g * (entity_rate / (jnp.sqrt(moments) + epsilon))


def operator_kernel(own, other, operators, state, new_operators, new_state):
    core, *_ = position()
    for i in range(operators.shape[0]):
        g = unpacked(jnp.where(core == i, own[...], other[...]), operators.shape[1])
        moments = state[i] + g * g
        new_state[i] = moments
        new_operators[i] = operators[i] - operator_rate * g / (jnp.sqrt(moments) + epsilon)


def rep_swapped(array, by):
    peers = lax.axis_size("rep")
    return lax.ppermute(array, "rep", [(i, i ^ by) for i in range(peers)])


def along_ring(array, offset_of):
    groups, reps = lax.axis_size("ent"), lax.axis_size("rep")
    pairs = []
    for e in range(groups):
        for r in range(reps):
            way = offset_of(r) if r % CORES == 1 else -offset_of(r)
            to = RING[(PLACE[e] + way) % groups]
            pairs.append((e * reps + r, to * reps + r))
    return lax.ppermute(array, ("ent", "rep"), pairs)


def ring_step(array):
    return along_ring(array, lambda r: -1)


def handed_on(array, k):
    return along_ring(array, lambda r: OFFSETS[k][0 if r < CORES else 1])


def gathered_shards(
    entity_table, entity_state, operators, operator_state, sources, destinations, relations, negatives
):
    groups, reps = lax.axis_size("ent"), lax.axis_size("rep")
    entities, width = entity_table.shape
    edges = sources.shape[0]
    relation_count = groups * operators.shape[0]
    half = entities // CORES
    core = lax.axis_index("rep") % CORES

    operators_half = operators.astype(bf16)
    table = entity_table.T
    ids = jnp.concatenate(
        [
            sources,
            destinations,
            relations[:, 0],
            negatives[0],
            jnp.full((5 * edges - negatives.shape[1],), -1, jnp.int32),
        ]
    ).reshape(8, edges)
    places = relation_count
    slot_out = [
        jax.ShapeDtypeStruct((reps, places, SLOTS, width), bf16),
        jax.ShapeDtypeStruct((reps, 8, edges), f32),
        jax.ShapeDtypeStruct((reps, 1, entities), f32),
    ]
    a1 = ring_step(operators_half)
    others = [rep_swapped(ids, by) for by in (1, 2, 3)]
    own_half = lax.dynamic_slice_in_dim(table, core * half, half, 1).astype(bf16)
    a1, own_half, *others = lax.optimization_barrier((a1, own_half, *others))
    a2 = ring_step(a1)
    b1 = rep_swapped(a1, 1)
    b1, own_half = lax.optimization_barrier((b1, own_half))
    mine = passed_along(own_half, "ent", -1)
    a2, b1, late_table = lax.optimization_barrier((a2, b1, table))
    a3 = ring_step(a2)
    b2 = rep_swapped(a2, 1)
    table_half = late_table.astype(bf16)
    slots = call(slot_kernel, slot_out, "slots", 10**8, 10**6, (ids, *others, table_half))
    a3, b2, mine, *slots = lax.optimization_barrier((a3, b2, mine, *slots))
    slotted, rows, counts = slots
    a4 = ring_step(lax.dynamic_slice_in_dim(a3, core, 1, 0))
    other = rep_swapped(mine, 1)
    a4, a3 = lax.optimization_barrier((a4, a3))
    b3 = rep_swapped(a3, 1)
    b4 = rep_swapped(a4, 1)
    gathered = (operators_half, a1, a2, a3, a4, b4, b3, b2, b1)

    score_out = [jax.ShapeDtypeStruct((width + SIDE + 16, LANES), bf16)] * len(OFFSETS) + [
        jax.ShapeDtypeStruct((reps, edges, entities), bf16),
        jax.ShapeDtypeStruct((reps, 3 * edges, width), bf16),
        jax.ShapeDtypeStruct((reps, edges, width), bf16),
    ]
    *handed, weights, sides, query = call(
        functools.partial(score_kernel, negatives.shape[1]), score_out, "scores", 10**9, 10**6,
        (*gathered, slotted, rows, counts, mine, other),
        scratch=[
            VMEM((width, entities), bf16),
            VMEM((reps, places, SLOTS, width), bf16),
            VMEM((reps, len(OFFSETS), SLOTS, width), bf16),
        ],
    )
    arrived = [handed_on(matrix, k) for k, matrix in enumerate(handed)]
    (target_half,) = call(
        target_kernel,
        [jax.ShapeDtypeStruct((width, half), bf16)],
        "targets", 10**8, 10**6, (rows, weights, sides),
        scratch=[VMEM((width, entities), f32)],
    )
    query, target_half = lax.optimization_barrier((query, target_half))
    (source_total,) = call(
        source_kernel,
        [jax.ShapeDtypeStruct((width, entities), f32)],
        "sources", 10**8, 10**6, (*gathered, rows, query),
        scratch=[VMEM((reps, places, SLOTS, width), bf16)],
    )
    home_mine = passed_along(target_half, "ent", 1)
    home_other = rep_swapped(home_mine, 1)
    source_total, *arrived = lax.optimization_barrier((source_total, *arrived))
    one_chip = sum(matrix.astype(f32) for matrix in arrived).astype(bf16)
    one_relation = one_chip.astype(f32) + rep_swapped(one_chip, CORES).astype(f32)
    other_relation = rep_swapped(one_relation, 1)
    new_table, new_state = call(
        entity_kernel,
        [
            jax.ShapeDtypeStruct((width, entities), f32),
            jax.ShapeDtypeStruct((1, entities), f32),
        ],
        "entity_update", 10**6, 10**6,
        (source_total, home_mine, home_other, table, entity_state.reshape(1, -1)),
    )
    new_operators, new_operator_state = call(
        operator_kernel,
        [jax.ShapeDtypeStruct(operators.shape, f32)] * 2,
        "operator_update", 10**6, 10**6,
        (one_relation, other_relation, operators, operator_state),
    )
    return (new_table.T, new_state.reshape(-1), new_operators, new_operator_state)


def solution(mesh):
    placed = (
        P("ent", None),
        P("ent"),
        P("ent", None, None),
        P("ent", None, None),
        P(("ent", "rep")),
        P(("ent", "rep")),
        P(("ent", "rep"), None),
        P(("ent", "rep"), None),
    )
    small = mesh.shape["ent"] == len(RING) and mesh.shape["rep"] == 2 * CORES
    return jax.shard_map(
        gathered_shards if small else exchanged_shards,
        mesh=mesh,
        in_specs=placed,
        out_specs=(P("ent", None), P("ent"), P("ent", None, None), P("ent", None, None)),
        check_vma=False,
    )
```

```python
import functools

import jax
import jax.numpy as jnp
from jax import lax
from jax.experimental import pallas as pl
from jax.experimental.pallas import tpu as pltpu
from jax.sharding import PartitionSpec as P

SPAN = 256
EDGE_DEV = 256
REL_DEV = 2


entity_rate = 0.1
operator_rate = 0.02
epsilon = 1e-06


def passed_along(array, axis, by):
    peers = lax.axis_size(axis)
    return lax.ppermute(array, axis, [(i, (i + by) % peers) for i in range(peers)])


def place_slots(relation_ids, capacity):
    count_edges = relation_ids.shape[0]
    ordering = jnp.argsort(relation_ids, stable=True)
    ranked = relation_ids[ordering]
    leading = jnp.searchsorted(ranked, ranked, side="left")
    within = jnp.arange(count_edges, dtype=jnp.int32) - leading
    position = jnp.zeros((count_edges,), jnp.int32).at[ordering].set(within)
    return relation_ids * capacity + position


def score_grads(transformed, target_ids, negative_ids, table_rows):
    target_rows = jnp.take(table_rows, target_ids, axis=0)
    positive = jnp.sum(transformed.astype(jnp.float32) * target_rows.astype(jnp.float32), axis=-1)
    positive_grad = -jax.nn.sigmoid(-positive)
    width = transformed.shape[1]
    blocks = transformed.reshape(-1, SPAN, width)
    negative_count = negative_ids.shape[1]

    def span_step(running, pieces):
        query_block, negative_block = pieces
        negative_rows = jnp.take(table_rows, negative_block, axis=0)
        scores = lax.dot_general(
            query_block, negative_rows, (((1,), (1,)), ((), ())), preferred_element_type=jnp.float32
        )
        negative_grad = (jax.nn.sigmoid(scores) / negative_count).astype(jnp.bfloat16)
        query_part = jnp.dot(negative_grad, negative_rows, preferred_element_type=jnp.float32)
        row_update = lax.dot_general(
            negative_grad, query_block, (((0,), (0,)), ((), ())), preferred_element_type=jnp.float32
        )
        return (running.at[negative_block].add(row_update), query_part)

    starting = jnp.zeros((table_rows.shape[0], width), jnp.float32)
    negative_total, query_parts = lax.scan(span_step, starting, (blocks, negative_ids))
    query_grad = (
        positive_grad[:, None] * target_rows.astype(jnp.float32) + query_parts.reshape(-1, width)
    ).astype(jnp.bfloat16)
    target_grad = negative_total.at[target_ids].add(
        positive_grad[:, None] * transformed.astype(jnp.float32)
    )
    return (query_grad, target_grad)


def row_adagrad(weights, moments, gradient):
    fresh_moments = moments + jnp.mean(gradient * gradient, axis=-1)
    updated = weights - entity_rate * gradient / (jnp.sqrt(fresh_moments)[:, None] + epsilon)
    return (updated, fresh_moments)


def dense_adagrad(weights, moments, gradient):
    fresh_moments = moments + gradient * gradient
    updated = weights - operator_rate * gradient / (jnp.sqrt(fresh_moments) + epsilon)
    return (updated, fresh_moments)


def exchanged_shards(
    entity_table,
    entity_state,
    operators,
    operator_state,
    sources,
    destinations,
    relations,
    negatives,
):
    groups = lax.axis_size("ent")
    relation_count = REL_DEV * groups
    capacity = max(2, (2 * EDGE_DEV + relation_count - 1) // relation_count)
    width = entity_table.shape[1]
    table_half = entity_table.astype(jnp.bfloat16)
    operators_half = operators.astype(jnp.bfloat16)
    slot_index = place_slots(relations[:, 0], capacity)
    source_rows = jnp.take(table_half, sources, axis=0)
    outgoing = (
        jnp.zeros((relation_count * capacity, width), jnp.bfloat16).at[slot_index].set(source_rows)
    )
    outgoing = outgoing.reshape(groups, REL_DEV, capacity, width)
    arrived = lax.all_to_all(outgoing, "ent", split_axis=0, concat_axis=0, tiled=True)
    result = jnp.einsum(
        "srmd,rdk->srmk", arrived, operators_half, preferred_element_type=jnp.float32
    ).astype(jnp.bfloat16)
    returned = lax.all_to_all(result, "ent", split_axis=0, concat_axis=0, tiled=True)
    transformed_slots = returned
    transformed = jnp.take(transformed_slots.reshape(-1, width), slot_index, axis=0)
    neighbour_table = passed_along(table_half, "ent", -1)
    query_grad, target_grad = score_grads(transformed, destinations, negatives, neighbour_table)
    home_grad = passed_along(target_grad, "ent", 1)
    grad_slots = (
        jnp.zeros((relation_count * capacity, width), jnp.bfloat16).at[slot_index].set(query_grad)
    )
    grad_slots = grad_slots.reshape(groups, REL_DEV, capacity, width)
    arrived_grads = lax.all_to_all(grad_slots, "ent", split_axis=0, concat_axis=0, tiled=True)
    source_grads = jnp.einsum(
        "srmk,rdk->srmd", arrived_grads, operators_half, preferred_element_type=jnp.float32
    ).astype(jnp.bfloat16)
    returned = lax.all_to_all(source_grads, "ent", split_axis=0, concat_axis=0, tiled=True)
    operator_grad = jnp.einsum(
        "srmd,srmk->rdk", arrived, arrived_grads, preferred_element_type=jnp.float32
    )
    source_grad = jnp.take(returned.reshape(-1, width), slot_index, axis=0)
    entity_grad = (
        jnp.zeros(entity_table.shape, jnp.float32).at[sources].add(source_grad.astype(jnp.float32))
        + home_grad
    )
    total_grad, total_operator = lax.psum((entity_grad, operator_grad), "rep")
    new_table, new_entity_state = row_adagrad(entity_table, entity_state, total_grad)
    new_operators, new_operator_state = dense_adagrad(operators, operator_state, total_operator)
    return (new_table, new_entity_state, new_operators, new_operator_state)


bf16 = jnp.bfloat16
f32 = jnp.float32
CORES = 2
LANES = 128
RING = (0, 2, 4, 6, 7, 5, 3, 1)
PLACE = tuple(RING.index(e) for e in range(8))
SLOTS = 32
SIDE = 104
OFFSETS = ((0, 4), (3, 1), (5, 7), (2, 6))
VMEM = pltpu.VMEM
NT = (((1,), (1,)), ((), ()))
TN = (((0,), (0,)), ((), ()))


def dot(a, b, dims=(((1,), (0,)), ((), ()))):
    return lax.dot_general(a, b, dims, preferred_element_type=f32)


def lanes_of(shape):
    return lax.broadcasted_iota(jnp.int32, shape, 1)


def rows_of(shape):
    return lax.broadcasted_iota(jnp.int32, shape, 0)


def one_hot(mask):
    return jnp.where(mask, 1.0, 0.0).astype(bf16)


def call(body, outs, name, flops, size, operands, limit=16, scratch=()):
    whole = pl.BlockSpec(memory_space=VMEM)
    return pl.pallas_call(
        body,
        out_shape=outs,
        in_specs=[whole] * len(operands),
        out_specs=[whole] * len(outs),
        scratch_shapes=list(scratch),
        name=name,
        cost_estimate=pl.CostEstimate(flops=flops, bytes_accessed=size, transcendentals=0),
        compiler_params=pltpu.CompilerParams(vmem_limit_bytes=limit * 2**20),
    )(*operands)


def chosen_from(listed, at):
    found = jnp.zeros_like(at)
    for i, value in enumerate(listed):
        found = jnp.where(at == i, value, found)
    return found


def position():
    rep = lax.axis_index("rep")
    core = lax.rem(rep, CORES)
    return core, rep, chosen_from(PLACE, lax.axis_index("ent")), 2 * core - 1


def slot_kernel(own, near, far, across, table, slotted, rows, counts):
    core, me, here, sign = position()
    ring = len(RING)
    reps, _, edges = rows.shape
    places = slotted.shape[1]
    ids = [ref[...] for ref in (own, near, far, across)]
    before = one_hot(rows_of((edges, edges)) > lanes_of((edges, edges)))
    relation = jnp.concatenate([block[2:3] for block in ids], axis=0)
    offset = lax.bitwise_and(
        sign * (chosen_from(PLACE, lax.shift_right_logical(relation, 1)) - here), ring - 1
    )
    parity = lax.bitwise_and(relation, 1)
    local = 2 * offset + jnp.where(offset == ring // 2, lax.bitwise_xor(parity, core), parity)
    ends = [block[i : i + 1] for i in (0, 1) for block in ids]
    standing = jnp.concatenate([local, *ends], axis=0).astype(f32).T
    column = lambda i: standing[:, i : i + 1].astype(jnp.int32)
    named = [lanes_of((edges, LANES)) == column(m) for m in range(reps)]
    ahead = dot(before, one_hot(jnp.concatenate(named, axis=1)))
    slots = jnp.concatenate(
        [
            standing[:, m : m + 1] * SLOTS
            + jnp.sum(
                jnp.where(named[m], ahead[:, m * LANES : (m + 1) * LANES], 0.0), axis=1, keepdims=True
            )
            for m in range(reps)
        ],
        axis=1,
    ).T
    for m in range(reps):
        block = lax.bitwise_xor(me, m)
        lying = jnp.concatenate(
            [ids[m][0:2].astype(f32), slots[m : m + 1], ids[m][3:8].astype(f32)], axis=0
        )
        rows[block] = lying
        tally = jnp.zeros((8, LANES), f32)
        for k in range(3, 7):
            drawn = ids[m][k : k + 1]
            high = one_hot(rows_of((8, edges)) == lax.shift_right_arithmetic(drawn, 7))
            low = one_hot(rows_of((LANES, edges)) == lax.bitwise_and(drawn, LANES - 1))
            tally = tally + dot(high, low, NT)
        counts[block] = jnp.concatenate([tally[k : k + 1] for k in range(8)], axis=1)
    picked = [
        one_hot(lanes_of((edges, table.shape[1])) == column(reps + m)) for m in range(reps)
    ]
    source_rows = dot(jnp.concatenate(picked, axis=0), table[...], NT).astype(bf16)
    for m in range(reps):
        into = one_hot(rows_of((places * SLOTS, edges)) == slots[m : m + 1].astype(jnp.int32))
        given = dot(into, source_rows[m * edges : (m + 1) * edges]).astype(bf16)
        slotted[lax.bitwise_xor(me, m)] = given.reshape(places, SLOTS, -1)


def score_kernel(
    negative_count, o0, a1, a2, a3, a4, b4, b3, b2, b1, slotted, rows, counts, mine, other,
    s0, s1, s2, s3, weights, sides, query, table, moved, asking,
):
    core, me, *_ = position()
    reps, places = slotted.shape[:2]
    width, entities = table.shape
    half = mine.shape[1]
    edges = rows.shape[2]
    table[:, pl.ds(pl.multiple_of(core * half, half), half)] = mine[...]
    table[:, pl.ds(pl.multiple_of((1 - core) * half, half), half)] = other[...]
    for place, op in enumerate(operator_list(o0, a1, a2, a3, a4, b4, b3, b2, b1)):
        given = slotted[:, place].reshape(reps * SLOTS, width)
        moved[:, place] = dot(given, op()).astype(bf16).reshape(reps, SLOTS, width)
    sent = (s0, s1, s2, s3)
    handed = []
    for near, far in OFFSETS:
        offset = jnp.where(me < CORES, near, far)
        handed.append(2 * offset + jnp.where(offset == len(RING) // 2, 0, core))
    lying = [rows[b] for b in range(reps)]
    standing = [block.T.astype(jnp.int32) for block in lying]
    made = []
    for b in range(reps):
        out_of = one_hot(lanes_of((edges, places * SLOTS)) == standing[b][:, 2:3])
        made.append(dot(out_of, moved[b].reshape(places * SLOTS, width)))
    made = jnp.concatenate(made, axis=0)
    made_half = made.astype(bf16)
    scores = dot(made_half, table[...])
    aimed = lanes_of((reps * edges, entities)) == jnp.concatenate(
        [block[:, 1:2] for block in standing], axis=0
    )
    positive = jnp.sum(jnp.where(aimed, scores, 0.0), axis=1, keepdims=True)
    positive_grad = -(0.5 * jnp.tanh(-0.5 * positive) + 0.5)
    share = (0.5 * jnp.tanh(0.5 * scores) + 0.5) * (1.0 / negative_count)
    share = share.astype(bf16).astype(f32)
    weighted = jnp.concatenate(
        [share[b * edges : (b + 1) * edges] * counts[b] for b in range(reps)], axis=0
    ).astype(bf16)
    target_rows = dot(one_hot(aimed), table[...], NT)
    asked = (positive_grad * target_rows + dot(weighted, table[...], NT)).astype(bf16)
    push = positive_grad * made
    push_half = push.astype(bf16)
    push_rest = (push - push_half.astype(f32)).astype(bf16)
    for b in range(reps):
        at = slice(b * edges, (b + 1) * edges)
        weights[b] = weighted[at]
        sides[b, :edges] = made_half[at]
        sides[b, edges : 2 * edges] = push_half[at]
        sides[b, 2 * edges :] = push_rest[at]
        query[b] = asked[at]
        slot = lying[b][2:3].astype(jnp.int32)
        into = jnp.concatenate(
            [one_hot(rows_of((SLOTS, edges)) + place * SLOTS == slot) for place in handed], axis=0
        )
        asking[b] = dot(into, asked[at]).astype(bf16).reshape(len(sent), SLOTS, width)
    for k, place in enumerate(handed):
        given = slotted[:, pl.ds(place, 1)].reshape(reps * SLOTS, width)
        sent[k][...] = packed(dot(given, asking[:, k].reshape(reps * SLOTS, width), TN)).astype(bf16)


def packed(matrix):
    low, side, spare = matrix[:, :LANES], matrix[:, LANES : LANES + 64], matrix[:, LANES + 64 :]
    side = jnp.concatenate([side[:SIDE], side[side.shape[0] - SIDE :]], axis=1)
    spare = spare.T
    rest = jnp.zeros((spare.shape[0], 2 * LANES - spare.shape[1]), spare.dtype)
    return jnp.concatenate(
        [low, side, spare[:, :LANES], jnp.concatenate([spare[:, LANES:], rest], axis=1)], axis=0
    )


def unpacked(rows, size):
    low, side, spare = rows[:size], rows[size : size + SIDE], rows[size + SIDE :]
    side = jnp.concatenate([side[:, :64], side[2 * SIDE - size :, 64:]], axis=0)
    count = size - LANES - 64
    spare = jnp.concatenate([spare[:count], spare[count:, : size - LANES]], axis=1)
    return jnp.concatenate([low, side, spare.T], axis=1)


def operator_list(o0, a1, a2, a3, a4, b4, b3, b2, b1):
    listed = [(o0, 0), (o0, 1)]
    for ref in (a1, a2, a3):
        listed += [(ref, 0), (ref, 1)]
    listed += [(a4, 0), (b4, 0)]
    for ref in (b3, b2, b1):
        listed += [(ref, 0), (ref, 1)]
    return [lambda ref=ref, i=i: ref[i] for ref, i in listed]


def target_kernel(rows, weights, sides, target_half, total):
    core, *_ = position()
    reps, edges, entities = weights.shape
    half = target_half.shape[1]
    for b in range(reps):
        aimed = one_hot(lanes_of((edges, entities)) == rows[b].T[:, 1:2].astype(jnp.int32))
        grown = dot(sides[b], jnp.concatenate([weights[b], aimed, aimed], axis=0), TN)
        if b == 0:
            total[...] = grown
        else:
            total[...] += grown
    target_half[...] = total[:, pl.ds(pl.multiple_of(core * half, half), half)].astype(bf16)


def source_kernel(o0, a1, a2, a3, a4, b4, b3, b2, b1, rows, query, source_total, held):
    reps, places, _, width = held.shape
    edges, entities = rows.shape[2], source_total.shape[1]
    for b in range(reps):
        into = one_hot(rows_of((places * SLOTS, edges)) == rows[b][2:3].astype(jnp.int32))
        held[b] = dot(into, query[b]).astype(bf16).reshape(places, SLOTS, width)
    for place, op in enumerate(operator_list(o0, a1, a2, a3, a4, b4, b3, b2, b1)):
        given = held[:, place].reshape(-1, width)
        held[:, place] = dot(given, op(), NT).astype(bf16).reshape(-1, SLOTS, width)
    for b in range(reps):
        standing = rows[b].T.astype(jnp.int32)
        out_of = one_hot(lanes_of((edges, places * SLOTS)) == standing[:, 2:3])
        back = dot(out_of, held[b].reshape(places * SLOTS, width)).astype(bf16)
        spread = one_hot(lanes_of((edges, entities)) == standing[:, 0:1])
        grown = dot(back, spread, TN)
        if b == 0:
            source_total[...] = grown
        else:
            source_total[...] += grown


def entity_kernel(source_total, mine, other, table, state, new_table, new_state):
    core, *_ = position()
    half = mine.shape[1]
    width = table.shape[0]
    for part, side in ((mine, core), (other, 1 - core)):
        at = pl.ds(pl.multiple_of(side * half, half), half)
        g = source_total[:, at] + part[...].astype(f32)
        moments = state[:, at] + jnp.sum(g * g, axis=0, keepdims=True) * (1.0 / width)
        new_state[:, at] = moments
        new_table[:, at] = table[:, at] - g * (entity_rate / (jnp.sqrt(moments) + epsilon))


def operator_kernel(own, other, operators, state, new_operators, new_state):
    core, *_ = position()
    for i in range(operators.shape[0]):
        g = unpacked(jnp.where(core == i, own[...], other[...]), operators.shape[1])
        moments = state[i] + g * g
        new_state[i] = moments
        new_operators[i] = operators[i] - operator_rate * g / (jnp.sqrt(moments) + epsilon)


def rep_swapped(array, by):
    peers = lax.axis_size("rep")
    return lax.ppermute(array, "rep", [(i, i ^ by) for i in range(peers)])


def along_ring(array, offset_of):
    groups, reps = lax.axis_size("ent"), lax.axis_size("rep")
    pairs = []
    for e in range(groups):
        for r in range(reps):
            way = offset_of(r) if r % CORES == 1 else -offset_of(r)
            to = RING[(PLACE[e] + way) % groups]
            pairs.append((e * reps + r, to * reps + r))
    return lax.ppermute(array, ("ent", "rep"), pairs)


def ring_step(array):
    return along_ring(array, lambda r: -1)


def handed_on(array, k):
    return along_ring(array, lambda r: OFFSETS[k][0 if r < CORES else 1])


def gathered_shards(
    entity_table, entity_state, operators, operator_state, sources, destinations, relations, negatives
):
    groups, reps = lax.axis_size("ent"), lax.axis_size("rep")
    entities, width = entity_table.shape
    edges = sources.shape[0]
    relation_count = groups * operators.shape[0]
    half = entities // CORES
    core = lax.axis_index("rep") % CORES

    operators_half = operators.astype(bf16)
    table = entity_table.T
    ids = jnp.concatenate(
        [
            sources,
            destinations,
            relations[:, 0],
            negatives[0],
            jnp.full((5 * edges - negatives.shape[1],), -1, jnp.int32),
        ]
    ).reshape(8, edges)
    places = relation_count
    slot_out = [
        jax.ShapeDtypeStruct((reps, places, SLOTS, width), bf16),
        jax.ShapeDtypeStruct((reps, 8, edges), f32),
        jax.ShapeDtypeStruct((reps, 1, entities), f32),
    ]
    a1 = ring_step(operators_half)
    others = [rep_swapped(ids, by) for by in (1, 2, 3)]
    own_half = lax.dynamic_slice_in_dim(table, core * half, half, 1).astype(bf16)
    a1, own_half, *others = lax.optimization_barrier((a1, own_half, *others))
    a2 = ring_step(a1)
    b1 = rep_swapped(a1, 1)
    b1, own_half = lax.optimization_barrier((b1, own_half))
    mine = passed_along(own_half, "ent", -1)
    a2, b1, late_table = lax.optimization_barrier((a2, b1, table))
    a3 = ring_step(a2)
    a4 = along_ring(lax.dynamic_slice_in_dim(a2, core, 1, 0), lambda r: -2)
    b2 = rep_swapped(a2, 1)
    table_half = late_table.astype(bf16)
    slots = call(slot_kernel, slot_out, "slots", 10**8, 10**6, (ids, *others, table_half))
    a3, a4, b2, mine, *slots = lax.optimization_barrier((a3, a4, b2, mine, *slots))
    slotted, rows, counts = slots
    other = rep_swapped(mine, 1)
    b3 = rep_swapped(a3, 1)
    b4 = rep_swapped(a4, 1)
    gathered = (operators_half, a1, a2, a3, a4, b4, b3, b2, b1)

    score_out = [jax.ShapeDtypeStruct((width + SIDE + 16, LANES), bf16)] * len(OFFSETS) + [
        jax.ShapeDtypeStruct((reps, edges, entities), bf16),
        jax.ShapeDtypeStruct((reps, 3 * edges, width), bf16),
        jax.ShapeDtypeStruct((reps, edges, width), bf16),
    ]
    *handed, weights, sides, query = call(
        functools.partial(score_kernel, negatives.shape[1]), score_out, "scores", 10**9, 10**6,
        (*gathered, slotted, rows, counts, mine, other),
        scratch=[
            VMEM((width, entities), bf16),
            VMEM((reps, places, SLOTS, width), bf16),
            VMEM((reps, len(OFFSETS), SLOTS, width), bf16),
        ],
    )
    arrived = [handed_on(matrix, k) for k, matrix in enumerate(handed)]
    (target_half,) = call(
        target_kernel,
        [jax.ShapeDtypeStruct((width, half), bf16)],
        "targets", 10**8, 10**6, (rows, weights, sides),
        scratch=[VMEM((width, entities), f32)],
    )
    query, target_half = lax.optimization_barrier((query, target_half))
    (source_total,) = call(
        source_kernel,
        [jax.ShapeDtypeStruct((width, entities), f32)],
        "sources", 10**8, 10**6, (*gathered, rows, query),
        scratch=[VMEM((reps, places, SLOTS, width), bf16)],
    )
    home_mine = passed_along(target_half, "ent", 1)
    home_other = rep_swapped(home_mine, 1)
    source_total, *arrived = lax.optimization_barrier((source_total, *arrived))
    one_chip = sum(matrix.astype(f32) for matrix in arrived).astype(bf16)
    one_relation = one_chip.astype(f32) + rep_swapped(one_chip, CORES).astype(f32)
    other_relation = rep_swapped(one_relation, 1)
    new_table, new_state = call(
        entity_kernel,
        [
            jax.ShapeDtypeStruct((width, entities), f32),
            jax.ShapeDtypeStruct((1, entities), f32),
        ],
        "entity_update", 10**6, 10**6,
        (source_total, home_mine, home_other, table, entity_state.reshape(1, -1)),
    )
    new_operators, new_operator_state = call(
        operator_kernel,
        [jax.ShapeDtypeStruct(operators.shape, f32)] * 2,
        "operator_update", 10**6, 10**6,
        (one_relation, other_relation, operators, operator_state),
    )
    return (new_table.T, new_state.reshape(-1), new_operators, new_operator_state)


def solution(mesh):
    placed = (
        P("ent", None),
        P("ent"),
        P("ent", None, None),
        P("ent", None, None),
        P(("ent", "rep")),
        P(("ent", "rep")),
        P(("ent", "rep"), None),
        P(("ent", "rep"), None),
    )
    small = mesh.shape["ent"] == len(RING) and mesh.shape["rep"] == 2 * CORES
    return jax.shard_map(
        gathered_shards if small else exchanged_shards,
        mesh=mesh,
        in_specs=placed,
        out_specs=(P("ent", None), P("ent"), P("ent", None, None), P("ent", None, None)),
        check_vma=False,
    )
```

```python
import functools

import jax
import jax.numpy as jnp
from jax import lax
from jax.experimental import pallas as pl
from jax.experimental.pallas import tpu as pltpu
from jax.sharding import PartitionSpec as P

SPAN = 256
EDGE_DEV = 256
REL_DEV = 2


entity_rate = 0.1
operator_rate = 0.02
epsilon = 1e-06


def passed_along(array, axis, by):
    peers = lax.axis_size(axis)
    return lax.ppermute(array, axis, [(i, (i + by) % peers) for i in range(peers)])


def place_slots(relation_ids, capacity):
    count_edges = relation_ids.shape[0]
    ordering = jnp.argsort(relation_ids, stable=True)
    ranked = relation_ids[ordering]
    leading = jnp.searchsorted(ranked, ranked, side="left")
    within = jnp.arange(count_edges, dtype=jnp.int32) - leading
    position = jnp.zeros((count_edges,), jnp.int32).at[ordering].set(within)
    return relation_ids * capacity + position


def score_grads(transformed, target_ids, negative_ids, table_rows):
    target_rows = jnp.take(table_rows, target_ids, axis=0)
    positive = jnp.sum(transformed.astype(jnp.float32) * target_rows.astype(jnp.float32), axis=-1)
    positive_grad = -jax.nn.sigmoid(-positive)
    width = transformed.shape[1]
    blocks = transformed.reshape(-1, SPAN, width)
    negative_count = negative_ids.shape[1]

    def span_step(running, pieces):
        query_block, negative_block = pieces
        negative_rows = jnp.take(table_rows, negative_block, axis=0)
        scores = lax.dot_general(
            query_block, negative_rows, (((1,), (1,)), ((), ())), preferred_element_type=jnp.float32
        )
        negative_grad = (jax.nn.sigmoid(scores) / negative_count).astype(jnp.bfloat16)
        query_part = jnp.dot(negative_grad, negative_rows, preferred_element_type=jnp.float32)
        row_update = lax.dot_general(
            negative_grad, query_block, (((0,), (0,)), ((), ())), preferred_element_type=jnp.float32
        )
        return (running.at[negative_block].add(row_update), query_part)

    starting = jnp.zeros((table_rows.shape[0], width), jnp.float32)
    negative_total, query_parts = lax.scan(span_step, starting, (blocks, negative_ids))
    query_grad = (
        positive_grad[:, None] * target_rows.astype(jnp.float32) + query_parts.reshape(-1, width)
    ).astype(jnp.bfloat16)
    target_grad = negative_total.at[target_ids].add(
        positive_grad[:, None] * transformed.astype(jnp.float32)
    )
    return (query_grad, target_grad)


def row_adagrad(weights, moments, gradient):
    fresh_moments = moments + jnp.mean(gradient * gradient, axis=-1)
    updated = weights - entity_rate * gradient / (jnp.sqrt(fresh_moments)[:, None] + epsilon)
    return (updated, fresh_moments)


def dense_adagrad(weights, moments, gradient):
    fresh_moments = moments + gradient * gradient
    updated = weights - operator_rate * gradient / (jnp.sqrt(fresh_moments) + epsilon)
    return (updated, fresh_moments)


def exchanged_shards(
    entity_table,
    entity_state,
    operators,
    operator_state,
    sources,
    destinations,
    relations,
    negatives,
):
    groups = lax.axis_size("ent")
    relation_count = REL_DEV * groups
    capacity = max(2, (2 * EDGE_DEV + relation_count - 1) // relation_count)
    width = entity_table.shape[1]
    table_half = entity_table.astype(jnp.bfloat16)
    operators_half = operators.astype(jnp.bfloat16)
    slot_index = place_slots(relations[:, 0], capacity)
    source_rows = jnp.take(table_half, sources, axis=0)
    outgoing = (
        jnp.zeros((relation_count * capacity, width), jnp.bfloat16).at[slot_index].set(source_rows)
    )
    outgoing = outgoing.reshape(groups, REL_DEV, capacity, width)
    arrived = lax.all_to_all(outgoing, "ent", split_axis=0, concat_axis=0, tiled=True)
    result = jnp.einsum(
        "srmd,rdk->srmk", arrived, operators_half, preferred_element_type=jnp.float32
    ).astype(jnp.bfloat16)
    returned = lax.all_to_all(result, "ent", split_axis=0, concat_axis=0, tiled=True)
    transformed_slots = returned
    transformed = jnp.take(transformed_slots.reshape(-1, width), slot_index, axis=0)
    neighbour_table = passed_along(table_half, "ent", -1)
    query_grad, target_grad = score_grads(transformed, destinations, negatives, neighbour_table)
    home_grad = passed_along(target_grad, "ent", 1)
    grad_slots = (
        jnp.zeros((relation_count * capacity, width), jnp.bfloat16).at[slot_index].set(query_grad)
    )
    grad_slots = grad_slots.reshape(groups, REL_DEV, capacity, width)
    arrived_grads = lax.all_to_all(grad_slots, "ent", split_axis=0, concat_axis=0, tiled=True)
    source_grads = jnp.einsum(
        "srmk,rdk->srmd", arrived_grads, operators_half, preferred_element_type=jnp.float32
    ).astype(jnp.bfloat16)
    returned = lax.all_to_all(source_grads, "ent", split_axis=0, concat_axis=0, tiled=True)
    operator_grad = jnp.einsum(
        "srmd,srmk->rdk", arrived, arrived_grads, preferred_element_type=jnp.float32
    )
    source_grad = jnp.take(returned.reshape(-1, width), slot_index, axis=0)
    entity_grad = (
        jnp.zeros(entity_table.shape, jnp.float32).at[sources].add(source_grad.astype(jnp.float32))
        + home_grad
    )
    total_grad, total_operator = lax.psum((entity_grad, operator_grad), "rep")
    new_table, new_entity_state = row_adagrad(entity_table, entity_state, total_grad)
    new_operators, new_operator_state = dense_adagrad(operators, operator_state, total_operator)
    return (new_table, new_entity_state, new_operators, new_operator_state)


bf16 = jnp.bfloat16
f32 = jnp.float32
CORES = 2
LANES = 128
RING = (0, 2, 4, 6, 7, 5, 3, 1)
PLACE = tuple(RING.index(e) for e in range(8))
SLOTS = 32
SIDE = 104
OFFSETS = ((0, 4), (3, 1), (5, 7), (2, 6))
VMEM = pltpu.VMEM
NT = (((1,), (1,)), ((), ()))
TN = (((0,), (0,)), ((), ()))


def dot(a, b, dims=(((1,), (0,)), ((), ()))):
    return lax.dot_general(a, b, dims, preferred_element_type=f32)


def lanes_of(shape):
    return lax.broadcasted_iota(jnp.int32, shape, 1)


def rows_of(shape):
    return lax.broadcasted_iota(jnp.int32, shape, 0)


def one_hot(mask):
    return jnp.where(mask, 1.0, 0.0).astype(bf16)


def call(body, outs, name, flops, size, operands, limit=16, scratch=()):
    whole = pl.BlockSpec(memory_space=VMEM)
    return pl.pallas_call(
        body,
        out_shape=outs,
        in_specs=[whole] * len(operands),
        out_specs=[whole] * len(outs),
        scratch_shapes=list(scratch),
        name=name,
        cost_estimate=pl.CostEstimate(flops=flops, bytes_accessed=size, transcendentals=0),
        compiler_params=pltpu.CompilerParams(vmem_limit_bytes=limit * 2**20),
    )(*operands)


def chosen_from(listed, at):
    found = jnp.zeros_like(at)
    for i, value in enumerate(listed):
        found = jnp.where(at == i, value, found)
    return found


def position():
    rep = lax.axis_index("rep")
    core = lax.rem(rep, CORES)
    return core, rep, chosen_from(PLACE, lax.axis_index("ent")), 2 * core - 1


def slot_kernel(own, near, far, across, table, slotted, rows, counts):
    core, me, here, sign = position()
    ring = len(RING)
    reps, _, edges = rows.shape
    places = slotted.shape[1]
    ids = [ref[...] for ref in (own, near, far, across)]
    before = one_hot(rows_of((edges, edges)) > lanes_of((edges, edges)))
    relation = jnp.concatenate([block[2:3] for block in ids], axis=0)
    offset = lax.bitwise_and(
        sign * (chosen_from(PLACE, lax.shift_right_logical(relation, 1)) - here), ring - 1
    )
    parity = lax.bitwise_and(relation, 1)
    local = 2 * offset + jnp.where(offset == ring // 2, lax.bitwise_xor(parity, core), parity)
    ends = [block[i : i + 1] for i in (0, 1) for block in ids]
    standing = jnp.concatenate([local, *ends], axis=0).astype(f32).T
    column = lambda i: standing[:, i : i + 1].astype(jnp.int32)
    named = [lanes_of((edges, LANES)) == column(m) for m in range(reps)]
    ahead = dot(before, one_hot(jnp.concatenate(named, axis=1)))
    slots = jnp.concatenate(
        [
            standing[:, m : m + 1] * SLOTS
            + jnp.sum(
                jnp.where(named[m], ahead[:, m * LANES : (m + 1) * LANES], 0.0), axis=1, keepdims=True
            )
            for m in range(reps)
        ],
        axis=1,
    ).T
    for m in range(reps):
        block = lax.bitwise_xor(me, m)
        lying = jnp.concatenate(
            [ids[m][0:2].astype(f32), slots[m : m + 1], ids[m][3:8].astype(f32)], axis=0
        )
        rows[block] = lying
        tally = jnp.zeros((8, LANES), f32)
        for k in range(3, 7):
            drawn = ids[m][k : k + 1]
            high = one_hot(rows_of((8, edges)) == lax.shift_right_arithmetic(drawn, 7))
            low = one_hot(rows_of((LANES, edges)) == lax.bitwise_and(drawn, LANES - 1))
            tally = tally + dot(high, low, NT)
        counts[block] = jnp.concatenate([tally[k : k + 1] for k in range(8)], axis=1)
    picked = [
        one_hot(lanes_of((edges, table.shape[1])) == column(reps + m)) for m in range(reps)
    ]
    source_rows = dot(jnp.concatenate(picked, axis=0), table[...], NT).astype(bf16)
    for m in range(reps):
        into = one_hot(rows_of((places * SLOTS, edges)) == slots[m : m + 1].astype(jnp.int32))
        given = dot(into, source_rows[m * edges : (m + 1) * edges]).astype(bf16)
        slotted[lax.bitwise_xor(me, m)] = given.reshape(places, SLOTS, -1)


def join(table, mine, other):
    half = mine.shape[1]
    core, *_ = position()
    table[:, pl.ds(pl.multiple_of(core * half, half), half)] = mine[...]
    table[:, pl.ds(pl.multiple_of((1 - core) * half, half), half)] = other[...]


LATE = (6, 12)


def transform(moved, slotted, place, at, op):
    reps, _, _, width = slotted.shape
    given = slotted[:, place].reshape(reps * SLOTS, width)
    moved[:, at] = dot(given, op).astype(bf16).reshape(reps, SLOTS, width)


def ready_kernel(o0, a1, a2, b2, b1, slotted, rows, made_early, moved):
    reps, _, edges = rows.shape
    places, width = slotted.shape[1], slotted.shape[3]
    moved[:, LATE[0] : LATE[1]] = jnp.zeros((reps, LATE[1] - LATE[0], SLOTS, width), bf16)
    for place, op in enumerate(operator_list(o0, a1, a2, None, None, None, None, b2, b1)):
        if op is not None:
            transform(moved, slotted, place, place, op())
    for b in range(reps):
        slot = rows[b].T[:, 2:3].astype(jnp.int32)
        out_of = one_hot(lanes_of((edges, places * SLOTS)) == slot)
        made = dot(out_of, moved[b].reshape(places * SLOTS, width))
        made_early[b * edges : (b + 1) * edges] = made.astype(bf16)


def score_kernel(
    negative_count, a3, a4, b4, b3, slotted, rows, counts, mine, other, made_early,
    s0, s1, s2, s3, weights, sides, query, table, moved, asking,
):
    core, me, *_ = position()
    reps, places = slotted.shape[:2]
    width, entities = table.shape
    edges = rows.shape[2]
    join(table, mine, other)
    for place, op in enumerate(operator_list(None, None, None, a3, a4, b4, b3, None, None)):
        if op is not None:
            transform(moved, slotted, place, place - LATE[0], op())
    sent = (s0, s1, s2, s3)
    handed = []
    for near, far in OFFSETS:
        offset = jnp.where(me < CORES, near, far)
        handed.append(2 * offset + jnp.where(offset == len(RING) // 2, 0, core))
    lying = [rows[b] for b in range(reps)]
    standing = [block.T.astype(jnp.int32) for block in lying]
    made = []
    for b in range(reps):
        late = (LATE[1] - LATE[0]) * SLOTS
        out_of = one_hot(lanes_of((edges, late)) + LATE[0] * SLOTS == standing[b][:, 2:3])
        made.append(dot(out_of, moved[b].reshape(late, width)))
    made = jnp.concatenate(made, axis=0) + made_early[...].astype(f32)
    made_half = made.astype(bf16)
    scores = dot(made_half, table[...])
    aimed = lanes_of((reps * edges, entities)) == jnp.concatenate(
        [block[:, 1:2] for block in standing], axis=0
    )
    positive = jnp.sum(jnp.where(aimed, scores, 0.0), axis=1, keepdims=True)
    positive_grad = -(0.5 * jnp.tanh(-0.5 * positive) + 0.5)
    share = (0.5 * jnp.tanh(0.5 * scores) + 0.5) * (1.0 / negative_count)
    share = share.astype(bf16).astype(f32)
    weighted = jnp.concatenate(
        [share[b * edges : (b + 1) * edges] * counts[b] for b in range(reps)], axis=0
    ).astype(bf16)
    target_rows = dot(one_hot(aimed), table[...], NT)
    asked = (positive_grad * target_rows + dot(weighted, table[...], NT)).astype(bf16)
    push = positive_grad * made
    push_half = push.astype(bf16)
    push_rest = (push - push_half.astype(f32)).astype(bf16)
    for b in range(reps):
        at = slice(b * edges, (b + 1) * edges)
        weights[b] = weighted[at]
        sides[b, :edges] = made_half[at]
        sides[b, edges : 2 * edges] = push_half[at]
        sides[b, 2 * edges :] = push_rest[at]
        query[b] = asked[at]
        slot = lying[b][2:3].astype(jnp.int32)
        into = jnp.concatenate(
            [one_hot(rows_of((SLOTS, edges)) + place * SLOTS == slot) for place in handed], axis=0
        )
        asking[b] = dot(into, asked[at]).astype(bf16).reshape(len(sent), SLOTS, width)
    for k, place in enumerate(handed):
        given = slotted[:, pl.ds(place, 1)].reshape(reps * SLOTS, width)
        sent[k][...] = packed(dot(given, asking[:, k].reshape(reps * SLOTS, width), TN)).astype(bf16)


def packed(matrix):
    low, side, spare = matrix[:, :LANES], matrix[:, LANES : LANES + 64], matrix[:, LANES + 64 :]
    side = jnp.concatenate([side[:SIDE], side[side.shape[0] - SIDE :]], axis=1)
    spare = spare.T
    rest = jnp.zeros((spare.shape[0], 2 * LANES - spare.shape[1]), spare.dtype)
    return jnp.concatenate(
        [low, side, spare[:, :LANES], jnp.concatenate([spare[:, LANES:], rest], axis=1)], axis=0
    )


def unpacked(rows, size):
    low, side, spare = rows[:size], rows[size : size + SIDE], rows[size + SIDE :]
    side = jnp.concatenate([side[:, :64], side[2 * SIDE - size :, 64:]], axis=0)
    count = size - LANES - 64
    spare = jnp.concatenate([spare[:count], spare[count:, : size - LANES]], axis=1)
    return jnp.concatenate([low, side, spare.T], axis=1)


def operator_list(o0, a1, a2, a3, a4, b4, b3, b2, b1):
    listed = [(o0, 0), (o0, 1)]
    for ref in (a1, a2, a3):
        listed += [(ref, 0), (ref, 1)]
    listed += [(a4, 0), (b4, 0)]
    for ref in (b3, b2, b1):
        listed += [(ref, 0), (ref, 1)]
    return [None if ref is None else lambda ref=ref, i=i: ref[i] for ref, i in listed]


def target_kernel(rows, weights, sides, target_half, total):
    core, *_ = position()
    reps, edges, entities = weights.shape
    half = target_half.shape[1]
    for b in range(reps):
        aimed = one_hot(lanes_of((edges, entities)) == rows[b].T[:, 1:2].astype(jnp.int32))
        grown = dot(sides[b], jnp.concatenate([weights[b], aimed, aimed], axis=0), TN)
        if b == 0:
            total[...] = grown
        else:
            total[...] += grown
    target_half[...] = total[:, pl.ds(pl.multiple_of(core * half, half), half)].astype(bf16)


def source_kernel(o0, a1, a2, a3, a4, b4, b3, b2, b1, rows, query, source_total, held):
    reps, places, _, width = held.shape
    edges, entities = rows.shape[2], source_total.shape[1]
    for b in range(reps):
        into = one_hot(rows_of((places * SLOTS, edges)) == rows[b][2:3].astype(jnp.int32))
        held[b] = dot(into, query[b]).astype(bf16).reshape(places, SLOTS, width)
    for place, op in enumerate(operator_list(o0, a1, a2, a3, a4, b4, b3, b2, b1)):
        given = held[:, place].reshape(-1, width)
        held[:, place] = dot(given, op(), NT).astype(bf16).reshape(-1, SLOTS, width)
    for b in range(reps):
        standing = rows[b].T.astype(jnp.int32)
        out_of = one_hot(lanes_of((edges, places * SLOTS)) == standing[:, 2:3])
        back = dot(out_of, held[b].reshape(places * SLOTS, width)).astype(bf16)
        spread = one_hot(lanes_of((edges, entities)) == standing[:, 0:1])
        grown = dot(back, spread, TN)
        if b == 0:
            source_total[...] = grown
        else:
            source_total[...] += grown


def entity_kernel(source_total, mine, other, table, state, new_table, new_state):
    core, *_ = position()
    half = mine.shape[1]
    width = table.shape[0]
    for part, side in ((mine, core), (other, 1 - core)):
        at = pl.ds(pl.multiple_of(side * half, half), half)
        g = source_total[:, at] + part[...].astype(f32)
        moments = state[:, at] + jnp.sum(g * g, axis=0, keepdims=True) * (1.0 / width)
        new_state[:, at] = moments
        new_table[:, at] = table[:, at] - g * (entity_rate / (jnp.sqrt(moments) + epsilon))


def operator_kernel(own, other, operators, state, new_operators, new_state):
    core, *_ = position()
    for i in range(operators.shape[0]):
        g = unpacked(jnp.where(core == i, own[...], other[...]), operators.shape[1])
        moments = state[i] + g * g
        new_state[i] = moments
        new_operators[i] = operators[i] - operator_rate * g / (jnp.sqrt(moments) + epsilon)


def rep_swapped(array, by):
    peers = lax.axis_size("rep")
    return lax.ppermute(array, "rep", [(i, i ^ by) for i in range(peers)])


def along_ring(array, offset_of):
    groups, reps = lax.axis_size("ent"), lax.axis_size("rep")
    pairs = []
    for e in range(groups):
        for r in range(reps):
            way = offset_of(r) if r % CORES == 1 else -offset_of(r)
            to = RING[(PLACE[e] + way) % groups]
            pairs.append((e * reps + r, to * reps + r))
    return lax.ppermute(array, ("ent", "rep"), pairs)


def ring_step(array):
    return along_ring(array, lambda r: -1)


def handed_on(array, k):
    return along_ring(array, lambda r: OFFSETS[k][0 if r < CORES else 1])


def gathered_shards(
    entity_table, entity_state, operators, operator_state, sources, destinations, relations, negatives
):
    groups, reps = lax.axis_size("ent"), lax.axis_size("rep")
    entities, width = entity_table.shape
    edges = sources.shape[0]
    relation_count = groups * operators.shape[0]
    half = entities // CORES
    core = lax.axis_index("rep") % CORES

    operators_half = operators.astype(bf16)
    table = entity_table.T
    ids = jnp.concatenate(
        [
            sources,
            destinations,
            relations[:, 0],
            negatives[0],
            jnp.full((5 * edges - negatives.shape[1],), -1, jnp.int32),
        ]
    ).reshape(8, edges)
    places = relation_count
    slot_out = [
        jax.ShapeDtypeStruct((reps, places, SLOTS, width), bf16),
        jax.ShapeDtypeStruct((reps, 8, edges), f32),
        jax.ShapeDtypeStruct((reps, 1, entities), f32),
    ]
    a1 = ring_step(operators_half)
    others = [rep_swapped(ids, by) for by in (1, 2, 3)]
    own_half = lax.dynamic_slice_in_dim(table, core * half, half, 1).astype(bf16)
    a1, own_half, *others = lax.optimization_barrier((a1, own_half, *others))
    a2 = ring_step(a1)
    b1 = rep_swapped(a1, 1)
    b1, own_half = lax.optimization_barrier((b1, own_half))
    mine = passed_along(own_half, "ent", -1)
    a2, b1, late_table = lax.optimization_barrier((a2, b1, table))
    a3 = ring_step(a2)
    a4 = along_ring(lax.dynamic_slice_in_dim(a2, core, 1, 0), lambda r: -2)
    b2 = rep_swapped(a2, 1)
    table_half = late_table.astype(bf16)
    slots = call(slot_kernel, slot_out, "slots", 10**8, 10**6, (ids, *others, table_half))
    a3, a4, b2, mine, *slots = lax.optimization_barrier((a3, a4, b2, mine, *slots))
    slotted, rows, counts = slots
    other = rep_swapped(mine, 1)
    b3 = rep_swapped(a3, 1)
    b4 = rep_swapped(a4, 1)
    (made_early,) = call(
        ready_kernel,
        [jax.ShapeDtypeStruct((reps * edges, width), bf16)],
        "ready", 10**8, 10**6, (operators_half, a1, a2, b2, b1, slotted, rows),
        scratch=[VMEM((reps, places, SLOTS, width), bf16)],
    )
    gathered = (operators_half, a1, a2, a3, a4, b4, b3, b2, b1)

    score_out = [jax.ShapeDtypeStruct((width + SIDE + 16, LANES), bf16)] * len(OFFSETS) + [
        jax.ShapeDtypeStruct((reps, edges, entities), bf16),
        jax.ShapeDtypeStruct((reps, 3 * edges, width), bf16),
        jax.ShapeDtypeStruct((reps, edges, width), bf16),
    ]
    *handed, weights, sides, query = call(
        functools.partial(score_kernel, negatives.shape[1]), score_out, "scores", 10**9, 10**6,
        (a3, a4, b4, b3, slotted, rows, counts, mine, other, made_early),
        scratch=[
            VMEM((width, entities), bf16),
            VMEM((reps, LATE[1] - LATE[0], SLOTS, width), bf16),
            VMEM((reps, len(OFFSETS), SLOTS, width), bf16),
        ],
    )
    arrived = [handed_on(matrix, k) for k, matrix in enumerate(handed)]
    (target_half,) = call(
        target_kernel,
        [jax.ShapeDtypeStruct((width, half), bf16)],
        "targets", 10**8, 10**6, (rows, weights, sides),
        scratch=[VMEM((width, entities), f32)],
    )
    query, target_half = lax.optimization_barrier((query, target_half))
    (source_total,) = call(
        source_kernel,
        [jax.ShapeDtypeStruct((width, entities), f32)],
        "sources", 10**8, 10**6, (*gathered, rows, query),
        scratch=[VMEM((reps, places, SLOTS, width), bf16)],
    )
    home_mine = passed_along(target_half, "ent", 1)
    home_other = rep_swapped(home_mine, 1)
    source_total, *arrived = lax.optimization_barrier((source_total, *arrived))
    one_chip = sum(matrix.astype(f32) for matrix in arrived).astype(bf16)
    one_relation = one_chip.astype(f32) + rep_swapped(one_chip, CORES).astype(f32)
    other_relation = rep_swapped(one_relation, 1)
    new_table, new_state = call(
        entity_kernel,
        [
            jax.ShapeDtypeStruct((width, entities), f32),
            jax.ShapeDtypeStruct((1, entities), f32),
        ],
        "entity_update", 10**6, 10**6,
        (source_total, home_mine, home_other, table, entity_state.reshape(1, -1)),
    )
    other_relation, new_table, new_state = lax.optimization_barrier(
        (other_relation, new_table, new_state)
    )
    new_operators, new_operator_state = call(
        operator_kernel,
        [jax.ShapeDtypeStruct(operators.shape, f32)] * 2,
        "operator_update", 10**6, 10**6,
        (one_relation, other_relation, operators, operator_state),
    )
    return (new_table.T, new_state.reshape(-1), new_operators, new_operator_state)


def solution(mesh):
    placed = (
        P("ent", None),
        P("ent"),
        P("ent", None, None),
        P("ent", None, None),
        P(("ent", "rep")),
        P(("ent", "rep")),
        P(("ent", "rep"), None),
        P(("ent", "rep"), None),
    )
    small = mesh.shape["ent"] == len(RING) and mesh.shape["rep"] == 2 * CORES
    return jax.shard_map(
        gathered_shards if small else exchanged_shards,
        mesh=mesh,
        in_specs=placed,
        out_specs=(P("ent", None), P("ent"), P("ent", None, None), P("ent", None, None)),
        check_vma=False,
    )
```

```python
import functools

import jax
import jax.numpy as jnp
from jax import lax
from jax.experimental import pallas as pl
from jax.experimental.pallas import tpu as pltpu
from jax.sharding import PartitionSpec as P

SPAN = 256
EDGE_DEV = 256
REL_DEV = 2


entity_rate = 0.1
operator_rate = 0.02
epsilon = 1e-06


def passed_along(array, axis, by):
    peers = lax.axis_size(axis)
    return lax.ppermute(array, axis, [(i, (i + by) % peers) for i in range(peers)])


def place_slots(relation_ids, capacity):
    count_edges = relation_ids.shape[0]
    ordering = jnp.argsort(relation_ids, stable=True)
    ranked = relation_ids[ordering]
    leading = jnp.searchsorted(ranked, ranked, side="left")
    within = jnp.arange(count_edges, dtype=jnp.int32) - leading
    position = jnp.zeros((count_edges,), jnp.int32).at[ordering].set(within)
    return relation_ids * capacity + position


def score_grads(transformed, target_ids, negative_ids, table_rows):
    target_rows = jnp.take(table_rows, target_ids, axis=0)
    positive = jnp.sum(transformed.astype(jnp.float32) * target_rows.astype(jnp.float32), axis=-1)
    positive_grad = -jax.nn.sigmoid(-positive)
    width = transformed.shape[1]
    blocks = transformed.reshape(-1, SPAN, width)
    negative_count = negative_ids.shape[1]

    def span_step(running, pieces):
        query_block, negative_block = pieces
        negative_rows = jnp.take(table_rows, negative_block, axis=0)
        scores = lax.dot_general(
            query_block, negative_rows, (((1,), (1,)), ((), ())), preferred_element_type=jnp.float32
        )
        negative_grad = (jax.nn.sigmoid(scores) / negative_count).astype(jnp.bfloat16)
        query_part = jnp.dot(negative_grad, negative_rows, preferred_element_type=jnp.float32)
        row_update = lax.dot_general(
            negative_grad, query_block, (((0,), (0,)), ((), ())), preferred_element_type=jnp.float32
        )
        return (running.at[negative_block].add(row_update), query_part)

    starting = jnp.zeros((table_rows.shape[0], width), jnp.float32)
    negative_total, query_parts = lax.scan(span_step, starting, (blocks, negative_ids))
    query_grad = (
        positive_grad[:, None] * target_rows.astype(jnp.float32) + query_parts.reshape(-1, width)
    ).astype(jnp.bfloat16)
    target_grad = negative_total.at[target_ids].add(
        positive_grad[:, None] * transformed.astype(jnp.float32)
    )
    return (query_grad, target_grad)


def row_adagrad(weights, moments, gradient):
    fresh_moments = moments + jnp.mean(gradient * gradient, axis=-1)
    updated = weights - entity_rate * gradient / (jnp.sqrt(fresh_moments)[:, None] + epsilon)
    return (updated, fresh_moments)


def dense_adagrad(weights, moments, gradient):
    fresh_moments = moments + gradient * gradient
    updated = weights - operator_rate * gradient / (jnp.sqrt(fresh_moments) + epsilon)
    return (updated, fresh_moments)


def exchanged_shards(
    entity_table,
    entity_state,
    operators,
    operator_state,
    sources,
    destinations,
    relations,
    negatives,
):
    groups = lax.axis_size("ent")
    relation_count = REL_DEV * groups
    capacity = max(2, (2 * EDGE_DEV + relation_count - 1) // relation_count)
    width = entity_table.shape[1]
    table_half = entity_table.astype(jnp.bfloat16)
    operators_half = operators.astype(jnp.bfloat16)
    slot_index = place_slots(relations[:, 0], capacity)
    source_rows = jnp.take(table_half, sources, axis=0)
    outgoing = (
        jnp.zeros((relation_count * capacity, width), jnp.bfloat16).at[slot_index].set(source_rows)
    )
    outgoing = outgoing.reshape(groups, REL_DEV, capacity, width)
    arrived = lax.all_to_all(outgoing, "ent", split_axis=0, concat_axis=0, tiled=True)
    result = jnp.einsum(
        "srmd,rdk->srmk", arrived, operators_half, preferred_element_type=jnp.float32
    ).astype(jnp.bfloat16)
    returned = lax.all_to_all(result, "ent", split_axis=0, concat_axis=0, tiled=True)
    transformed_slots = returned
    transformed = jnp.take(transformed_slots.reshape(-1, width), slot_index, axis=0)
    neighbour_table = passed_along(table_half, "ent", -1)
    query_grad, target_grad = score_grads(transformed, destinations, negatives, neighbour_table)
    home_grad = passed_along(target_grad, "ent", 1)
    grad_slots = (
        jnp.zeros((relation_count * capacity, width), jnp.bfloat16).at[slot_index].set(query_grad)
    )
    grad_slots = grad_slots.reshape(groups, REL_DEV, capacity, width)
    arrived_grads = lax.all_to_all(grad_slots, "ent", split_axis=0, concat_axis=0, tiled=True)
    source_grads = jnp.einsum(
        "srmk,rdk->srmd", arrived_grads, operators_half, preferred_element_type=jnp.float32
    ).astype(jnp.bfloat16)
    returned = lax.all_to_all(source_grads, "ent", split_axis=0, concat_axis=0, tiled=True)
    operator_grad = jnp.einsum(
        "srmd,srmk->rdk", arrived, arrived_grads, preferred_element_type=jnp.float32
    )
    source_grad = jnp.take(returned.reshape(-1, width), slot_index, axis=0)
    entity_grad = (
        jnp.zeros(entity_table.shape, jnp.float32).at[sources].add(source_grad.astype(jnp.float32))
        + home_grad
    )
    total_grad, total_operator = lax.psum((entity_grad, operator_grad), "rep")
    new_table, new_entity_state = row_adagrad(entity_table, entity_state, total_grad)
    new_operators, new_operator_state = dense_adagrad(operators, operator_state, total_operator)
    return (new_table, new_entity_state, new_operators, new_operator_state)


bf16 = jnp.bfloat16
f32 = jnp.float32
CORES = 2
LANES = 128
RING = (0, 2, 4, 6, 7, 5, 3, 1)
PLACE = tuple(RING.index(e) for e in range(8))
SLOTS = 32
SIDE = 104
OFFSETS = ((3, 4), (5, 6), (2, 1), (0, 7))
VMEM = pltpu.VMEM
NT = (((1,), (1,)), ((), ()))
TN = (((0,), (0,)), ((), ()))


def dot(a, b, dims=(((1,), (0,)), ((), ()))):
    return lax.dot_general(a, b, dims, preferred_element_type=f32)


def lanes_of(shape):
    return lax.broadcasted_iota(jnp.int32, shape, 1)


def rows_of(shape):
    return lax.broadcasted_iota(jnp.int32, shape, 0)


def one_hot(mask):
    return jnp.where(mask, 1.0, 0.0).astype(bf16)


def call(body, outs, name, flops, size, operands, limit=16, scratch=()):
    whole = pl.BlockSpec(memory_space=VMEM)
    return pl.pallas_call(
        body,
        out_shape=outs,
        in_specs=[whole] * len(operands),
        out_specs=[whole] * len(outs),
        scratch_shapes=list(scratch),
        name=name,
        cost_estimate=pl.CostEstimate(flops=flops, bytes_accessed=size, transcendentals=0),
        compiler_params=pltpu.CompilerParams(vmem_limit_bytes=limit * 2**20),
    )(*operands)


def chosen_from(listed, at):
    found = jnp.zeros_like(at)
    for i, value in enumerate(listed):
        found = jnp.where(at == i, value, found)
    return found


def position():
    rep = lax.axis_index("rep")
    core = lax.rem(rep, CORES)
    return core, rep, chosen_from(PLACE, lax.axis_index("ent")), 2 * core - 1


def slot_kernel(own, near, far, across, table, slotted, rows, counts):
    core, me, here, sign = position()
    ring = len(RING)
    reps, _, edges = rows.shape
    places = slotted.shape[1]
    ids = [ref[...] for ref in (own, near, far, across)]
    before = one_hot(rows_of((edges, edges)) > lanes_of((edges, edges)))
    relation = jnp.concatenate([block[2:3] for block in ids], axis=0)
    offset = lax.bitwise_and(
        sign * (chosen_from(PLACE, lax.shift_right_logical(relation, 1)) - here), ring - 1
    )
    parity = lax.bitwise_and(relation, 1)
    local = 2 * offset + jnp.where(offset == ring // 2, lax.bitwise_xor(parity, core), parity)
    ends = [block[i : i + 1] for i in (0, 1) for block in ids]
    standing = jnp.concatenate([local, *ends], axis=0).astype(f32).T
    column = lambda i: standing[:, i : i + 1].astype(jnp.int32)
    named = [lanes_of((edges, LANES)) == column(m) for m in range(reps)]
    ahead = dot(before, one_hot(jnp.concatenate(named, axis=1)))
    slots = jnp.concatenate(
        [
            standing[:, m : m + 1] * SLOTS
            + jnp.sum(
                jnp.where(named[m], ahead[:, m * LANES : (m + 1) * LANES], 0.0), axis=1, keepdims=True
            )
            for m in range(reps)
        ],
        axis=1,
    ).T
    for m in range(reps):
        block = lax.bitwise_xor(me, m)
        lying = jnp.concatenate(
            [ids[m][0:2].astype(f32), slots[m : m + 1], ids[m][3:8].astype(f32)], axis=0
        )
        rows[block] = lying
        tally = jnp.zeros((8, LANES), f32)
        for k in range(3, 7):
            drawn = ids[m][k : k + 1]
            high = one_hot(rows_of((8, edges)) == lax.shift_right_arithmetic(drawn, 7))
            low = one_hot(rows_of((LANES, edges)) == lax.bitwise_and(drawn, LANES - 1))
            tally = tally + dot(high, low, NT)
        counts[block] = jnp.concatenate([tally[k : k + 1] for k in range(8)], axis=1)
    picked = [
        one_hot(lanes_of((edges, table.shape[1])) == column(reps + m)) for m in range(reps)
    ]
    source_rows = dot(jnp.concatenate(picked, axis=0), table[...], NT).astype(bf16)
    for m in range(reps):
        into = one_hot(rows_of((places * SLOTS, edges)) == slots[m : m + 1].astype(jnp.int32))
        given = dot(into, source_rows[m * edges : (m + 1) * edges]).astype(bf16)
        slotted[lax.bitwise_xor(me, m)] = given.reshape(places, SLOTS, -1)


def join(table, mine, other):
    half = mine.shape[1]
    core, *_ = position()
    table[:, pl.ds(pl.multiple_of(core * half, half), half)] = mine[...]
    table[:, pl.ds(pl.multiple_of((1 - core) * half, half), half)] = other[...]


LATE = (6, 12)


def transform(moved, slotted, place, at, op):
    reps, _, _, width = slotted.shape
    given = slotted[:, place].reshape(reps * SLOTS, width)
    moved[:, at] = dot(given, op).astype(bf16).reshape(reps, SLOTS, width)


def ready_kernel(o0, a1, a2, b2, b1, slotted, rows, made_early, moved):
    reps, _, edges = rows.shape
    places, width = slotted.shape[1], slotted.shape[3]
    moved[:, LATE[0] : LATE[1]] = jnp.zeros((reps, LATE[1] - LATE[0], SLOTS, width), bf16)
    for place, op in enumerate(operator_list(o0, a1, a2, None, None, None, None, b2, b1)):
        if op is not None:
            transform(moved, slotted, place, place, op())
    for b in range(reps):
        slot = rows[b].T[:, 2:3].astype(jnp.int32)
        out_of = one_hot(lanes_of((edges, places * SLOTS)) == slot)
        made = dot(out_of, moved[b].reshape(places * SLOTS, width))
        made_early[b * edges : (b + 1) * edges] = made.astype(bf16)


def score_kernel(
    negative_count, a3, a4, b4, b3, slotted, rows, counts, mine, other, made_early,
    s0, s1, s2, s3, weights, sides, query, table, moved, asking,
):
    core, me, *_ = position()
    reps, places = slotted.shape[:2]
    width, entities = table.shape
    edges = rows.shape[2]
    join(table, mine, other)
    for place, op in enumerate(operator_list(None, None, None, a3, a4, b4, b3, None, None)):
        if op is not None:
            transform(moved, slotted, place, place - LATE[0], op())
    sent = (s0, s1, s2, s3)
    handed = []
    for near, far in OFFSETS:
        offset = jnp.where(me < CORES, near, far)
        handed.append(2 * offset + jnp.where(offset == len(RING) // 2, 0, core))
    lying = [rows[b] for b in range(reps)]
    standing = [block.T.astype(jnp.int32) for block in lying]
    made = []
    for b in range(reps):
        late = (LATE[1] - LATE[0]) * SLOTS
        out_of = one_hot(lanes_of((edges, late)) + LATE[0] * SLOTS == standing[b][:, 2:3])
        made.append(dot(out_of, moved[b].reshape(late, width)))
    made = jnp.concatenate(made, axis=0) + made_early[...].astype(f32)
    made_half = made.astype(bf16)
    scores = dot(made_half, table[...])
    aimed = lanes_of((reps * edges, entities)) == jnp.concatenate(
        [block[:, 1:2] for block in standing], axis=0
    )
    positive = jnp.sum(jnp.where(aimed, scores, 0.0), axis=1, keepdims=True)
    positive_grad = -(0.5 * jnp.tanh(-0.5 * positive) + 0.5)
    share = (0.5 * jnp.tanh(0.5 * scores) + 0.5) * (1.0 / negative_count)
    share = share.astype(bf16).astype(f32)
    weighted = jnp.concatenate(
        [share[b * edges : (b + 1) * edges] * counts[b] for b in range(reps)], axis=0
    ).astype(bf16)
    target_rows = dot(one_hot(aimed), table[...], NT)
    asked = (positive_grad * target_rows + dot(weighted, table[...], NT)).astype(bf16)
    push = positive_grad * made
    push_half = push.astype(bf16)
    push_rest = (push - push_half.astype(f32)).astype(bf16)
    for b in range(reps):
        at = slice(b * edges, (b + 1) * edges)
        weights[b] = weighted[at]
        sides[b, :edges] = made_half[at]
        sides[b, edges : 2 * edges] = push_half[at]
        sides[b, 2 * edges :] = push_rest[at]
        query[b] = asked[at]
        slot = lying[b][2:3].astype(jnp.int32)
        into = jnp.concatenate(
            [one_hot(rows_of((SLOTS, edges)) + place * SLOTS == slot) for place in handed], axis=0
        )
        asking[b] = dot(into, asked[at]).astype(bf16).reshape(len(sent), SLOTS, width)
    for k, place in enumerate(handed):
        given = slotted[:, pl.ds(place, 1)].reshape(reps * SLOTS, width)
        sent[k][...] = packed(dot(given, asking[:, k].reshape(reps * SLOTS, width), TN)).astype(bf16)


def packed(matrix):
    low, side, spare = matrix[:, :LANES], matrix[:, LANES : LANES + 64], matrix[:, LANES + 64 :]
    side = jnp.concatenate([side[:SIDE], side[side.shape[0] - SIDE :]], axis=1)
    spare = spare.T
    rest = jnp.zeros((spare.shape[0], 2 * LANES - spare.shape[1]), spare.dtype)
    return jnp.concatenate(
        [low, side, spare[:, :LANES], jnp.concatenate([spare[:, LANES:], rest], axis=1)], axis=0
    )


def unpacked(rows, size):
    low, side, spare = rows[:size], rows[size : size + SIDE], rows[size + SIDE :]
    side = jnp.concatenate([side[:, :64], side[2 * SIDE - size :, 64:]], axis=0)
    count = size - LANES - 64
    spare = jnp.concatenate([spare[:count], spare[count:, : size - LANES]], axis=1)
    return jnp.concatenate([low, side, spare.T], axis=1)


def operator_list(o0, a1, a2, a3, a4, b4, b3, b2, b1):
    listed = [(o0, 0), (o0, 1)]
    for ref in (a1, a2, a3):
        listed += [(ref, 0), (ref, 1)]
    listed += [(a4, 0), (b4, 0)]
    for ref in (b3, b2, b1):
        listed += [(ref, 0), (ref, 1)]
    return [None if ref is None else lambda ref=ref, i=i: ref[i] for ref, i in listed]


def target_kernel(rows, weights, sides, target_half):
    core, *_ = position()
    reps, edges, _ = weights.shape
    half = target_half.shape[1]
    at = pl.ds(pl.multiple_of(core * half, half), half)
    grown = jnp.zeros(target_half.shape, f32)
    for b in range(reps):
        aimed = one_hot(
            lanes_of((edges, half)) + core * half == rows[b].T[:, 1:2].astype(jnp.int32)
        )
        faces = jnp.concatenate([weights[b, :, at], aimed, aimed], axis=0)
        grown = grown + dot(sides[b], faces, TN)
    target_half[...] = grown.astype(bf16)


def source_kernel(o0, a1, a2, a3, a4, b4, b3, b2, b1, rows, query, source_total, held):
    reps, places, _, width = held.shape
    edges, entities = rows.shape[2], source_total.shape[1]
    for b in range(reps):
        into = one_hot(rows_of((places * SLOTS, edges)) == rows[b][2:3].astype(jnp.int32))
        held[b] = dot(into, query[b]).astype(bf16).reshape(places, SLOTS, width)
    for place, op in enumerate(operator_list(o0, a1, a2, a3, a4, b4, b3, b2, b1)):
        given = held[:, place].reshape(-1, width)
        held[:, place] = dot(given, op(), NT).astype(bf16).reshape(-1, SLOTS, width)
    for b in range(reps):
        standing = rows[b].T.astype(jnp.int32)
        out_of = one_hot(lanes_of((edges, places * SLOTS)) == standing[:, 2:3])
        back = dot(out_of, held[b].reshape(places * SLOTS, width)).astype(bf16)
        spread = one_hot(lanes_of((edges, entities)) == standing[:, 0:1])
        grown = dot(back, spread, TN)
        if b == 0:
            source_total[...] = grown
        else:
            source_total[...] += grown


def entity_kernel(source_total, mine, other, table, state, new_table, new_state):
    core, *_ = position()
    half = mine.shape[1]
    width = table.shape[0]
    for part, side in ((mine, core), (other, 1 - core)):
        at = pl.ds(pl.multiple_of(side * half, half), half)
        g = source_total[:, at] + part[...].astype(f32)
        moments = state[:, at] + jnp.sum(g * g, axis=0, keepdims=True) * (1.0 / width)
        new_state[:, at] = moments
        new_table[:, at] = table[:, at] - g * (entity_rate / (jnp.sqrt(moments) + epsilon))


def operator_kernel(own, other, operators, state, new_operators, new_state):
    core, *_ = position()
    for i in range(operators.shape[0]):
        g = unpacked(jnp.where(core == i, own[...], other[...]), operators.shape[1])
        moments = state[i] + g * g
        new_state[i] = moments
        new_operators[i] = operators[i] - operator_rate * g / (jnp.sqrt(moments) + epsilon)


def rep_swapped(array, by):
    peers = lax.axis_size("rep")
    return lax.ppermute(array, "rep", [(i, i ^ by) for i in range(peers)])


def along_ring(array, offset_of):
    groups, reps = lax.axis_size("ent"), lax.axis_size("rep")
    pairs = []
    for e in range(groups):
        for r in range(reps):
            way = offset_of(r) if r % CORES == 1 else -offset_of(r)
            to = RING[(PLACE[e] + way) % groups]
            pairs.append((e * reps + r, to * reps + r))
    return lax.ppermute(array, ("ent", "rep"), pairs)


def ring_step(array):
    return along_ring(array, lambda r: -1)


def handed_on(array, k):
    return along_ring(array, lambda r: OFFSETS[k][0 if r < CORES else 1])


def gathered_shards(
    entity_table, entity_state, operators, operator_state, sources, destinations, relations, negatives
):
    groups, reps = lax.axis_size("ent"), lax.axis_size("rep")
    entities, width = entity_table.shape
    edges = sources.shape[0]
    relation_count = groups * operators.shape[0]
    half = entities // CORES
    core = lax.axis_index("rep") % CORES

    operators_half = operators.astype(bf16)
    table = entity_table.T
    ids = jnp.concatenate(
        [
            sources,
            destinations,
            relations[:, 0],
            negatives[0],
            jnp.full((5 * edges - negatives.shape[1],), -1, jnp.int32),
        ]
    ).reshape(8, edges)
    places = relation_count
    slot_out = [
        jax.ShapeDtypeStruct((reps, places, SLOTS, width), bf16),
        jax.ShapeDtypeStruct((reps, 8, edges), f32),
        jax.ShapeDtypeStruct((reps, 1, entities), f32),
    ]
    a1 = ring_step(operators_half)
    others = [rep_swapped(ids, by) for by in (1, 2, 3)]
    own_half = lax.dynamic_slice_in_dim(table, core * half, half, 1).astype(bf16)
    a1, own_half, *others = lax.optimization_barrier((a1, own_half, *others))
    a2 = ring_step(a1)
    b1 = rep_swapped(a1, 1)
    b1, own_half = lax.optimization_barrier((b1, own_half))
    mine = passed_along(own_half, "ent", -1)
    a2, b1, late_table = lax.optimization_barrier((a2, b1, table))
    a3 = ring_step(a2)
    a4 = along_ring(lax.dynamic_slice_in_dim(a2, core, 1, 0), lambda r: -2)
    b2 = rep_swapped(a2, 1)
    table_half = late_table.astype(bf16)
    slots = call(slot_kernel, slot_out, "slots", 10**8, 10**6, (ids, *others, table_half))
    a3, a4, b2, mine, *slots = lax.optimization_barrier((a3, a4, b2, mine, *slots))
    slotted, rows, counts = slots
    other = rep_swapped(mine, 1)
    b3 = rep_swapped(a3, 1)
    b4 = rep_swapped(a4, 1)
    (made_early,) = call(
        ready_kernel,
        [jax.ShapeDtypeStruct((reps * edges, width), bf16)],
        "ready", 10**8, 10**6, (operators_half, a1, a2, b2, b1, slotted, rows),
        scratch=[VMEM((reps, places, SLOTS, width), bf16)],
    )
    gathered = (operators_half, a1, a2, a3, a4, b4, b3, b2, b1)

    score_out = [jax.ShapeDtypeStruct((width + SIDE + 16, LANES), bf16)] * len(OFFSETS) + [
        jax.ShapeDtypeStruct((reps, edges, entities), bf16),
        jax.ShapeDtypeStruct((reps, 3 * edges, width), bf16),
        jax.ShapeDtypeStruct((reps, edges, width), bf16),
    ]
    *handed, weights, sides, query = call(
        functools.partial(score_kernel, negatives.shape[1]), score_out, "scores", 10**9, 10**6,
        (a3, a4, b4, b3, slotted, rows, counts, mine, other, made_early),
        scratch=[
            VMEM((width, entities), bf16),
            VMEM((reps, LATE[1] - LATE[0], SLOTS, width), bf16),
            VMEM((reps, len(OFFSETS), SLOTS, width), bf16),
        ],
    )
    arrived = [handed_on(matrix, k) for k, matrix in enumerate(handed)]
    (target_half,) = call(
        target_kernel,
        [jax.ShapeDtypeStruct((width, half), bf16)],
        "targets", 10**8, 10**6, (rows, weights, sides),
    )
    query, target_half = lax.optimization_barrier((query, target_half))
    (source_total,) = call(
        source_kernel,
        [jax.ShapeDtypeStruct((width, entities), f32)],
        "sources", 10**8, 10**6, (*gathered, rows, query),
        scratch=[VMEM((reps, places, SLOTS, width), bf16)],
    )
    home_mine = passed_along(target_half, "ent", 1)
    home_other = rep_swapped(home_mine, 1)
    source_total, *arrived = lax.optimization_barrier((source_total, *arrived))
    one_chip = sum(matrix.astype(f32) for matrix in arrived).astype(bf16)
    one_relation = one_chip.astype(f32) + rep_swapped(one_chip, CORES).astype(f32)
    other_relation = rep_swapped(one_relation, 1)
    new_table, new_state = call(
        entity_kernel,
        [
            jax.ShapeDtypeStruct((width, entities), f32),
            jax.ShapeDtypeStruct((1, entities), f32),
        ],
        "entity_update", 10**6, 10**6,
        (source_total, home_mine, home_other, table, entity_state.reshape(1, -1)),
    )
    other_relation, new_table, new_state = lax.optimization_barrier(
        (other_relation, new_table, new_state)
    )
    new_operators, new_operator_state = call(
        operator_kernel,
        [jax.ShapeDtypeStruct(operators.shape, f32)] * 2,
        "operator_update", 10**6, 10**6,
        (one_relation, other_relation, operators, operator_state),
    )
    return (new_table.T, new_state.reshape(-1), new_operators, new_operator_state)


def solution(mesh):
    placed = (
        P("ent", None),
        P("ent"),
        P("ent", None, None),
        P("ent", None, None),
        P(("ent", "rep")),
        P(("ent", "rep")),
        P(("ent", "rep"), None),
        P(("ent", "rep"), None),
    )
    small = mesh.shape["ent"] == len(RING) and mesh.shape["rep"] == 2 * CORES
    return jax.shard_map(
        gathered_shards if small else exchanged_shards,
        mesh=mesh,
        in_specs=placed,
        out_specs=(P("ent", None), P("ent"), P("ent", None, None), P("ent", None, None)),
        check_vma=False,
    )
```

```python
import functools

import jax
import jax.numpy as jnp
from jax import lax
from jax.experimental import pallas as pl
from jax.experimental.pallas import tpu as pltpu
from jax.sharding import PartitionSpec as P

SPAN = 256
EDGE_DEV = 256
REL_DEV = 2


entity_rate = 0.1
operator_rate = 0.02
epsilon = 1e-06


def passed_along(array, axis, by):
    peers = lax.axis_size(axis)
    return lax.ppermute(array, axis, [(i, (i + by) % peers) for i in range(peers)])


def place_slots(relation_ids, capacity):
    count_edges = relation_ids.shape[0]
    ordering = jnp.argsort(relation_ids, stable=True)
    ranked = relation_ids[ordering]
    leading = jnp.searchsorted(ranked, ranked, side="left")
    within = jnp.arange(count_edges, dtype=jnp.int32) - leading
    position = jnp.zeros((count_edges,), jnp.int32).at[ordering].set(within)
    return relation_ids * capacity + position


def score_grads(transformed, target_ids, negative_ids, table_rows):
    target_rows = jnp.take(table_rows, target_ids, axis=0)
    positive = jnp.sum(transformed.astype(jnp.float32) * target_rows.astype(jnp.float32), axis=-1)
    positive_grad = -jax.nn.sigmoid(-positive)
    width = transformed.shape[1]
    blocks = transformed.reshape(-1, SPAN, width)
    negative_count = negative_ids.shape[1]

    def span_step(running, pieces):
        query_block, negative_block = pieces
        negative_rows = jnp.take(table_rows, negative_block, axis=0)
        scores = lax.dot_general(
            query_block, negative_rows, (((1,), (1,)), ((), ())), preferred_element_type=jnp.float32
        )
        negative_grad = (jax.nn.sigmoid(scores) / negative_count).astype(jnp.bfloat16)
        query_part = jnp.dot(negative_grad, negative_rows, preferred_element_type=jnp.float32)
        row_update = lax.dot_general(
            negative_grad, query_block, (((0,), (0,)), ((), ())), preferred_element_type=jnp.float32
        )
        return (running.at[negative_block].add(row_update), query_part)

    starting = jnp.zeros((table_rows.shape[0], width), jnp.float32)
    negative_total, query_parts = lax.scan(span_step, starting, (blocks, negative_ids))
    query_grad = (
        positive_grad[:, None] * target_rows.astype(jnp.float32) + query_parts.reshape(-1, width)
    ).astype(jnp.bfloat16)
    target_grad = negative_total.at[target_ids].add(
        positive_grad[:, None] * transformed.astype(jnp.float32)
    )
    return (query_grad, target_grad)


def row_adagrad(weights, moments, gradient):
    fresh_moments = moments + jnp.mean(gradient * gradient, axis=-1)
    updated = weights - entity_rate * gradient / (jnp.sqrt(fresh_moments)[:, None] + epsilon)
    return (updated, fresh_moments)


def dense_adagrad(weights, moments, gradient):
    fresh_moments = moments + gradient * gradient
    updated = weights - operator_rate * gradient / (jnp.sqrt(fresh_moments) + epsilon)
    return (updated, fresh_moments)


def exchanged_shards(
    entity_table,
    entity_state,
    operators,
    operator_state,
    sources,
    destinations,
    relations,
    negatives,
):
    groups = lax.axis_size("ent")
    relation_count = REL_DEV * groups
    capacity = max(2, (2 * EDGE_DEV + relation_count - 1) // relation_count)
    width = entity_table.shape[1]
    table_half = entity_table.astype(jnp.bfloat16)
    operators_half = operators.astype(jnp.bfloat16)
    slot_index = place_slots(relations[:, 0], capacity)
    source_rows = jnp.take(table_half, sources, axis=0)
    outgoing = (
        jnp.zeros((relation_count * capacity, width), jnp.bfloat16).at[slot_index].set(source_rows)
    )
    outgoing = outgoing.reshape(groups, REL_DEV, capacity, width)
    arrived = lax.all_to_all(outgoing, "ent", split_axis=0, concat_axis=0, tiled=True)
    result = jnp.einsum(
        "srmd,rdk->srmk", arrived, operators_half, preferred_element_type=jnp.float32
    ).astype(jnp.bfloat16)
    returned = lax.all_to_all(result, "ent", split_axis=0, concat_axis=0, tiled=True)
    transformed_slots = returned
    transformed = jnp.take(transformed_slots.reshape(-1, width), slot_index, axis=0)
    neighbour_table = passed_along(table_half, "ent", -1)
    query_grad, target_grad = score_grads(transformed, destinations, negatives, neighbour_table)
    home_grad = passed_along(target_grad, "ent", 1)
    grad_slots = (
        jnp.zeros((relation_count * capacity, width), jnp.bfloat16).at[slot_index].set(query_grad)
    )
    grad_slots = grad_slots.reshape(groups, REL_DEV, capacity, width)
    arrived_grads = lax.all_to_all(grad_slots, "ent", split_axis=0, concat_axis=0, tiled=True)
    source_grads = jnp.einsum(
        "srmk,rdk->srmd", arrived_grads, operators_half, preferred_element_type=jnp.float32
    ).astype(jnp.bfloat16)
    returned = lax.all_to_all(source_grads, "ent", split_axis=0, concat_axis=0, tiled=True)
    operator_grad = jnp.einsum(
        "srmd,srmk->rdk", arrived, arrived_grads, preferred_element_type=jnp.float32
    )
    source_grad = jnp.take(returned.reshape(-1, width), slot_index, axis=0)
    entity_grad = (
        jnp.zeros(entity_table.shape, jnp.float32).at[sources].add(source_grad.astype(jnp.float32))
        + home_grad
    )
    total_grad, total_operator = lax.psum((entity_grad, operator_grad), "rep")
    new_table, new_entity_state = row_adagrad(entity_table, entity_state, total_grad)
    new_operators, new_operator_state = dense_adagrad(operators, operator_state, total_operator)
    return (new_table, new_entity_state, new_operators, new_operator_state)


bf16 = jnp.bfloat16
f32 = jnp.float32
CORES = 2
LANES = 128
RING = (0, 2, 4, 6, 7, 5, 3, 1)
PLACE = tuple(RING.index(e) for e in range(8))
SLOTS = 32
SIDE = 104
OFFSETS = ((3, 4), (5, 6), (2, 1), (0, 7))
VMEM = pltpu.VMEM
NT = (((1,), (1,)), ((), ()))
TN = (((0,), (0,)), ((), ()))


def dot(a, b, dims=(((1,), (0,)), ((), ()))):
    return lax.dot_general(a, b, dims, preferred_element_type=f32)


def lanes_of(shape):
    return lax.broadcasted_iota(jnp.int32, shape, 1)


def rows_of(shape):
    return lax.broadcasted_iota(jnp.int32, shape, 0)


def one_hot(mask):
    return jnp.where(mask, 1.0, 0.0).astype(bf16)


def call(body, outs, name, flops, size, operands, limit=16, scratch=()):
    whole = pl.BlockSpec(memory_space=VMEM)
    return pl.pallas_call(
        body,
        out_shape=outs,
        in_specs=[whole] * len(operands),
        out_specs=[whole] * len(outs),
        scratch_shapes=list(scratch),
        name=name,
        cost_estimate=pl.CostEstimate(flops=flops, bytes_accessed=size, transcendentals=0),
        compiler_params=pltpu.CompilerParams(vmem_limit_bytes=limit * 2**20),
    )(*operands)


def chosen_from(listed, at):
    found = jnp.zeros_like(at)
    for i, value in enumerate(listed):
        found = jnp.where(at == i, value, found)
    return found


def position():
    rep = lax.axis_index("rep")
    core = lax.rem(rep, CORES)
    return core, rep, chosen_from(PLACE, lax.axis_index("ent")), 2 * core - 1


def slot_kernel(own, near, far, across, table, slotted, rows, counts):
    core, me, here, sign = position()
    ring = len(RING)
    reps, _, edges = rows.shape
    places = slotted.shape[1]
    ids = [ref[...] for ref in (own, near, far, across)]
    before = one_hot(rows_of((edges, edges)) > lanes_of((edges, edges)))
    relation = jnp.concatenate([block[2:3] for block in ids], axis=0)
    offset = lax.bitwise_and(
        sign * (chosen_from(PLACE, lax.shift_right_logical(relation, 1)) - here), ring - 1
    )
    parity = lax.bitwise_and(relation, 1)
    local = 2 * offset + jnp.where(offset == ring // 2, lax.bitwise_xor(parity, core), parity)
    ends = [block[i : i + 1] for i in (0, 1) for block in ids]
    standing = jnp.concatenate([local, *ends], axis=0).astype(f32).T
    column = lambda i: standing[:, i : i + 1].astype(jnp.int32)
    named = [lanes_of((edges, LANES)) == column(m) for m in range(reps)]
    ahead = dot(before, one_hot(jnp.concatenate(named, axis=1)))
    slots = jnp.concatenate(
        [
            standing[:, m : m + 1] * SLOTS
            + jnp.sum(
                jnp.where(named[m], ahead[:, m * LANES : (m + 1) * LANES], 0.0), axis=1, keepdims=True
            )
            for m in range(reps)
        ],
        axis=1,
    ).T
    for m in range(reps):
        block = lax.bitwise_xor(me, m)
        lying = jnp.concatenate(
            [ids[m][0:2].astype(f32), slots[m : m + 1], ids[m][3:8].astype(f32)], axis=0
        )
        rows[block] = lying
        tally = jnp.zeros((8, LANES), f32)
        for k in range(3, 7):
            drawn = ids[m][k : k + 1]
            high = one_hot(rows_of((8, edges)) == lax.shift_right_arithmetic(drawn, 7))
            low = one_hot(rows_of((LANES, edges)) == lax.bitwise_and(drawn, LANES - 1))
            tally = tally + dot(high, low, NT)
        counts[block] = jnp.concatenate([tally[k : k + 1] for k in range(8)], axis=1)
    picked = [
        one_hot(lanes_of((edges, table.shape[1])) == column(reps + m)) for m in range(reps)
    ]
    source_rows = dot(jnp.concatenate(picked, axis=0), table[...], NT).astype(bf16)
    for m in range(reps):
        into = one_hot(rows_of((places * SLOTS, edges)) == slots[m : m + 1].astype(jnp.int32))
        given = dot(into, source_rows[m * edges : (m + 1) * edges]).astype(bf16)
        slotted[lax.bitwise_xor(me, m)] = given.reshape(places, SLOTS, -1)


def join(table, mine, other):
    half = mine.shape[1]
    core, *_ = position()
    table[:, pl.ds(pl.multiple_of(core * half, half), half)] = mine[...]
    table[:, pl.ds(pl.multiple_of((1 - core) * half, half), half)] = other[...]


LATE = (6, 12)


def transform(moved, slotted, place, at, op):
    reps, _, _, width = slotted.shape
    given = slotted[:, place].reshape(reps * SLOTS, width)
    moved[:, at] = dot(given, op).astype(bf16).reshape(reps, SLOTS, width)


def handed_places(core, me):
    handed = []
    for near, far in OFFSETS:
        offset = jnp.where(me < CORES, near, far)
        handed.append(2 * offset + jnp.where(offset == len(RING) // 2, 0, core))
    return handed


def ready_kernel(o0, a1, a2, b2, b1, slotted, rows, mine, made_early, target_early, turned, moved):
    reps, _, edges = rows.shape
    places, width = slotted.shape[1], slotted.shape[3]
    core, me, *_ = position()
    half = mine.shape[1]
    aimed = []
    moved[:, LATE[0] : LATE[1]] = jnp.zeros((reps, LATE[1] - LATE[0], SLOTS, width), bf16)
    for place, op in enumerate(operator_list(o0, a1, a2, None, None, None, None, b2, b1)):
        if op is not None:
            transform(moved, slotted, place, place, op())
    for b in range(reps):
        standing = rows[b].T.astype(jnp.int32)
        out_of = one_hot(lanes_of((edges, places * SLOTS)) == standing[:, 2:3])
        made = dot(out_of, moved[b].reshape(places * SLOTS, width))
        made_early[b * edges : (b + 1) * edges] = made.astype(bf16)
        aimed.append(lanes_of((edges, half)) + core * half == standing[:, 1:2])
    target_early[...] = dot(one_hot(jnp.concatenate(aimed, axis=0)), mine[...], NT).astype(bf16)
    for k, place in enumerate(handed_places(core, me)):
        given = slotted[:, pl.ds(place, 1)].reshape(reps * SLOTS, width)
        turned[k] = given.astype(f32).T.astype(bf16)


def score_kernel(
    negative_count, a3, a4, b4, b3, slotted, rows, counts, mine, other, made_early, target_early, turned,
    s0, s1, s2, s3, weights, sides, query, table, moved, asking,
):
    core, me, *_ = position()
    reps, places = slotted.shape[:2]
    width, entities = table.shape
    edges = rows.shape[2]
    join(table, mine, other)
    for place, op in enumerate(operator_list(None, None, None, a3, a4, b4, b3, None, None)):
        if op is not None:
            transform(moved, slotted, place, place - LATE[0], op())
    sent = (s0, s1, s2, s3)
    handed = handed_places(core, me)
    lying = [rows[b] for b in range(reps)]
    standing = [block.T.astype(jnp.int32) for block in lying]
    made = []
    for b in range(reps):
        late = (LATE[1] - LATE[0]) * SLOTS
        out_of = one_hot(lanes_of((edges, late)) + LATE[0] * SLOTS == standing[b][:, 2:3])
        made.append(dot(out_of, moved[b].reshape(late, width)))
    made = jnp.concatenate(made, axis=0) + made_early[...].astype(f32)
    made_half = made.astype(bf16)
    half = other.shape[1]
    ends = jnp.concatenate([block[:, 1:2] for block in standing], axis=0)
    far_aimed = one_hot(lanes_of((reps * edges, half)) + (1 - core) * half == ends)
    target_rows = target_early[...].astype(f32) + dot(far_aimed, other[...], NT)
    positive = jnp.sum(made * target_rows, axis=1, keepdims=True)
    positive_grad = -(0.5 * jnp.tanh(-0.5 * positive) + 0.5)
    scale = 0.5 / negative_count
    share = jnp.tanh(dot((0.5 * made).astype(bf16), table[...])) * scale + scale
    share = share.astype(bf16)
    weighted = jnp.concatenate(
        [share[b * edges : (b + 1) * edges] * counts[b].astype(bf16) for b in range(reps)], axis=0
    )
    asked = (positive_grad * target_rows + dot(weighted, table[...], NT)).astype(bf16)
    push = positive_grad * made
    push_half = push.astype(bf16)
    push_rest = (push - push_half.astype(f32)).astype(bf16)
    for b in range(reps):
        at = slice(b * edges, (b + 1) * edges)
        weights[b] = weighted[at]
        sides[b, :edges] = made_half[at]
        sides[b, edges : 2 * edges] = push_half[at]
        sides[b, 2 * edges :] = push_rest[at]
        query[b] = asked[at]
        slot = lying[b][2:3].astype(jnp.int32)
        into = jnp.concatenate(
            [one_hot(rows_of((SLOTS, edges)) + place * SLOTS == slot) for place in handed], axis=0
        )
        asking[b] = dot(into, asked[at]).astype(bf16).reshape(len(sent), SLOTS, width)
    for k in range(len(sent)):
        sent[k][...] = packed(dot(turned[k], asking[:, k].reshape(reps * SLOTS, width))).astype(bf16)


def packed(matrix):
    low, side, spare = matrix[:, :LANES], matrix[:, LANES : LANES + 64], matrix[:, LANES + 64 :]
    side = jnp.concatenate([side[:SIDE], side[side.shape[0] - SIDE :]], axis=1)
    spare = spare.T
    rest = jnp.zeros((spare.shape[0], 2 * LANES - spare.shape[1]), spare.dtype)
    return jnp.concatenate(
        [low, side, spare[:, :LANES], jnp.concatenate([spare[:, LANES:], rest], axis=1)], axis=0
    )


def unpacked(rows, size):
    low, side, spare = rows[:size], rows[size : size + SIDE], rows[size + SIDE :]
    side = jnp.concatenate([side[:, :64], side[2 * SIDE - size :, 64:]], axis=0)
    count = size - LANES - 64
    spare = jnp.concatenate([spare[:count], spare[count:, : size - LANES]], axis=1)
    return jnp.concatenate([low, side, spare.T], axis=1)


def operator_list(o0, a1, a2, a3, a4, b4, b3, b2, b1):
    listed = [(o0, 0), (o0, 1)]
    for ref in (a1, a2, a3):
        listed += [(ref, 0), (ref, 1)]
    listed += [(a4, 0), (b4, 0)]
    for ref in (b3, b2, b1):
        listed += [(ref, 0), (ref, 1)]
    return [None if ref is None else lambda ref=ref, i=i: ref[i] for ref, i in listed]


def target_kernel(rows, weights, sides, target_half):
    core, *_ = position()
    reps, edges, _ = weights.shape
    half = target_half.shape[1]
    at = pl.ds(pl.multiple_of(core * half, half), half)
    grown = jnp.zeros(target_half.shape, f32)
    for b in range(reps):
        aimed = one_hot(
            lanes_of((edges, half)) + core * half == rows[b].T[:, 1:2].astype(jnp.int32)
        )
        faces = jnp.concatenate([weights[b, :, at], aimed, aimed], axis=0)
        grown = grown + dot(sides[b], faces, TN)
    target_half[...] = grown.astype(bf16)


def source_kernel(o0, a1, a2, a3, a4, b4, b3, b2, b1, rows, query, source_total, held):
    reps, places, _, width = held.shape
    edges, entities = rows.shape[2], source_total.shape[1]
    for b in range(reps):
        into = one_hot(rows_of((places * SLOTS, edges)) == rows[b][2:3].astype(jnp.int32))
        held[b] = dot(into, query[b]).astype(bf16).reshape(places, SLOTS, width)
    for place, op in enumerate(operator_list(o0, a1, a2, a3, a4, b4, b3, b2, b1)):
        given = held[:, place].reshape(-1, width)
        held[:, place] = dot(given, op(), NT).astype(bf16).reshape(-1, SLOTS, width)
    for b in range(reps):
        standing = rows[b].T.astype(jnp.int32)
        out_of = one_hot(lanes_of((edges, places * SLOTS)) == standing[:, 2:3])
        back = dot(out_of, held[b].reshape(places * SLOTS, width)).astype(bf16)
        spread = one_hot(lanes_of((edges, entities)) == standing[:, 0:1])
        grown = dot(back, spread, TN)
        if b == 0:
            source_total[...] = grown
        else:
            source_total[...] += grown


def entity_kernel(source_total, mine, other, table, state, new_table, new_state):
    core, *_ = position()
    half = mine.shape[1]
    width = table.shape[0]
    for part, side in ((mine, core), (other, 1 - core)):
        at = pl.ds(pl.multiple_of(side * half, half), half)
        g = source_total[:, at] + part[...].astype(f32)
        moments = state[:, at] + jnp.sum(g * g, axis=0, keepdims=True) * (1.0 / width)
        new_state[:, at] = moments
        new_table[:, at] = table[:, at] - g * (entity_rate / (jnp.sqrt(moments) + epsilon))


def operator_kernel(own, other, operators, state, new_operators, new_state):
    core, *_ = position()
    for i in range(operators.shape[0]):
        g = unpacked(jnp.where(core == i, own[...], other[...]), operators.shape[1])
        moments = state[i] + g * g
        new_state[i] = moments
        new_operators[i] = operators[i] - operator_rate * g / (jnp.sqrt(moments) + epsilon)


def rep_swapped(array, by):
    peers = lax.axis_size("rep")
    return lax.ppermute(array, "rep", [(i, i ^ by) for i in range(peers)])


def along_ring(array, offset_of):
    groups, reps = lax.axis_size("ent"), lax.axis_size("rep")
    pairs = []
    for e in range(groups):
        for r in range(reps):
            way = offset_of(r) if r % CORES == 1 else -offset_of(r)
            to = RING[(PLACE[e] + way) % groups]
            pairs.append((e * reps + r, to * reps + r))
    return lax.ppermute(array, ("ent", "rep"), pairs)


def ring_step(array):
    return along_ring(array, lambda r: -1)


def handed_on(array, k):
    return along_ring(array, lambda r: OFFSETS[k][0 if r < CORES else 1])


def gathered_shards(
    entity_table, entity_state, operators, operator_state, sources, destinations, relations, negatives
):
    groups, reps = lax.axis_size("ent"), lax.axis_size("rep")
    entities, width = entity_table.shape
    edges = sources.shape[0]
    relation_count = groups * operators.shape[0]
    half = entities // CORES
    core = lax.axis_index("rep") % CORES

    operators_half = operators.astype(bf16)
    table = entity_table.T
    ids = jnp.concatenate(
        [
            sources,
            destinations,
            relations[:, 0],
            negatives[0],
            jnp.full((5 * edges - negatives.shape[1],), -1, jnp.int32),
        ]
    ).reshape(8, edges)
    places = relation_count
    slot_out = [
        jax.ShapeDtypeStruct((reps, places, SLOTS, width), bf16),
        jax.ShapeDtypeStruct((reps, 8, edges), f32),
        jax.ShapeDtypeStruct((reps, 1, entities), f32),
    ]
    a1 = ring_step(operators_half)
    others = [rep_swapped(ids, by) for by in (1, 2, 3)]
    own_half = lax.dynamic_slice_in_dim(table, core * half, half, 1).astype(bf16)
    a1, own_half, *others = lax.optimization_barrier((a1, own_half, *others))
    a2 = ring_step(a1)
    b1 = rep_swapped(a1, 1)
    b1, own_half = lax.optimization_barrier((b1, own_half))
    mine = passed_along(own_half, "ent", -1)
    a2, b1, late_table = lax.optimization_barrier((a2, b1, table))
    a3 = ring_step(a2)
    a4 = along_ring(lax.dynamic_slice_in_dim(a2, core, 1, 0), lambda r: -2)
    b2 = rep_swapped(a2, 1)
    table_half = late_table.astype(bf16)
    slots = call(slot_kernel, slot_out, "slots", 10**8, 10**6, (ids, *others, table_half))
    a3, a4, b2, mine, *slots = lax.optimization_barrier((a3, a4, b2, mine, *slots))
    slotted, rows, counts = slots
    other = rep_swapped(mine, 1)
    b3 = rep_swapped(a3, 1)
    b4 = rep_swapped(a4, 1)
    early = call(
        ready_kernel,
        [jax.ShapeDtypeStruct((reps * edges, width), bf16)] * 2
        + [jax.ShapeDtypeStruct((len(OFFSETS), width, reps * SLOTS), bf16)],
        "ready", 10**8, 10**6, (operators_half, a1, a2, b2, b1, slotted, rows, mine),
        scratch=[VMEM((reps, places, SLOTS, width), bf16)],
    )
    gathered = (operators_half, a1, a2, a3, a4, b4, b3, b2, b1)

    score_out = [jax.ShapeDtypeStruct((width + SIDE + 16, LANES), bf16)] * len(OFFSETS) + [
        jax.ShapeDtypeStruct((reps, edges, entities), bf16),
        jax.ShapeDtypeStruct((reps, 3 * edges, width), bf16),
        jax.ShapeDtypeStruct((reps, edges, width), bf16),
    ]
    *handed, weights, sides, query = call(
        functools.partial(score_kernel, negatives.shape[1]), score_out, "scores", 10**9, 10**6,
        (a3, a4, b4, b3, slotted, rows, counts, mine, other, *early),
        scratch=[
            VMEM((width, entities), bf16),
            VMEM((reps, LATE[1] - LATE[0], SLOTS, width), bf16),
            VMEM((reps, len(OFFSETS), SLOTS, width), bf16),
        ],
    )
    arrived = [handed_on(matrix, k) for k, matrix in enumerate(handed)]
    (target_half,) = call(
        target_kernel,
        [jax.ShapeDtypeStruct((width, half), bf16)],
        "targets", 10**8, 10**6, (rows, weights, sides),
    )
    query, target_half = lax.optimization_barrier((query, target_half))
    (source_total,) = call(
        source_kernel,
        [jax.ShapeDtypeStruct((width, entities), f32)],
        "sources", 10**8, 10**6, (*gathered, rows, query),
        scratch=[VMEM((reps, places, SLOTS, width), bf16)],
    )
    home_mine = passed_along(target_half, "ent", 1)
    home_other = rep_swapped(home_mine, 1)
    source_total, *arrived = lax.optimization_barrier((source_total, *arrived))
    one_chip = sum(matrix.astype(f32) for matrix in arrived).astype(bf16)
    one_relation = one_chip.astype(f32) + rep_swapped(one_chip, CORES).astype(f32)
    other_relation = rep_swapped(one_relation, 1)
    new_table, new_state = call(
        entity_kernel,
        [
            jax.ShapeDtypeStruct((width, entities), f32),
            jax.ShapeDtypeStruct((1, entities), f32),
        ],
        "entity_update", 10**6, 10**6,
        (source_total, home_mine, home_other, table, entity_state.reshape(1, -1)),
    )
    other_relation, new_table, new_state = lax.optimization_barrier(
        (other_relation, new_table, new_state)
    )
    new_operators, new_operator_state = call(
        operator_kernel,
        [jax.ShapeDtypeStruct(operators.shape, f32)] * 2,
        "operator_update", 10**6, 10**6,
        (one_relation, other_relation, operators, operator_state),
    )
    return (new_table.T, new_state.reshape(-1), new_operators, new_operator_state)


def solution(mesh):
    placed = (
        P("ent", None),
        P("ent"),
        P("ent", None, None),
        P("ent", None, None),
        P(("ent", "rep")),
        P(("ent", "rep")),
        P(("ent", "rep"), None),
        P(("ent", "rep"), None),
    )
    small = mesh.shape["ent"] == len(RING) and mesh.shape["rep"] == 2 * CORES
    return jax.shard_map(
        gathered_shards if small else exchanged_shards,
        mesh=mesh,
        in_specs=placed,
        out_specs=(P("ent", None), P("ent"), P("ent", None, None), P("ent", None, None)),
        check_vma=False,
    )
```
